32 devices in a mesh: grp: 8 (over y, x, core), tile: 4 (over z).
Axes of the slice: x: 2, y: 2, z: 4, core: 2. Of those that a mesh axis runs over, the one named last changes fastest.
Arguments:
- log_cond: float32 [8, 32, 32, 128], P('grp', 'tile'), may hold values from -3 to 3
- potential: float32 [8, 32, 32, 128], P('grp', 'tile'), may hold values from -6 to 6
- noise: float32 [2, 8, 32, 32, 128], P(None, 'grp', 'tile'), may hold values from -3 to 3
- source: float32 [32, 32, 128], P('tile'), may hold values from -6 to 6
- parents: int32 [8], replicated, may hold values from 0 to 7
- accept: int32 [2, 8], P(None, 'grp'), may hold values 0 or 1
- weights: float32 [8], P('grp'), may hold values from 0.1 to 10
Outputs:
- conduct_out: float32 [8, 32, 32, 128], P('grp', 'tile')
- potential_out: float32 [8, 32, 32, 128], P('grp', 'tile')
- moments: float32 [1024, 1024], P('tile')
The draws below stay inside these ranges and needn't reach their ends.
Inputs may be any that keep to these rules, and one draw needn't show every extreme that they name: `parents`: parent indices of offspring.
All inputs are finite; a program needn't handle non-finite values. No bound on the sum of `accept` on one device may be relied on, other than what follows from the above.
Results may differ from the reference program's by a relative error of at most 0.0001.
Values sent between devices are 32-bit elements; how exact they have to be, the bound alone decides.
No kernel may reach another device: no remote copies, remote signals or barrier semaphores. Data moves between devices by JAX's collectives and lax.ppermute only.
A program may use at most 64 MiB of HBM per device.

```python
import math
import jax
import jax.numpy as jnp
import numpy as np
from jax import lax

CX = 8
NY = 32
NZ = 128
MOVES = 2
P_SIZE = 8
NX = 32
COEF = 1024
N_TILE = 4


def with_ends(result, own_key, low, high):
    place = [jax.random.randint(jax.random.fold_in(own_key, axis), (), 0, length) for axis, length in enumerate(result.shape)]
    longest = result.shape.index(max(result.shape))
    next_to = place[:longest] + [(place[longest] + 1) % result.shape[longest]] + place[longest + 1:]
    return result.at[tuple(place)].set(low).at[tuple(next_to)].set(high)


def levels(key, extent, split, low, largest):
    def one(position, parts):
        draws = jax.random.uniform(jax.random.fold_in(jax.random.fold_in(key, 6), position), (parts,), jnp.float32, low / len(split), largest / len(split))
        return jnp.repeat(jnp.exp(draws), extent[position] // parts).reshape((-1,) + (1,) * (len(extent) - position - 1))

    gain = one(*split[0])
    for cut in split[1:]:
        gain = gain * one(*cut)
    return gain


def rank_bounds(amount, slope):
    weights = [(1 << 20) // math.isqrt(rank ** slope) + 1 for rank in range(1, amount + 1)]
    deviation = 1 + sum(weights) // (1 << 30)
    return np.cumsum(np.array([max(1, weight // deviation) for weight in weights]))


def ranked_ids(stream_key, extent, number_of, slope):
    table = rank_bounds(number_of, slope)
    pick = jax.random.randint(jax.random.fold_in(stream_key, 1), extent, 0, int(table[number_of - 1]))
    grade = jnp.searchsorted(jnp.asarray(table, jnp.int32), pick, side="right")
    return jax.random.permutation(jax.random.fold_in(stream_key, 2), number_of)[grade].astype(jnp.int32)


def bell_draw(own_key, shape, scale, most, shards=(), dtype=jnp.bfloat16):
    level = levels(own_key, shape, shards, -0.22, 0.18) if shards else 1.0
    values = jax.random.normal(own_key, shape, jnp.float32) * scale * level
    return jnp.minimum(jnp.maximum(values, -most), most).astype(dtype)


def setup_inputs(seed: int = 0) -> dict:
    seeds = jax.random.split(jax.random.key(seed), 8)
    log_cond = bell_draw(seeds[0], (P_SIZE, NX, NY, NZ), 0.5, 3.0, ((0, 8), (1, 4)), jnp.float32)
    potential = bell_draw(seeds[1], (P_SIZE, NX, NY, NZ), 1.0, 6.0, ((0, 8), (1, 4)), jnp.float32)
    noise = bell_draw(seeds[2], (MOVES, P_SIZE, NX, NY, NZ), 0.5, 3.0, ((1, 8), (2, 4)), jnp.float32)
    source = bell_draw(seeds[3], (NX, NY, NZ), 1.0, 6.0, ((0, 4),), jnp.float32)
    parents = with_ends(ranked_ids(seeds[4], (P_SIZE,), P_SIZE, 2), jax.random.fold_in(seeds[4], 3), 0, P_SIZE - 1).astype(jnp.int32)
    accept = with_ends((jax.random.randint(seeds[5], (MOVES, P_SIZE), 0, 2) < 1).astype(jnp.int32), jax.random.fold_in(seeds[5], 1), 0, 1)
    weights = jnp.clip(jnp.exp(math.log(10.0) - 4.6051702 * jax.random.uniform(seeds[6], (P_SIZE,), jnp.float32) ** levels(seeds[6], (P_SIZE,), ((0, 8),), -0.2, 0.2)), 0.1, 10.0)
    return dict(log_cond=log_cond, potential=potential, noise=noise, source=source, parents=parents, accept=accept, weights=weights)


prior_keep = 0.8
prior_fresh = 0.6
relax_weight = 0.8


def neighbours(padded):
    return [padded[2:, 1:-1, 1:-1], padded[:-2, 1:-1, 1:-1],
            padded[1:-1, 2:, 1:-1], padded[1:-1, :-2, 1:-1],
            padded[1:-1, 1:-1, 2:], padded[1:-1, 1:-1, :-2]]


def relax_sweep(cond_ext, pot_ext, source):
    cond_pad = jnp.pad(cond_ext, ((0, 0), (1, 1), (1, 1)))
    pot_pad = jnp.pad(pot_ext, ((0, 0), (1, 1), (1, 1)))
    conductivity = jnp.exp(cond_pad)
    centre_k = conductivity[1:-1, 1:-1, 1:-1]
    centre = pot_pad[1:-1, 1:-1, 1:-1]
    flux_sum = jnp.zeros_like(centre)
    coef_sum = jnp.zeros_like(centre)
    for near_k, near_v in zip(neighbours(conductivity), neighbours(pot_pad)):
        face = 0.5 * (centre_k + near_k)
        flux_sum = flux_sum + face * near_v
        coef_sum = coef_sum + face
    return (1.0 - relax_weight) * centre + relax_weight * (source + flux_sum) / coef_sum


def pad_first(field):
    return jnp.pad(field, ((1, 1), (0, 0), (0, 0)))


def reference(log_cond, potential, noise, source, parents, accept, weights):
    conduct = log_cond[parents]
    pot = potential[parents]
    sweep_all = jax.vmap(lambda cond_now, pot_now: relax_sweep(pad_first(cond_now), pad_first(pot_now), source))
    for move_index in range(MOVES):
        proposal = prior_keep * conduct + prior_fresh * noise[move_index]
        relaxed_once = sweep_all(proposal, pot)
        relaxed_twice = sweep_all(proposal, relaxed_once)
        accepted = (accept[move_index] > 0)[:, None, None, None]
        conduct = jnp.where(accepted, proposal, conduct)
        pot = jnp.where(accepted, relaxed_twice, pot)
    weight_sum = jnp.sum(weights)

    def accumulate(running, element):
        field, share = element
        blocks = field.reshape(N_TILE, CX, NY, NZ)
        moment_one = jnp.einsum('txyz,tuyw->xzuw', blocks, blocks,
                                precision=lax.Precision.HIGHEST).reshape(COEF, COEF)
        return running + share * moment_one, None

    moments, _ = lax.scan(accumulate, jnp.zeros((COEF, COEF), jnp.float32), (pot, weights / weight_sum))
    return conduct, pot, moments
```

```python
import functools

import jax
import jax.numpy as jnp
from jax import lax
from jax.experimental import pallas as pl
from jax.experimental.pallas import tpu as pltpu
from jax.sharding import PartitionSpec as P

prior_keep = 0.8
prior_fresh = 0.6
relax_weight = 0.8


def choose_kernel(parents_ref, pieces_ref, chosen_ref):
    for place in range(chosen_ref.shape[0]):
        chosen_ref[place] = pieces_ref[parents_ref[place]]


def choose(parents, pieces):
    return pl.pallas_call(
        choose_kernel,
        out_shape=jax.ShapeDtypeStruct(pieces.shape, pieces.dtype),
        in_specs=[
            pl.BlockSpec(memory_space=pltpu.SMEM),
            pl.BlockSpec(memory_space=pltpu.VMEM),
        ],
        out_specs=pl.BlockSpec(memory_space=pltpu.VMEM),
        name="choose",
    )(parents, pieces)


def exchange_halo(low_edge, high_edge):
    count = lax.axis_size("tile")
    forward = [(i, i + 1) for i in range(count - 1)]
    backward = [(target, source) for source, target in forward]
    low = lax.ppermute(high_edge, "tile", forward)
    high = lax.ppermute(low_edge, "tile", backward)
    return low, high


def neighbours(padded):
    return [
        padded[2:, 1:-1, 1:-1],
        padded[:-2, 1:-1, 1:-1],
        padded[1:-1, 2:, 1:-1],
        padded[1:-1, :-2, 1:-1],
        padded[1:-1, 1:-1, 2:],
        padded[1:-1, 1:-1, :-2],
    ]


def relax_sweep(cond_ext, pot_ext, source):
    cond_pad = jnp.pad(cond_ext, ((0, 0), (1, 1), (1, 1)))
    pot_pad = jnp.pad(pot_ext, ((0, 0), (1, 1), (1, 1)))
    conductivity = jnp.exp(cond_pad)
    centre_k = conductivity[1:-1, 1:-1, 1:-1]
    centre = pot_pad[1:-1, 1:-1, 1:-1]
    flux_sum = jnp.zeros_like(centre)
    coef_sum = jnp.zeros_like(centre)
    for near_k, near_v in zip(neighbours(conductivity), neighbours(pot_pad)):
        face = 0.5 * (centre_k + near_k)
        flux_sum = flux_sum + face * near_v
        coef_sum = coef_sum + face
    return (1.0 - relax_weight) * centre + relax_weight * (source + flux_sum) / coef_sum


def inside(block, halo, width):
    if halo == 0:
        return block
    tile = lax.axis_index("tile")
    layer = lax.broadcasted_iota(jnp.int32, (block.shape[0], 1, 1), 0)
    low_ok = (tile > 0) | (layer >= halo)
    high_ok = (tile < lax.axis_size("tile") - 1) | (layer < halo + width)
    return jnp.where(low_ok & high_ok, block, 0.0)


def local(log_cond, potential, noise, source, parents, accept, weights):
    moves = noise.shape[0]
    width, ny, nz = source.shape
    reach = 2 * moves
    particles = lax.axis_size("grp")

    fixed = [noise[m, 0] for m in range(moves)] + [source]
    depth = [reach - 2 * m for m in range(moves)] + [reach - 1]
    low_fixed, high_fixed = exchange_halo(
        jnp.concatenate([field[:h] for field, h in zip(fixed, depth)]),
        jnp.concatenate([field[width - h:] for field, h in zip(fixed, depth)]),
    )
    wide = []
    at = 0
    for field, h in zip(fixed, depth):
        wide.append(jnp.concatenate([low_fixed[at:at + h], field, high_fixed[at:at + h]]))
        at += h
    noise_wide, source_wide = wide[:moves], wide[moves]

    bundle = jnp.stack([log_cond[0], potential[0]])
    rows = bundle.size // (particles * nz)
    pieces = jnp.concatenate(
        [
            bundle.reshape(particles, rows, nz),
            jnp.broadcast_to(weights[0], (particles, 8, nz)),
        ],
        axis=1,
    )
    pieces = lax.all_to_all(pieces, "grp", 0, 0, tiled=True)
    share = weights[0] / jnp.sum(pieces[:, rows, 0])
    moved = lax.all_to_all(choose(parents, pieces[:, :rows]), "grp", 0, 0, tiled=True)
    moved = moved.reshape(2, width, ny, nz)

    low, high = exchange_halo(moved[:, :reach], moved[:, width - reach:])
    extended = jnp.concatenate([low, moved, high], axis=1)
    conduct, pot = extended[0], extended[1]

    halo = reach
    for m in range(moves):
        proposal = prior_keep * conduct + prior_fresh * noise_wide[m]
        once = relax_sweep(proposal, pot, source_wide[reach - halo:source_wide.shape[0] - reach + halo])
        once = inside(once, halo - 1, width)
        twice = relax_sweep(
            proposal[1:-1], once,
            source_wide[reach - halo + 1:source_wide.shape[0] - reach + halo - 1],
        )
        twice = inside(twice, halo - 2, width)
        accepted = accept[m, 0] > 0
        conduct = jnp.where(accepted, proposal, conduct)[2:-2]
        pot = jnp.where(accepted, twice, pot[2:-2])
        halo -= 2

    traces = jnp.transpose(pot, (1, 0, 2)).reshape(ny, width * nz)
    rows_here = traces.shape[1] // lax.axis_size("tile")
    own_start = lax.axis_index("tile") * rows_here
    piece = lax.all_gather(traces, "tile", axis=0, tiled=True)
    columns = lax.dynamic_slice_in_dim(piece, own_start, rows_here, 1)
    product = lax.dot_general(
        columns,
        piece,
        (((0,), (0,)), ((), ())),
        precision=lax.Precision.HIGHEST,
        preferred_element_type=jnp.float32,
    )
    partial_rows = share * product
    parts = lax.all_to_all(
        partial_rows.reshape(particles, rows_here // particles, -1), "grp", 0, 0, tiled=True
    )
    moments = lax.all_gather(jnp.sum(parts, axis=0), "grp", axis=0, tiled=True)
    return (conduct[None], pot[None], moments)


def solution(mesh):
    placed = (
        P("grp", "tile", None, None),
        P("grp", "tile", None, None),
        P(None, "grp", "tile", None, None),
        P("tile", None, None),
        P(),
        P(None, "grp"),
        P("grp"),
    )
    return jax.shard_map(
        local,
        mesh=mesh,
        in_specs=placed,
        out_specs=(P("grp", "tile", None, None), P("grp", "tile", None, None), P("tile", None)),
        check_vma=False,
    )
```

```python
import functools

import jax
import jax.numpy as jnp
from jax import lax
from jax.experimental import pallas as pl
from jax.experimental.pallas import tpu as pltpu
from jax.sharding import PartitionSpec as P

prior_keep = 0.8
prior_fresh = 0.6
relax_weight = 0.8

SMEM = pl.BlockSpec(memory_space=pltpu.SMEM)
VMEM = pl.BlockSpec(memory_space=pltpu.VMEM)
ANY = pl.BlockSpec(memory_space=pl.ANY)


def in_vmem(array):
    return pltpu.with_memory_space_constraint(array, pltpu.VMEM)


def pack_kernel(rows, weight_ref, cond_ref, pot_ref, out_ref, sems):
    copies = []
    for piece in range(out_ref.shape[0]):
        row = piece * rows
        field = cond_ref if row < cond_ref.shape[0] else pot_ref
        row %= cond_ref.shape[0]
        copies.append(
            pltpu.make_async_copy(
                field.at[pl.ds(row, rows)], out_ref.at[piece, pl.ds(0, rows)], sems.at[piece]
            )
        )
    for copy in copies:
        copy.start()
    weight = jnp.full((8, out_ref.shape[2]), weight_ref[0], jnp.float32)
    for piece in range(out_ref.shape[0]):
        out_ref[piece, rows:rows + 8] = weight
    for copy in copies:
        copy.wait()


def pack(weights, log_cond, potential, particles):
    nz = log_cond.shape[-1]
    rows = 2 * log_cond.size // (particles * nz)
    return pl.pallas_call(
        functools.partial(pack_kernel, rows),
        out_shape=pltpu.VMEM((particles, rows + 8, nz), jnp.float32),
        in_specs=[SMEM, ANY, ANY],
        out_specs=VMEM,
        scratch_shapes=[pltpu.SemaphoreType.DMA((particles,))],
        name="pack",
    )(weights, log_cond.reshape(-1, nz), potential.reshape(-1, nz))


def choose_kernel(parents_ref, weight_ref, pieces_ref, chosen_ref, root_ref):
    rows = chosen_ref.shape[1]
    for place in range(chosen_ref.shape[0]):
        chosen_ref[place] = pieces_ref[parents_ref[place], pl.ds(0, rows)]
    total = pieces_ref[0, rows:rows + 8]
    for place in range(1, pieces_ref.shape[0]):
        total += pieces_ref[place, rows:rows + 8]
    root_ref[...] = jnp.sqrt(weight_ref[0] / total)


def choose(parents, weights, pieces):
    particles, rows, nz = pieces.shape
    return pl.pallas_call(
        choose_kernel,
        out_shape=(
            pltpu.VMEM((particles, rows - 8, nz), jnp.float32),
            pltpu.VMEM((8, nz), jnp.float32),
        ),
        in_specs=[SMEM, SMEM, VMEM],
        out_specs=(VMEM, VMEM),
        name="choose",
    )(parents, weights, in_vmem(pieces))


def six_sum(before, here, after, edge):
    row = lax.broadcasted_iota(jnp.int32, here.shape, 0)
    lane = lax.broadcasted_iota(jnp.int32, here.shape, 1)
    ny, nz = here.shape
    down = jnp.where(row == 0, edge, pltpu.roll(here, 1, 0))
    up = jnp.where(row == ny - 1, edge, pltpu.roll(here, ny - 1, 0))
    left = jnp.where(lane == 0, edge, pltpu.roll(here, 1, 1))
    right = jnp.where(lane == nz - 1, edge, pltpu.roll(here, nz - 1, 1))
    return ((before + after) + (down + up)) + (left + right)


def moves_kernel(
    depth, accept_ref, root_ref, moved_ref, low_ref, high_ref, noise_ref, source_ref,
    cond_out, pot_out, traces_out, cond, pot, once, conductivity, gain,
):
    moves, width, _, nz = noise_ref.shape
    reach = 2 * moves
    span = width + 2 * reach
    tile = lax.axis_index("tile")
    first = tile == 0
    last = tile == lax.axis_size("tile") - 1

    def fetch(field, at, h, i):
        if i < 0:
            return low_ref[at + h + i]
        if i >= width:
            return high_ref[at + i - width]
        return field[i]

    def keep_inside(value, i):
        outside = (first & (i < reach)) | (last & (i >= reach + width))
        return jnp.where(outside, 0.0, value)

    for i in range(span):
        cond[i] = fetch(moved_ref.at[0], 0, reach, i - reach)
        pot[i] = fetch(moved_ref.at[1], reach, reach, i - reach)

    source_at = 2 * reach + sum(depth[:moves])
    for m in range(moves):
        start = 2 * m
        noise_at = 2 * reach + sum(depth[:m])
        accepted = accept_ref[m, 0] > 0

        def sweep(old, lo, hi):
            for i in range(lo, hi):
                here, here_k = old[i], conductivity[i]
                before, after = old[i - 1], old[i + 1]
                plain = six_sum(before, here, after, 0.0)
                scaled = six_sum(
                    before * conductivity[i - 1], here * here_k, after * conductivity[i + 1], 0.0
                )
                source = fetch(source_ref, source_at, reach - 1, i - reach)
                value = (1.0 - relax_weight) * here + (
                    2.0 * source + (here_k * plain + scaled)
                ) * gain[i]
                yield i, keep_inside(value, i)

        for i in range(start, span - start):
            proposal = prior_keep * cond[i] + prior_fresh * fetch(
                noise_ref.at[m], noise_at, depth[m], i - reach
            )
            conductivity[i] = jnp.exp(proposal)
            cond[i] = jnp.where(accepted, proposal, cond[i])
        for i in range(start + 1, span - start - 1):
            here_k = conductivity[i]
            gain[i] = relax_weight / (
                6.0 * here_k + six_sum(conductivity[i - 1], here_k, conductivity[i + 1], 1.0)
            )
        for i, value in sweep(pot, start + 1, span - start - 1):
            once[i] = value
        for i, value in sweep(once, start + 2, span - start - 2):
            pot[i] = jnp.where(accepted, value, pot[i])

    root = root_ref[0:1]
    for i in range(width):
        cond_out[i] = cond[i + reach]
        value = pot[i + reach]
        pot_out[i] = value
        traces_out[:, i * nz:(i + 1) * nz] = value * root


def run_moves(depth, accept, root, moved, low, high, noise, source):
    moves, width, ny, nz = noise.shape
    span = width + 4 * moves
    return pl.pallas_call(
        functools.partial(moves_kernel, depth),
        out_shape=(
            pltpu.VMEM((width, ny, nz), jnp.float32),
            pltpu.VMEM((width, ny, nz), jnp.float32),
            pltpu.VMEM((ny, width * nz), jnp.float32),
        ),
        in_specs=[SMEM] + [VMEM] * 6,
        out_specs=(VMEM, VMEM, VMEM),
        scratch_shapes=[pltpu.VMEM((span, ny, nz), jnp.float32)] * 5,
        name="moves",
    )(accept, root, *[in_vmem(a) for a in (moved, low, high, noise, source)])


def exchange_halo(low_edge, high_edge):
    count = lax.axis_size("tile")
    forward = [(i, i + 1) for i in range(count - 1)]
    backward = [(target, source) for source, target in forward]
    low = lax.ppermute(high_edge, "tile", forward)
    high = lax.ppermute(low_edge, "tile", backward)
    return low, high


def local(log_cond, potential, noise, source, parents, accept, weights):
    moves = noise.shape[0]
    width, ny, nz = source.shape
    reach = 2 * moves
    particles = lax.axis_size("grp")

    pieces = pack(weights, log_cond, potential, particles)
    pieces = lax.all_to_all(pieces, "grp", 0, 0, tiled=True)
    chosen, root = choose(parents, weights, pieces)
    moved = lax.all_to_all(chosen, "grp", 0, 0, tiled=True).reshape(2, width, ny, nz)

    fields = [moved[0], moved[1]] + [noise[m, 0] for m in range(moves)] + [source]
    depth = [reach, reach] + [reach - 2 * m for m in range(moves)] + [reach - 1]
    low, high = exchange_halo(
        jnp.concatenate([field[:h] for field, h in zip(fields, depth)]),
        jnp.concatenate([field[width - h:] for field, h in zip(fields, depth)]),
    )
    conduct, pot, traces = run_moves(
        tuple(depth[2:]), accept, root, moved, low, high, noise[:, 0], source
    )

    rows_here = traces.shape[1] // lax.axis_size("tile")
    own_start = lax.axis_index("tile") * rows_here
    piece = lax.all_gather(traces, "tile", axis=0, tiled=True)
    columns = lax.dynamic_slice_in_dim(piece, own_start, rows_here, 1)
    product = lax.dot_general(
        columns,
        piece,
        (((0,), (0,)), ((), ())),
        precision=lax.Precision.HIGHEST,
        preferred_element_type=jnp.float32,
    )
    parts = lax.all_to_all(
        product.reshape(particles, rows_here // particles, -1), "grp", 0, 0, tiled=True
    )
    mine = jnp.sum(parts, axis=0)
    copies = jnp.broadcast_to(mine, (particles,) + mine.shape)
    moments = lax.all_to_all(copies, "grp", 0, 0, tiled=True).reshape(rows_here, -1)
    return (conduct[None], pot[None], moments)


def solution(mesh):
    placed = (
        P("grp", "tile", None, None),
        P("grp", "tile", None, None),
        P(None, "grp", "tile", None, None),
        P("tile", None, None),
        P(),
        P(None, "grp"),
        P("grp"),
    )
    return jax.shard_map(
        local,
        mesh=mesh,
        in_specs=placed,
        out_specs=(P("grp", "tile", None, None), P("grp", "tile", None, None), P("tile", None)),
        check_vma=False,
    )
```

```python
import functools

import jax
import jax.numpy as jnp
from jax import lax
from jax.experimental import pallas as pl
from jax.experimental.pallas import tpu as pltpu
from jax.sharding import PartitionSpec as P

prior_keep = 0.8
prior_fresh = 0.6
relax_weight = 0.8

SMEM = pl.BlockSpec(memory_space=pltpu.SMEM)
VMEM = pl.BlockSpec(memory_space=pltpu.VMEM)
ANY = pl.BlockSpec(memory_space=pl.ANY)


def in_vmem(array):
    return pltpu.with_memory_space_constraint(array, pltpu.VMEM)


def pack_kernel(
    rows, depth, weight_ref, cond_ref, pot_ref, noise_ref, source_ref,
    pieces_ref, noise_out, source_out, low_ref, high_ref, sems,
):
    moves = noise_ref.shape[0]
    pairs = []
    for piece in range(pieces_ref.shape[0]):
        row = piece * rows
        field = cond_ref if row < cond_ref.shape[0] else pot_ref
        row %= cond_ref.shape[0]
        pairs.append((field.at[pl.ds(row, rows)], pieces_ref.at[piece, pl.ds(0, rows)]))
    pairs += [(noise_ref, noise_out), (source_ref, source_out)]
    at = 0
    for field, h in zip([noise_ref.at[m] for m in range(moves)] + [source_ref], depth):
        pairs.append((field.at[pl.ds(0, h)], low_ref.at[pl.ds(at, h)]))
        pairs.append((field.at[pl.ds(field.shape[0] - h, h)], high_ref.at[pl.ds(at, h)]))
        at += h
    copies = [
        pltpu.make_async_copy(here, there, sems.at[i]) for i, (here, there) in enumerate(pairs)
    ]
    for copy in copies:
        copy.start()
    weight = jnp.full((8, pieces_ref.shape[2]), weight_ref[0], jnp.float32)
    for piece in range(pieces_ref.shape[0]):
        pieces_ref[piece, rows:rows + 8] = weight
    for copy in copies:
        copy.wait()


def pack(weights, log_cond, potential, noise, source, particles, depth):
    _, ny, nz = source.shape
    rows = 2 * log_cond.size // (particles * nz)
    edge = pltpu.VMEM((sum(depth), ny, nz), jnp.float32)
    return pl.pallas_call(
        functools.partial(pack_kernel, rows, depth),
        out_shape=(
            pltpu.VMEM((particles, rows + 8, nz), jnp.float32),
            pltpu.VMEM(noise.shape, jnp.float32),
            pltpu.VMEM(source.shape, jnp.float32),
            edge,
            edge,
        ),
        in_specs=[SMEM, ANY, ANY, ANY, ANY],
        out_specs=(VMEM,) * 5,
        scratch_shapes=[pltpu.SemaphoreType.DMA((particles + 2 + 2 * len(depth),))],
        name="pack",
    )(weights, log_cond.reshape(-1, nz), potential.reshape(-1, nz), noise, source)


def choose_kernel(parents_ref, weight_ref, pieces_ref, chosen_ref, root_ref):
    rows = chosen_ref.shape[1]
    for place in range(chosen_ref.shape[0]):
        chosen_ref[place] = pieces_ref[parents_ref[place], pl.ds(0, rows)]
    total = pieces_ref[0, rows:rows + 8]
    for place in range(1, pieces_ref.shape[0]):
        total += pieces_ref[place, rows:rows + 8]
    root_ref[...] = jnp.sqrt(weight_ref[0] / total)


def choose(parents, weights, pieces):
    particles, rows, nz = pieces.shape
    return pl.pallas_call(
        choose_kernel,
        out_shape=(
            pltpu.VMEM((particles, rows - 8, nz), jnp.float32),
            pltpu.VMEM((8, nz), jnp.float32),
        ),
        in_specs=[SMEM, SMEM, VMEM],
        out_specs=(VMEM, VMEM),
        name="choose",
    )(parents, weights, in_vmem(pieces))


def six_sum(before, here, after, edge):
    row = lax.broadcasted_iota(jnp.int32, here.shape, 0)
    lane = lax.broadcasted_iota(jnp.int32, here.shape, 1)
    ny, nz = here.shape
    down = jnp.where(row == 0, edge, pltpu.roll(here, 1, 0))
    up = jnp.where(row == ny - 1, edge, pltpu.roll(here, ny - 1, 0))
    left = jnp.where(lane == 0, edge, pltpu.roll(here, 1, 1))
    right = jnp.where(lane == nz - 1, edge, pltpu.roll(here, nz - 1, 1))
    return ((before + after) + (down + up)) + (left + right)


def moves_kernel(
    depth, accept_ref, root_ref, moved_ref, noise_ref, source_ref,
    moved_low, moved_high, fixed_low, fixed_high,
    cond_out, pot_out, traces_out, cond, pot, once, conductivity, gain,
):
    moves, width, _, nz = noise_ref.shape
    reach = 2 * moves
    span = width + 2 * reach
    tile = lax.axis_index("tile")
    first = tile == 0
    last = tile == lax.axis_size("tile") - 1

    def fetch(field, low, high, at, h, i):
        if i < 0:
            return low[at + h + i]
        if i >= width:
            return high[at + i - width]
        return field[i]

    def keep_inside(value, i):
        outside = (first & (i < reach)) | (last & (i >= reach + width))
        return jnp.where(outside, 0.0, value)

    for i in range(span):
        cond[i] = fetch(moved_ref.at[0], moved_low, moved_high, 0, reach, i - reach)
        pot[i] = fetch(moved_ref.at[1], moved_low, moved_high, reach, reach, i - reach)

    source_at = sum(depth[:moves])
    for m in range(moves):
        start = 2 * m
        noise_at = sum(depth[:m])
        accepted = accept_ref[m] > 0

        def sweep(old, lo, hi):
            for i in range(lo, hi):
                here, here_k = old[i], conductivity[i]
                before, after = old[i - 1], old[i + 1]
                plain = six_sum(before, here, after, 0.0)
                scaled = six_sum(
                    before * conductivity[i - 1], here * here_k, after * conductivity[i + 1], 0.0
                )
                source = fetch(
                    source_ref, fixed_low, fixed_high, source_at, depth[moves], i - reach
                )
                value = (1.0 - relax_weight) * here + (
                    2.0 * source + (here_k * plain + scaled)
                ) * gain[i]
                yield i, keep_inside(value, i)

        for i in range(start, span - start):
            proposal = prior_keep * cond[i] + prior_fresh * fetch(
                noise_ref.at[m], fixed_low, fixed_high, noise_at, depth[m], i - reach
            )
            conductivity[i] = jnp.exp(proposal)
            cond[i] = jnp.where(accepted, proposal, cond[i])
        for i in range(start + 1, span - start - 1):
            here_k = conductivity[i]
            gain[i] = relax_weight / (
                6.0 * here_k + six_sum(conductivity[i - 1], here_k, conductivity[i + 1], 1.0)
            )
        for i, value in sweep(pot, start + 1, span - start - 1):
            once[i] = value
        for i, value in sweep(once, start + 2, span - start - 2):
            pot[i] = jnp.where(accepted, value, pot[i])

    root = root_ref[0:1]
    for i in range(width):
        cond_out[i] = cond[i + reach]
        value = pot[i + reach]
        pot_out[i] = value
        traces_out[:, i * nz:(i + 1) * nz] = value * root


def run_moves(depth, accept, root, *fields):
    moves, width, ny, nz = fields[1].shape
    span = width + 4 * moves
    return pl.pallas_call(
        functools.partial(moves_kernel, depth),
        out_shape=(
            pltpu.VMEM((width, ny, nz), jnp.float32),
            pltpu.VMEM((width, ny, nz), jnp.float32),
            pltpu.VMEM((ny, width * nz), jnp.float32),
        ),
        in_specs=[SMEM] + [VMEM] * (1 + len(fields)),
        out_specs=(VMEM, VMEM, VMEM),
        scratch_shapes=[pltpu.VMEM((span, ny, nz), jnp.float32)] * 5,
        name="moves",
    )(accept, root, *[in_vmem(field) for field in fields])


def sum_copies_kernel(parts_ref, copies_ref):
    total = parts_ref[0]
    for place in range(1, parts_ref.shape[0]):
        total += parts_ref[place]
    for place in range(copies_ref.shape[0]):
        copies_ref[place] = total


def sum_copies(parts):
    return pl.pallas_call(
        sum_copies_kernel,
        out_shape=pltpu.VMEM(parts.shape, jnp.float32),
        in_specs=[VMEM],
        out_specs=VMEM,
        name="sum_copies",
    )(in_vmem(parts))


def exchange_halo(low_edge, high_edge):
    count = lax.axis_size("tile")
    forward = [(i, i + 1) for i in range(count - 1)]
    backward = [(target, source) for source, target in forward]
    low = lax.ppermute(high_edge, "tile", forward)
    high = lax.ppermute(low_edge, "tile", backward)
    return low, high


def local(log_cond, potential, noise, source, parents, accept, weights):
    moves = noise.shape[0]
    width, ny, nz = source.shape
    reach = 2 * moves
    particles = lax.axis_size("grp")

    depth = tuple(reach - 2 * m for m in range(moves)) + (reach - 1,)
    pieces, noise, source, low_edge, high_edge = pack(
        weights, log_cond, potential, noise[:, 0], source, particles, depth
    )
    pieces = lax.all_to_all(pieces, "grp", 0, 0, tiled=True)
    fixed_low, fixed_high = exchange_halo(low_edge, high_edge)
    chosen, root = choose(parents, weights, pieces)
    moved = lax.all_to_all(chosen, "grp", 0, 0, tiled=True).reshape(2, width, ny, nz)
    moved_low, moved_high = exchange_halo(
        moved[:, :reach].reshape(-1, ny, nz), moved[:, width - reach:].reshape(-1, ny, nz)
    )
    conduct, pot, traces = run_moves(
        depth, accept[:, 0], root, moved, noise, source, moved_low, moved_high, fixed_low, fixed_high
    )

    rows_here = traces.shape[1] // lax.axis_size("tile")
    own_start = lax.axis_index("tile") * rows_here
    piece = lax.all_gather(traces, "tile", axis=0, tiled=True)
    columns = lax.dynamic_slice_in_dim(piece, own_start, rows_here, 1)
    product = lax.dot_general(
        columns,
        piece,
        (((0,), (0,)), ((), ())),
        precision=lax.Precision.HIGHEST,
        preferred_element_type=jnp.float32,
    )
    parts = lax.all_to_all(
        product.reshape(particles, rows_here // particles, -1), "grp", 0, 0, tiled=True
    )
    moments = lax.all_to_all(sum_copies(parts), "grp", 0, 0, tiled=True).reshape(rows_here, -1)
    return (conduct[None], pot[None], moments)


def solution(mesh):
    placed = (
        P("grp", "tile", None, None),
        P("grp", "tile", None, None),
        P(None, "grp", "tile", None, None),
        P("tile", None, None),
        P(),
        P(None, "grp"),
        P("grp"),
    )
    return jax.shard_map(
        local,
        mesh=mesh,
        in_specs=placed,
        out_specs=(P("grp", "tile", None, None), P("grp", "tile", None, None), P("tile", None)),
        check_vma=False,
    )
```

```python
import functools

import jax
import jax.numpy as jnp
from jax import lax
from jax.experimental import pallas as pl
from jax.experimental.pallas import tpu as pltpu
from jax.sharding import PartitionSpec as P

prior_keep = 0.8
prior_fresh = 0.6
relax_weight = 0.8
chunks = 2

SMEM = pl.BlockSpec(memory_space=pltpu.SMEM)
VMEM = pl.BlockSpec(memory_space=pltpu.VMEM)
ANY = pl.BlockSpec(memory_space=pl.ANY)


def in_vmem(array):
    return pltpu.with_memory_space_constraint(array, pltpu.VMEM)


def pack_kernel(
    rows, depth, weight_ref, cond_ref, pot_ref, noise_ref, source_ref,
    pieces_ref, noise_out, source_out, low_ref, high_ref, sems,
):
    moves = noise_ref.shape[0]
    pairs = []
    for piece in range(pieces_ref.shape[0]):
        row = piece * rows
        field = cond_ref if row < cond_ref.shape[0] else pot_ref
        row %= cond_ref.shape[0]
        pairs.append((field.at[pl.ds(row, rows)], pieces_ref.at[piece, pl.ds(0, rows)]))
    pairs += [(noise_ref, noise_out), (source_ref, source_out)]
    at = 0
    for field, h in zip([noise_ref.at[m] for m in range(moves)] + [source_ref], depth):
        pairs.append((field.at[pl.ds(0, h)], low_ref.at[pl.ds(at, h)]))
        pairs.append((field.at[pl.ds(field.shape[0] - h, h)], high_ref.at[pl.ds(at, h)]))
        at += h
    copies = [
        pltpu.make_async_copy(here, there, sems.at[i]) for i, (here, there) in enumerate(pairs)
    ]
    for copy in copies:
        copy.start()
    weight = jnp.full((8, pieces_ref.shape[2]), weight_ref[0], jnp.float32)
    for piece in range(pieces_ref.shape[0]):
        pieces_ref[piece, rows:rows + 8] = weight
    for copy in copies:
        copy.wait()


def pack(weights, log_cond, potential, noise, source, particles, depth):
    _, ny, nz = source.shape
    rows = 2 * log_cond.size // (particles * nz)
    edge = pltpu.VMEM((sum(depth), ny, nz), jnp.float32)
    return pl.pallas_call(
        functools.partial(pack_kernel, rows, depth),
        out_shape=(
            pltpu.VMEM((particles, rows + 8, nz), jnp.float32),
            pltpu.VMEM(noise.shape, jnp.float32),
            pltpu.VMEM(source.shape, jnp.float32),
            edge,
            edge,
        ),
        in_specs=[SMEM, ANY, ANY, ANY, ANY],
        out_specs=(VMEM,) * 5,
        scratch_shapes=[pltpu.SemaphoreType.DMA((particles + 2 + 2 * len(depth),))],
        name="pack",
    )(weights, log_cond.reshape(-1, nz), potential.reshape(-1, nz), noise, source)


def choose_kernel(parents_ref, weight_ref, pieces_ref, chosen_ref, root_ref):
    rows = chosen_ref.shape[1]
    for place in range(chosen_ref.shape[0]):
        chosen_ref[place] = pieces_ref[parents_ref[place], pl.ds(0, rows)]
    total = pieces_ref[0, rows:rows + 8]
    for place in range(1, pieces_ref.shape[0]):
        total += pieces_ref[place, rows:rows + 8]
    root_ref[...] = jnp.sqrt(weight_ref[0] / total)


def choose(parents, weights, pieces):
    particles, rows, nz = pieces.shape
    return pl.pallas_call(
        choose_kernel,
        out_shape=(
            pltpu.VMEM((particles, rows - 8, nz), jnp.float32),
            pltpu.VMEM((8, nz), jnp.float32),
        ),
        in_specs=[SMEM, SMEM, VMEM],
        out_specs=(VMEM, VMEM),
        name="choose",
    )(parents, weights, in_vmem(pieces))


def six_sum(before, here, after, edge):
    row = lax.broadcasted_iota(jnp.int32, here.shape, 0)
    lane = lax.broadcasted_iota(jnp.int32, here.shape, 1)
    ny, nz = here.shape
    down = jnp.where(row == 0, edge, pltpu.roll(here, 1, 0))
    up = jnp.where(row == ny - 1, edge, pltpu.roll(here, ny - 1, 0))
    left = jnp.where(lane == 0, edge, pltpu.roll(here, 1, 1))
    right = jnp.where(lane == nz - 1, edge, pltpu.roll(here, nz - 1, 1))
    return ((before + after) + (down + up)) + (left + right)


def moves_kernel(
    depth, accept_ref, root_ref, moved_ref, noise_ref, source_ref,
    moved_low, moved_high, fixed_low, fixed_high,
    cond_out, pot_out, traces_out, cond, pot, once, conductivity, gain,
):
    moves, width, _, nz = noise_ref.shape
    reach = 2 * moves
    span = width + 2 * reach
    tile = lax.axis_index("tile")
    first = tile == 0
    last = tile == lax.axis_size("tile") - 1

    def fetch(field, low, high, at, h, i):
        if i < 0:
            return low[at + h + i]
        if i >= width:
            return high[at + i - width]
        return field[i]

    def keep_inside(value, i):
        outside = (first & (i < reach)) | (last & (i >= reach + width))
        return jnp.where(outside, 0.0, value)

    for i in range(span):
        cond[i] = fetch(moved_ref.at[0], moved_low, moved_high, 0, reach, i - reach)
        pot[i] = fetch(moved_ref.at[1], moved_low, moved_high, reach, reach, i - reach)

    source_at = sum(depth[:moves])
    for m in range(moves):
        start = 2 * m
        noise_at = sum(depth[:m])
        accepted = accept_ref[m] > 0

        def sweep(old, lo, hi):
            for i in range(lo, hi):
                here, here_k = old[i], conductivity[i]
                before, after = old[i - 1], old[i + 1]
                plain = six_sum(before, here, after, 0.0)
                scaled = six_sum(
                    before * conductivity[i - 1], here * here_k, after * conductivity[i + 1], 0.0
                )
                source = fetch(
                    source_ref, fixed_low, fixed_high, source_at, depth[moves], i - reach
                )
                value = (1.0 - relax_weight) * here + (
                    2.0 * source + (here_k * plain + scaled)
                ) * gain[i]
                yield i, keep_inside(value, i)

        for i in range(start, span - start):
            proposal = prior_keep * cond[i] + prior_fresh * fetch(
                noise_ref.at[m], fixed_low, fixed_high, noise_at, depth[m], i - reach
            )
            conductivity[i] = jnp.exp(proposal)
            cond[i] = jnp.where(accepted, proposal, cond[i])
        for i in range(start + 1, span - start - 1):
            here_k = conductivity[i]
            gain[i] = relax_weight / (
                6.0 * here_k + six_sum(conductivity[i - 1], here_k, conductivity[i + 1], 1.0)
            )
        for i, value in sweep(pot, start + 1, span - start - 1):
            once[i] = value
        for i, value in sweep(once, start + 2, span - start - 2):
            pot[i] = jnp.where(accepted, value, pot[i])

    root = root_ref[0:1]
    for i in range(width):
        cond_out[i] = cond[i + reach]
        value = pot[i + reach]
        pot_out[i] = value
        traces_out[:, i * nz:(i + 1) * nz] = value * root


def run_moves(depth, accept, root, *fields):
    moves, width, ny, nz = fields[1].shape
    span = width + 4 * moves
    return pl.pallas_call(
        functools.partial(moves_kernel, depth),
        out_shape=(
            pltpu.VMEM((width, ny, nz), jnp.float32),
            pltpu.VMEM((width, ny, nz), jnp.float32),
            pltpu.VMEM((ny, width * nz), jnp.float32),
        ),
        in_specs=[SMEM] + [VMEM] * (1 + len(fields)),
        out_specs=(VMEM, VMEM, VMEM),
        scratch_shapes=[pltpu.VMEM((span, ny, nz), jnp.float32)] * 5,
        name="moves",
    )(accept, in_vmem(root), *[in_vmem(field) for field in fields])


def sum_copies_kernel(parts_ref, copies_ref):
    total = parts_ref[0]
    for place in range(1, parts_ref.shape[0]):
        total += parts_ref[place]
    for place in range(copies_ref.shape[0]):
        copies_ref[place] = total


def sum_copies(parts):
    return pl.pallas_call(
        sum_copies_kernel,
        out_shape=pltpu.VMEM(parts.shape, jnp.float32),
        in_specs=[VMEM],
        out_specs=VMEM,
        name="sum_copies",
    )(in_vmem(parts))


def exchange_halo(low_edge, high_edge):
    count = lax.axis_size("tile")
    forward = [(i, i + 1) for i in range(count - 1)]
    backward = [(target, source) for source, target in forward]
    low = lax.ppermute(high_edge, "tile", forward)
    high = lax.ppermute(low_edge, "tile", backward)
    return low, high


def local(log_cond, potential, noise, source, parents, accept, weights):
    moves = noise.shape[0]
    width, ny, nz = source.shape
    reach = 2 * moves
    particles = lax.axis_size("grp")

    depth = tuple(reach - 2 * m for m in range(moves)) + (reach - 1,)
    pieces, noise, source, low_edge, high_edge = pack(
        weights, log_cond, potential, noise[:, 0], source, particles, depth
    )
    pieces = lax.all_to_all(pieces, "grp", 0, 0, tiled=True)
    fixed_low, fixed_high = exchange_halo(low_edge, high_edge)
    chosen, root = choose(parents, weights, pieces)
    moved = lax.all_to_all(chosen, "grp", 0, 0, tiled=True).reshape(2, width, ny, nz)
    moved_low, moved_high = exchange_halo(
        moved[:, :reach].reshape(-1, ny, nz), moved[:, width - reach:].reshape(-1, ny, nz)
    )
    conduct, pot, traces = run_moves(
        depth, accept[:, 0], root, moved, noise, source, moved_low, moved_high, fixed_low, fixed_high
    )

    rows_here = traces.shape[1] // lax.axis_size("tile")
    own_start = lax.axis_index("tile") * rows_here
    piece = lax.all_gather(traces, "tile", axis=0, tiled=True)
    columns = lax.dynamic_slice_in_dim(piece, own_start, rows_here, 1)
    wide = traces.shape[1] // chunks
    finished = []
    for chunk in range(chunks):
        product = lax.dot_general(
            columns,
            piece[:, chunk * wide:(chunk + 1) * wide],
            (((0,), (0,)), ((), ())),
            precision=lax.Precision.HIGHEST,
            preferred_element_type=jnp.float32,
        )
        parts = lax.all_to_all(
            product.reshape(particles, rows_here // particles, wide), "grp", 0, 0, tiled=True
        )
        finished.append(
            lax.all_to_all(sum_copies(parts), "grp", 0, 0, tiled=True).reshape(rows_here, wide)
        )
    moments = jnp.concatenate(finished, axis=1)
    return (conduct[None], pot[None], moments)


def solution(mesh):
    placed = (
        P("grp", "tile", None, None),
        P("grp", "tile", None, None),
        P(None, "grp", "tile", None, None),
        P("tile", None, None),
        P(),
        P(None, "grp"),
        P("grp"),
    )
    return jax.shard_map(
        local,
        mesh=mesh,
        in_specs=placed,
        out_specs=(P("grp", "tile", None, None), P("grp", "tile", None, None), P("tile", None)),
        check_vma=False,
    )
```

```python
import functools

import jax
import jax.numpy as jnp
from jax import lax
from jax.experimental import pallas as pl
from jax.experimental.pallas import tpu as pltpu
from jax.sharding import PartitionSpec as P

prior_keep = 0.8
prior_fresh = 0.6
relax_weight = 0.8
pair = 2
group = ("pairs", "member")

SMEM = pl.BlockSpec(memory_space=pltpu.SMEM)
VMEM = pl.BlockSpec(memory_space=pltpu.VMEM)
ANY = pl.BlockSpec(memory_space=pl.ANY)


def in_vmem(array):
    return pltpu.with_memory_space_constraint(array, pltpu.VMEM)


def pack_kernel(
    rows, depth, weight_ref, cond_ref, pot_ref, noise_ref, source_ref,
    pieces_ref, noise_out, source_out, low_ref, high_ref, sems,
):
    moves = noise_ref.shape[0]
    pairs = []
    for piece in range(pieces_ref.shape[0]):
        row = piece * rows
        field = cond_ref if row < cond_ref.shape[0] else pot_ref
        row %= cond_ref.shape[0]
        pairs.append((field.at[pl.ds(row, rows)], pieces_ref.at[piece, pl.ds(0, rows)]))
    pairs += [(noise_ref, noise_out), (source_ref, source_out)]
    at = 0
    for field, h in zip([noise_ref.at[m] for m in range(moves)] + [source_ref], depth):
        pairs.append((field.at[pl.ds(0, h)], low_ref.at[pl.ds(at, h)]))
        pairs.append((field.at[pl.ds(field.shape[0] - h, h)], high_ref.at[pl.ds(at, h)]))
        at += h
    copies = [
        pltpu.make_async_copy(here, there, sems.at[i]) for i, (here, there) in enumerate(pairs)
    ]
    for copy in copies:
        copy.start()
    weight = jnp.full((8, pieces_ref.shape[2]), weight_ref[0], jnp.float32)
    for piece in range(pieces_ref.shape[0]):
        pieces_ref[piece, rows:rows + 8] = weight
    for copy in copies:
        copy.wait()


def pack(weights, log_cond, potential, noise, source, particles, depth):
    _, ny, nz = source.shape
    rows = 2 * log_cond.size // (particles * nz)
    edge = pltpu.VMEM((sum(depth), ny, nz), jnp.float32)
    return pl.pallas_call(
        functools.partial(pack_kernel, rows, depth),
        out_shape=(
            pltpu.VMEM((particles, rows + 8, nz), jnp.float32),
            pltpu.VMEM(noise.shape, jnp.float32),
            pltpu.VMEM(source.shape, jnp.float32),
            edge,
            edge,
        ),
        in_specs=[SMEM, ANY, ANY, ANY, ANY],
        out_specs=(VMEM,) * 5,
        scratch_shapes=[pltpu.SemaphoreType.DMA((particles + 2 + 2 * len(depth),))],
        name="pack",
    )(weights, log_cond.reshape(-1, nz), potential.reshape(-1, nz), noise, source)


def choose_kernel(parents_ref, weight_ref, pieces_ref, chosen_ref, root_ref):
    rows = chosen_ref.shape[1]
    for place in range(chosen_ref.shape[0]):
        chosen_ref[place] = pieces_ref[parents_ref[place], pl.ds(0, rows)]
    total = pieces_ref[0, rows:rows + 8]
    for place in range(1, pieces_ref.shape[0]):
        total += pieces_ref[place, rows:rows + 8]
    root_ref[...] = jnp.sqrt(weight_ref[0] / total)


def choose(parents, weights, pieces):
    particles, rows, nz = pieces.shape
    return pl.pallas_call(
        choose_kernel,
        out_shape=(
            pltpu.VMEM((particles, rows - 8, nz), jnp.float32),
            pltpu.VMEM((8, nz), jnp.float32),
        ),
        in_specs=[SMEM, SMEM, VMEM],
        out_specs=(VMEM, VMEM),
        name="choose",
    )(parents, weights, in_vmem(pieces))


def six_sum(before, here, after, edge):
    row = lax.broadcasted_iota(jnp.int32, here.shape, 0)
    lane = lax.broadcasted_iota(jnp.int32, here.shape, 1)
    ny, nz = here.shape
    down = jnp.where(row == 0, edge, pltpu.roll(here, 1, 0))
    up = jnp.where(row == ny - 1, edge, pltpu.roll(here, ny - 1, 0))
    left = jnp.where(lane == 0, edge, pltpu.roll(here, 1, 1))
    right = jnp.where(lane == nz - 1, edge, pltpu.roll(here, nz - 1, 1))
    return ((before + after) + (down + up)) + (left + right)


def moves_kernel(
    depth, accept_ref, root_ref, moved_ref, noise_ref, source_ref,
    moved_low, moved_high, fixed_low, fixed_high,
    cond_out, pot_out, traces_out, cond, pot, once, conductivity, gain,
):
    moves, width, _, nz = noise_ref.shape
    reach = 2 * moves
    span = width + 2 * reach
    tile = lax.axis_index("tile")
    first = tile == 0
    last = tile == lax.axis_size("tile") - 1

    def fetch(field, low, high, at, h, i):
        if i < 0:
            return low[at + h + i]
        if i >= width:
            return high[at + i - width]
        return field[i]

    def keep_inside(value, i):
        outside = (first & (i < reach)) | (last & (i >= reach + width))
        return jnp.where(outside, 0.0, value)

    for i in range(span):
        cond[i] = fetch(moved_ref.at[0], moved_low, moved_high, 0, reach, i - reach)
        pot[i] = fetch(moved_ref.at[1], moved_low, moved_high, reach, reach, i - reach)

    source_at = sum(depth[:moves])
    for m in range(moves):
        start = 2 * m
        noise_at = sum(depth[:m])
        accepted = accept_ref[m] > 0

        def sweep(old, lo, hi):
            for i in range(lo, hi):
                here, here_k = old[i], conductivity[i]
                before, after = old[i - 1], old[i + 1]
                plain = six_sum(before, here, after, 0.0)
                scaled = six_sum(
                    before * conductivity[i - 1], here * here_k, after * conductivity[i + 1], 0.0
                )
                source = fetch(
                    source_ref, fixed_low, fixed_high, source_at, depth[moves], i - reach
                )
                value = (1.0 - relax_weight) * here + (
                    2.0 * source + (here_k * plain + scaled)
                ) * gain[i]
                yield i, keep_inside(value, i)

        for i in range(start, span - start):
            proposal = prior_keep * cond[i] + prior_fresh * fetch(
                noise_ref.at[m], fixed_low, fixed_high, noise_at, depth[m], i - reach
            )
            conductivity[i] = jnp.exp(proposal)
            cond[i] = jnp.where(accepted, proposal, cond[i])
        for i in range(start + 1, span - start - 1):
            here_k = conductivity[i]
            gain[i] = relax_weight / (
                6.0 * here_k + six_sum(conductivity[i - 1], here_k, conductivity[i + 1], 1.0)
            )
        for i, value in sweep(pot, start + 1, span - start - 1):
            once[i] = value
        for i, value in sweep(once, start + 2, span - start - 2):
            pot[i] = jnp.where(accepted, value, pot[i])

    root = root_ref[0:1]
    for i in range(width):
        cond_out[i] = cond[i + reach]
        value = pot[i + reach]
        pot_out[i] = value
        traces_out[:, i * nz:(i + 1) * nz] = value * root


def run_moves(depth, accept, root, *fields):
    moves, width, ny, nz = fields[1].shape
    span = width + 4 * moves
    return pl.pallas_call(
        functools.partial(moves_kernel, depth),
        out_shape=(
            pltpu.VMEM((width, ny, nz), jnp.float32),
            pltpu.VMEM((width, ny, nz), jnp.float32),
            pltpu.VMEM((ny, width * nz), jnp.float32),
        ),
        in_specs=[SMEM] + [VMEM] * (1 + len(fields)),
        out_specs=(VMEM, VMEM, VMEM),
        scratch_shapes=[pltpu.VMEM((span, ny, nz), jnp.float32)] * 5,
        name="moves",
    )(accept, in_vmem(root), *[in_vmem(field) for field in fields])


def sum_copies_kernel(parts_ref, copies_ref):
    total = parts_ref[0]
    for place in range(1, parts_ref.shape[0]):
        total += parts_ref[place]
    for place in range(copies_ref.shape[0]):
        copies_ref[place] = total


def sum_copies(parts):
    return pl.pallas_call(
        sum_copies_kernel,
        out_shape=pltpu.VMEM(parts.shape, jnp.float32),
        in_specs=[VMEM],
        out_specs=VMEM,
        name="sum_copies",
    )(in_vmem(parts))


def interleave_kernel(mine_ref, other_ref, out_ref, sems):
    member = lax.axis_index("member")
    copies = [
        pltpu.make_async_copy(mine_ref, out_ref.at[:, member], sems.at[0]),
        pltpu.make_async_copy(other_ref, out_ref.at[:, 1 - member], sems.at[1]),
    ]
    for copy in copies:
        copy.start()
    for copy in copies:
        copy.wait()


def interleave(mine, other):
    return pl.pallas_call(
        interleave_kernel,
        out_shape=jax.ShapeDtypeStruct(
            (mine.shape[0], pair) + mine.shape[1:], jnp.float32
        ),
        in_specs=[VMEM, VMEM],
        out_specs=ANY,
        scratch_shapes=[pltpu.SemaphoreType.DMA((2,))],
        name="interleave",
    )(in_vmem(mine), in_vmem(other))


def exchange_halo(low_edge, high_edge):
    count = lax.axis_size("tile")
    forward = [(i, i + 1) for i in range(count - 1)]
    backward = [(target, source) for source, target in forward]
    low = lax.ppermute(high_edge, "tile", forward)
    high = lax.ppermute(low_edge, "tile", backward)
    return low, high


def swap(block):
    return lax.ppermute(block, "member", [(0, 1), (1, 0)])


def local(log_cond, potential, noise, source, parents, accept, weights):
    moves = noise.shape[0]
    width, ny, nz = source.shape
    reach = 2 * moves
    particles = lax.axis_size(group)

    depth = tuple(reach - 2 * m for m in range(moves)) + (reach - 1,)
    pieces, noise, source, low_edge, high_edge = pack(
        weights, log_cond, potential, noise[:, 0], source, particles, depth
    )
    pieces = lax.all_to_all(pieces, group, 0, 0, tiled=True)
    fixed_low, fixed_high = exchange_halo(low_edge, high_edge)
    chosen, root = choose(parents, weights, pieces)
    moved = lax.all_to_all(chosen, group, 0, 0, tiled=True).reshape(2, width, ny, nz)
    moved_low, moved_high = exchange_halo(
        moved[:, :reach].reshape(-1, ny, nz), moved[:, width - reach:].reshape(-1, ny, nz)
    )
    conduct, pot, traces = run_moves(
        depth, accept[:, 0], root, moved, noise, source, moved_low, moved_high, fixed_low, fixed_high
    )

    rows_here = traces.shape[1] // lax.axis_size("tile")
    own_start = lax.axis_index("tile") * rows_here
    piece = lax.all_gather(traces, "tile", axis=0, tiled=True)
    columns = lax.dynamic_slice_in_dim(piece, own_start, rows_here, 1)
    product = lax.dot_general(
        columns,
        piece,
        (((0,), (0,)), ((), ())),
        precision=lax.Precision.HIGHEST,
        preferred_element_type=jnp.float32,
    )
    member = lax.axis_index("member")
    blocks = product.reshape(particles // pair, pair, rows_here // particles, -1)
    keep = lax.dynamic_index_in_dim(blocks, member, 1, keepdims=False)
    give = lax.dynamic_index_in_dim(blocks, 1 - member, 1, keepdims=False)
    parts = lax.all_to_all(keep + swap(give), "pairs", 0, 0, tiled=True)
    mine = lax.all_to_all(sum_copies(parts), "pairs", 0, 0, tiled=True)
    other = swap(mine)
    moments = interleave(mine, other).reshape(rows_here, -1)
    return (conduct[None], pot[None], moments)


def solution(mesh):
    tiles = mesh.shape["tile"]
    split = jax.sharding.Mesh(
        mesh.devices.reshape(-1, pair, tiles), ("pairs", "member", "tile")
    )
    placed = (
        P(group, "tile", None, None),
        P(group, "tile", None, None),
        P(None, group, "tile", None, None),
        P("tile", None, None),
        P(),
        P(None, group),
        P(group),
    )
    return jax.shard_map(
        local,
        mesh=split,
        in_specs=placed,
        out_specs=(P(group, "tile", None, None), P(group, "tile", None, None), P("tile", None)),
        check_vma=False,
    )
```

```python
import functools

import jax
import jax.numpy as jnp
from jax import lax
from jax.experimental import pallas as pl
from jax.experimental.pallas import tpu as pltpu
from jax.sharding import PartitionSpec as P

prior_keep = 0.8
prior_fresh = 0.6
relax_weight = 0.8
pair = 2
group = ("pairs", "member")

SMEM = pl.BlockSpec(memory_space=pltpu.SMEM)
VMEM = pl.BlockSpec(memory_space=pltpu.VMEM)
ANY = pl.BlockSpec(memory_space=pl.ANY)


def in_vmem(array):
    return pltpu.with_memory_space_constraint(array, pltpu.VMEM)


def pack_kernel(
    rows, depth, weight_ref, cond_ref, pot_ref, noise_ref, source_ref,
    pieces_ref, noise_out, source_out, low_ref, high_ref, sems,
):
    moves = noise_ref.shape[0]
    pairs = []
    for piece in range(pieces_ref.shape[0]):
        row = piece * rows
        field = cond_ref if row < cond_ref.shape[0] else pot_ref
        row %= cond_ref.shape[0]
        pairs.append((field.at[pl.ds(row, rows)], pieces_ref.at[piece, pl.ds(0, rows)]))
    pairs += [(noise_ref, noise_out), (source_ref, source_out)]
    at = 0
    for field, h in zip([noise_ref.at[m] for m in range(moves)] + [source_ref], depth):
        pairs.append((field.at[pl.ds(0, h)], low_ref.at[pl.ds(at, h)]))
        pairs.append((field.at[pl.ds(field.shape[0] - h, h)], high_ref.at[pl.ds(at, h)]))
        at += h
    copies = [
        pltpu.make_async_copy(here, there, sems.at[i]) for i, (here, there) in enumerate(pairs)
    ]
    for copy in copies:
        copy.start()
    weight = jnp.full((8, pieces_ref.shape[2]), weight_ref[0], jnp.float32)
    for piece in range(pieces_ref.shape[0]):
        pieces_ref[piece, rows:rows + 8] = weight
    for copy in copies:
        copy.wait()


def pack(weights, log_cond, potential, noise, source, pairs, depth):
    _, ny, nz = source.shape
    rows = 2 * log_cond.size // (pairs * nz)
    edge = pltpu.VMEM((sum(depth), ny, nz), jnp.float32)
    return pl.pallas_call(
        functools.partial(pack_kernel, rows, depth),
        out_shape=(
            pltpu.VMEM((pairs, rows + 8, nz), jnp.float32),
            pltpu.VMEM(noise.shape, jnp.float32),
            pltpu.VMEM(source.shape, jnp.float32),
            edge,
            edge,
        ),
        in_specs=[SMEM, ANY, ANY, ANY, ANY],
        out_specs=(VMEM,) * 5,
        scratch_shapes=[pltpu.SemaphoreType.DMA((pairs + 2 + 2 * len(depth),))],
        name="pack",
    )(weights, log_cond.reshape(-1, nz), potential.reshape(-1, nz), noise, source)


def choose_kernel(parents_ref, weight_ref, mine_ref, other_ref, chosen_ref, root_ref):
    member = lax.axis_index("member")
    rows = chosen_ref.shape[1]
    for place in range(chosen_ref.shape[0]):
        parent = parents_ref[place * pair + member]
        here = lax.rem(parent, pair) == member
        at = lax.div(parent, pair)
        chosen_ref[place] = jnp.where(
            here, mine_ref[at, pl.ds(0, rows)], other_ref[at, pl.ds(0, rows)]
        )
    total = jnp.zeros_like(root_ref)
    for place in range(chosen_ref.shape[0]):
        total += mine_ref[place, rows:rows + 8] + other_ref[place, rows:rows + 8]
    root_ref[...] = jnp.sqrt(weight_ref[0] / total)


def choose(parents, weights, mine, other):
    pairs, rows, nz = mine.shape
    return pl.pallas_call(
        choose_kernel,
        out_shape=(
            pltpu.VMEM((pairs, rows - 8, nz), jnp.float32),
            pltpu.VMEM((8, nz), jnp.float32),
        ),
        in_specs=[SMEM, SMEM, VMEM, VMEM],
        out_specs=(VMEM, VMEM),
        name="choose",
    )(parents, weights, in_vmem(mine), in_vmem(other))


def six_sum(before, here, after, edge):
    row = lax.broadcasted_iota(jnp.int32, here.shape, 0)
    lane = lax.broadcasted_iota(jnp.int32, here.shape, 1)
    ny, nz = here.shape
    down = jnp.where(row == 0, edge, pltpu.roll(here, 1, 0))
    up = jnp.where(row == ny - 1, edge, pltpu.roll(here, ny - 1, 0))
    left = jnp.where(lane == 0, edge, pltpu.roll(here, 1, 1))
    right = jnp.where(lane == nz - 1, edge, pltpu.roll(here, nz - 1, 1))
    return ((before + after) + (down + up)) + (left + right)


def moves_kernel(
    depth, accept_ref, root_ref, moved_ref, noise_ref, source_ref,
    moved_low, moved_high, fixed_low, fixed_high,
    cond_out, pot_out, traces_out, cond, pot, once, conductivity, gain,
):
    moves, width, _, nz = noise_ref.shape
    reach = 2 * moves
    span = width + 2 * reach
    tile = lax.axis_index("tile")
    first = tile == 0
    last = tile == lax.axis_size("tile") - 1

    def fetch(field, low, high, at, h, i):
        if i < 0:
            return low[at + h + i]
        if i >= width:
            return high[at + i - width]
        return field[i]

    def keep_inside(value, i):
        outside = (first & (i < reach)) | (last & (i >= reach + width))
        return jnp.where(outside, 0.0, value)

    for i in range(span):
        cond[i] = fetch(moved_ref.at[0], moved_low, moved_high, 0, reach, i - reach)
        pot[i] = fetch(moved_ref.at[1], moved_low, moved_high, reach, reach, i - reach)

    source_at = sum(depth[:moves])
    for m in range(moves):
        start = 2 * m
        noise_at = sum(depth[:m])
        accepted = accept_ref[m] > 0

        def sweep(old, lo, hi):
            for i in range(lo, hi):
                here, here_k = old[i], conductivity[i]
                before, after = old[i - 1], old[i + 1]
                plain = six_sum(before, here, after, 0.0)
                scaled = six_sum(
                    before * conductivity[i - 1], here * here_k, after * conductivity[i + 1], 0.0
                )
                source = fetch(
                    source_ref, fixed_low, fixed_high, source_at, depth[moves], i - reach
                )
                value = (1.0 - relax_weight) * here + (
                    2.0 * source + (here_k * plain + scaled)
                ) * gain[i]
                yield i, keep_inside(value, i)

        for i in range(start, span - start):
            proposal = prior_keep * cond[i] + prior_fresh * fetch(
                noise_ref.at[m], fixed_low, fixed_high, noise_at, depth[m], i - reach
            )
            conductivity[i] = jnp.exp(proposal)
            cond[i] = jnp.where(accepted, proposal, cond[i])
        for i in range(start + 1, span - start - 1):
            here_k = conductivity[i]
            gain[i] = relax_weight / (
                6.0 * here_k + six_sum(conductivity[i - 1], here_k, conductivity[i + 1], 1.0)
            )
        for i, value in sweep(pot, start + 1, span - start - 1):
            once[i] = value
        for i, value in sweep(once, start + 2, span - start - 2):
            pot[i] = jnp.where(accepted, value, pot[i])

    root = root_ref[0:1]
    for i in range(width):
        cond_out[i] = cond[i + reach]
        value = pot[i + reach]
        pot_out[i] = value
        traces_out[:, i * nz:(i + 1) * nz] = value * root


def run_moves(depth, accept, root, *fields):
    moves, width, ny, nz = fields[1].shape
    span = width + 4 * moves
    return pl.pallas_call(
        functools.partial(moves_kernel, depth),
        out_shape=(
            pltpu.VMEM((width, ny, nz), jnp.float32),
            pltpu.VMEM((width, ny, nz), jnp.float32),
            pltpu.VMEM((ny, width * nz), jnp.float32),
        ),
        in_specs=[SMEM] + [VMEM] * (1 + len(fields)),
        out_specs=(VMEM, VMEM, VMEM),
        scratch_shapes=[pltpu.VMEM((span, ny, nz), jnp.float32)] * 5,
        name="moves",
    )(accept, in_vmem(root), *[in_vmem(field) for field in fields])


def sum_copies_kernel(parts_ref, copies_ref):
    total = parts_ref[0]
    for place in range(1, parts_ref.shape[0]):
        total += parts_ref[place]
    for place in range(copies_ref.shape[0]):
        copies_ref[place] = total


def sum_copies(parts):
    return pl.pallas_call(
        sum_copies_kernel,
        out_shape=pltpu.VMEM(parts.shape, jnp.float32),
        in_specs=[VMEM],
        out_specs=VMEM,
        name="sum_copies",
    )(in_vmem(parts))


def join_kernel(mine_ref, other_ref, out_ref, sems):
    member = lax.axis_index("member")
    rows = mine_ref.shape[0]
    copies = [
        pltpu.make_async_copy(
            ref, out_ref.at[pl.ds(pl.multiple_of(owner * rows, rows), rows)], sems.at[i]
        )
        for i, (ref, owner) in enumerate([(mine_ref, member), (other_ref, 1 - member)])
    ]
    for copy in copies:
        copy.start()
    for copy in copies:
        copy.wait()


def join(mine, other):
    return pl.pallas_call(
        join_kernel,
        out_shape=jax.ShapeDtypeStruct((pair * mine.shape[0], mine.shape[1]), jnp.float32),
        in_specs=[VMEM, VMEM],
        out_specs=ANY,
        scratch_shapes=[pltpu.SemaphoreType.DMA((2,))],
        name="join",
    )(in_vmem(mine), in_vmem(other))


def exchange_halo(low_edge, high_edge):
    count = lax.axis_size("tile")
    forward = [(i, i + 1) for i in range(count - 1)]
    backward = [(target, source) for source, target in forward]
    low = lax.ppermute(high_edge, "tile", forward)
    high = lax.ppermute(low_edge, "tile", backward)
    return low, high


def swap(block):
    return lax.ppermute(block, "member", [(0, 1), (1, 0)])


def local(log_cond, potential, noise, source, parents, accept, weights):
    moves = noise.shape[0]
    width, ny, nz = source.shape
    reach = 2 * moves

    depth = tuple(reach - 2 * m for m in range(moves)) + (reach - 1,)
    pieces, noise, source, low_edge, high_edge = pack(
        weights, log_cond, potential, noise[:, 0], source, lax.axis_size("pairs"), depth
    )
    pieces = lax.all_to_all(pieces, "pairs", 0, 0, tiled=True)
    fixed_low, fixed_high = exchange_halo(low_edge, high_edge)
    chosen, root = choose(parents, weights, pieces, swap(pieces))
    moved = lax.all_to_all(chosen, "pairs", 0, 0, tiled=True).reshape(2, width, ny, nz)
    moved_low, moved_high = exchange_halo(
        moved[:, :reach].reshape(-1, ny, nz), moved[:, width - reach:].reshape(-1, ny, nz)
    )
    conduct, pot, traces = run_moves(
        depth, accept[:, 0], root, moved, noise, source, moved_low, moved_high, fixed_low, fixed_high
    )

    rows = traces.shape[1] // (lax.axis_size("tile") * pair)
    member = lax.axis_index("member")
    piece = lax.all_gather(traces, "tile", axis=0, tiled=True)

    def product(owner):
        columns = lax.dynamic_slice_in_dim(
            piece, (lax.axis_index("tile") * pair + owner) * rows, rows, 1
        )
        return lax.dot_general(
            columns,
            piece,
            (((0,), (0,)), ((), ())),
            precision=lax.Precision.HIGHEST,
            preferred_element_type=jnp.float32,
        ).reshape(lax.axis_size("pairs"), -1, piece.shape[1])

    got = swap(product(1 - member))
    parts = lax.all_to_all(product(member) + got, "pairs", 0, 0, tiled=True)
    mine = lax.all_to_all(sum_copies(parts), "pairs", 0, 0, tiled=True)
    moments = join(mine.reshape(rows, -1), swap(mine).reshape(rows, -1))
    return (conduct[None], pot[None], moments)


def solution(mesh):
    tiles = mesh.shape["tile"]
    split = jax.sharding.Mesh(
        mesh.devices.reshape(-1, pair, tiles), ("pairs", "member", "tile")
    )
    placed = (
        P(group, "tile", None, None),
        P(group, "tile", None, None),
        P(None, group, "tile", None, None),
        P("tile", None, None),
        P(),
        P(None, group),
        P(group),
    )
    return jax.shard_map(
        local,
        mesh=split,
        in_specs=placed,
        out_specs=(P(group, "tile", None, None), P(group, "tile", None, None), P("tile", None)),
        check_vma=False,
    )
```

```python
import functools

import jax
import jax.numpy as jnp
from jax import lax
from jax.experimental import pallas as pl
from jax.experimental.pallas import tpu as pltpu
from jax.sharding import PartitionSpec as P

prior_keep = 0.8
prior_fresh = 0.6
relax_weight = 0.8
pair = 2
group = ("pairs", "member")

SMEM = pl.BlockSpec(memory_space=pltpu.SMEM)
VMEM = pl.BlockSpec(memory_space=pltpu.VMEM)
ANY = pl.BlockSpec(memory_space=pl.ANY)


def in_vmem(array):
    return pltpu.with_memory_space_constraint(array, pltpu.VMEM)


def pack_kernel(
    rows, depth, weight_ref, cond_ref, pot_ref, noise_ref, source_ref,
    pieces_ref, noise_out, source_out, low_ref, high_ref, sems,
):
    moves = noise_ref.shape[0]
    pairs = []
    for piece in range(pieces_ref.shape[0]):
        row = piece * rows
        field = cond_ref if row < cond_ref.shape[0] else pot_ref
        row %= cond_ref.shape[0]
        pairs.append((field.at[pl.ds(row, rows)], pieces_ref.at[piece, pl.ds(0, rows)]))
    pairs += [(noise_ref, noise_out), (source_ref, source_out)]
    at = 0
    for field, h in zip([noise_ref.at[m] for m in range(moves)] + [source_ref], depth):
        pairs.append((field.at[pl.ds(0, h)], low_ref.at[pl.ds(at, h)]))
        pairs.append((field.at[pl.ds(field.shape[0] - h, h)], high_ref.at[pl.ds(at, h)]))
        at += h
    copies = [
        pltpu.make_async_copy(here, there, sems.at[i]) for i, (here, there) in enumerate(pairs)
    ]
    for copy in copies:
        copy.start()
    weight = jnp.full((8, pieces_ref.shape[2]), weight_ref[0], jnp.float32)
    for piece in range(pieces_ref.shape[0]):
        pieces_ref[piece, rows:rows + 8] = weight
    for copy in copies:
        copy.wait()


def pack(weights, log_cond, potential, noise, source, pairs, depth):
    _, ny, nz = source.shape
    rows = 2 * log_cond.size // (pairs * nz)
    edge = pltpu.VMEM((sum(depth), ny, nz), jnp.float32)
    return pl.pallas_call(
        functools.partial(pack_kernel, rows, depth),
        out_shape=(
            pltpu.VMEM((pairs, rows + 8, nz), jnp.float32),
            pltpu.VMEM(noise.shape, jnp.float32),
            pltpu.VMEM(source.shape, jnp.float32),
            edge,
            edge,
        ),
        in_specs=[SMEM, ANY, ANY, ANY, ANY],
        out_specs=(VMEM,) * 5,
        scratch_shapes=[pltpu.SemaphoreType.DMA((pairs + 2 + 2 * len(depth),))],
        name="pack",
    )(weights, log_cond.reshape(-1, nz), potential.reshape(-1, nz), noise, source)


def choose_kernel(parents_ref, weight_ref, mine_ref, other_ref, chosen_ref, root_ref):
    member = lax.axis_index("member")
    rows = chosen_ref.shape[1]
    for place in range(chosen_ref.shape[0]):
        parent = parents_ref[place * pair + member]
        here = lax.rem(parent, pair) == member
        at = lax.div(parent, pair)
        chosen_ref[place] = jnp.where(
            here, mine_ref[at, pl.ds(0, rows)], other_ref[at, pl.ds(0, rows)]
        )
    total = jnp.zeros_like(root_ref)
    for place in range(chosen_ref.shape[0]):
        total += mine_ref[place, rows:rows + 8] + other_ref[place, rows:rows + 8]
    root_ref[...] = jnp.sqrt(weight_ref[0] / total)


def choose(parents, weights, mine, other):
    pairs, rows, nz = mine.shape
    return pl.pallas_call(
        choose_kernel,
        out_shape=(
            pltpu.VMEM((pairs, rows - 8, nz), jnp.float32),
            pltpu.VMEM((8, nz), jnp.float32),
        ),
        in_specs=[SMEM, SMEM, VMEM, VMEM],
        out_specs=(VMEM, VMEM),
        name="choose",
    )(parents, weights, in_vmem(mine), in_vmem(other))


def six_sum(before, here, after, edge):
    row = lax.broadcasted_iota(jnp.int32, here.shape, 0)
    lane = lax.broadcasted_iota(jnp.int32, here.shape, 1)
    ny, nz = here.shape
    down = jnp.where(row == 0, edge, pltpu.roll(here, 1, 0))
    up = jnp.where(row == ny - 1, edge, pltpu.roll(here, ny - 1, 0))
    left = jnp.where(lane == 0, edge, pltpu.roll(here, 1, 1))
    right = jnp.where(lane == nz - 1, edge, pltpu.roll(here, nz - 1, 1))
    return ((before + after) + (down + up)) + (left + right)


def moves_kernel(
    depth, accept_ref, root_ref, moved_ref, noise_ref, source_ref,
    low_ref, high_ref,
    cond_out, pot_out, traces_out, cond, pot, once, conductivity, gain,
):
    moves, width, _, nz = noise_ref.shape
    reach = 2 * moves
    span = width + 2 * reach
    tile = lax.axis_index("tile")
    first = tile == 0
    last = tile == lax.axis_size("tile") - 1

    def fetch(field, at, h, i):
        if i < 0:
            return low_ref[at + h + i]
        if i >= width:
            return high_ref[at + i - width]
        return field[i]

    def keep_inside(value, i):
        outside = (first & (i < reach)) | (last & (i >= reach + width))
        return jnp.where(outside, 0.0, value)

    for i in range(span):
        cond[i] = fetch(moved_ref.at[0], 0, reach, i - reach)
        pot[i] = fetch(moved_ref.at[1], reach, reach, i - reach)

    source_at = 2 * reach + sum(depth[:moves])
    for m in range(moves):
        start = 2 * m
        noise_at = 2 * reach + sum(depth[:m])
        accepted = accept_ref[m] > 0

        def sweep(old, lo, hi):
            for i in range(lo, hi):
                here, here_k = old[i], conductivity[i]
                before, after = old[i - 1], old[i + 1]
                plain = six_sum(before, here, after, 0.0)
                scaled = six_sum(
                    before * conductivity[i - 1], here * here_k, after * conductivity[i + 1], 0.0
                )
                source = fetch(
                    source_ref, source_at, depth[moves], i - reach
                )
                value = (1.0 - relax_weight) * here + (
                    2.0 * source + (here_k * plain + scaled)
                ) * gain[i]
                yield i, keep_inside(value, i)

        for i in range(start, span - start):
            proposal = prior_keep * cond[i] + prior_fresh * fetch(
                noise_ref.at[m], noise_at, depth[m], i - reach
            )
            conductivity[i] = jnp.exp(proposal)
            cond[i] = jnp.where(accepted, proposal, cond[i])
        for i in range(start + 1, span - start - 1):
            here_k = conductivity[i]
            gain[i] = relax_weight / (
                6.0 * here_k + six_sum(conductivity[i - 1], here_k, conductivity[i + 1], 1.0)
            )
        for i, value in sweep(pot, start + 1, span - start - 1):
            once[i] = value
        for i, value in sweep(once, start + 2, span - start - 2):
            pot[i] = jnp.where(accepted, value, pot[i])

    root = root_ref[0:1]
    for i in range(width):
        cond_out[i] = cond[i + reach]
        value = pot[i + reach]
        pot_out[i] = value
        traces_out[:, i * nz:(i + 1) * nz] = value * root


def run_moves(depth, accept, root, *fields):
    moves, width, ny, nz = fields[1].shape
    span = width + 4 * moves
    return pl.pallas_call(
        functools.partial(moves_kernel, depth),
        out_shape=(
            pltpu.VMEM((width, ny, nz), jnp.float32),
            pltpu.VMEM((width, ny, nz), jnp.float32),
            pltpu.VMEM((ny, width * nz), jnp.float32),
        ),
        in_specs=[SMEM] + [VMEM] * (1 + len(fields)),
        out_specs=(VMEM, VMEM, VMEM),
        scratch_shapes=[pltpu.VMEM((span, ny, nz), jnp.float32)] * 5,
        name="moves",
    )(accept, in_vmem(root), *[in_vmem(field) for field in fields])


def sum_copies_kernel(parts_ref, copies_ref):
    total = parts_ref[0]
    for place in range(1, parts_ref.shape[0]):
        total += parts_ref[place]
    for place in range(copies_ref.shape[0]):
        copies_ref[place] = total


def sum_copies(parts):
    return pl.pallas_call(
        sum_copies_kernel,
        out_shape=pltpu.VMEM(parts.shape, jnp.float32),
        in_specs=[VMEM],
        out_specs=VMEM,
        name="sum_copies",
    )(in_vmem(parts))


def put_kernel(own, half_ref, *refs):
    out_ref, sem = refs[-2:]
    member = lax.axis_index("member")
    owner = member if own else 1 - member
    rows = half_ref.shape[0]
    copy = pltpu.make_async_copy(
        half_ref, out_ref.at[pl.ds(pl.multiple_of(owner * rows, rows), rows)], sem
    )
    copy.start()
    copy.wait()


def put(half, own, whole=()):
    return pl.pallas_call(
        functools.partial(put_kernel, own),
        out_shape=jax.ShapeDtypeStruct((pair * half.shape[0], half.shape[1]), jnp.float32),
        in_specs=[VMEM] + [ANY] * len(whole),
        out_specs=ANY,
        scratch_shapes=[pltpu.SemaphoreType.DMA],
        input_output_aliases={1: 0} if whole else {},
        name="put",
    )(in_vmem(half), *whole)


def exchange_halo(low_edge, high_edge):
    count = lax.axis_size("tile")
    forward = [(i, i + 1) for i in range(count - 1)]
    backward = [(target, source) for source, target in forward]
    low = lax.ppermute(high_edge, "tile", forward)
    high = lax.ppermute(low_edge, "tile", backward)
    return low, high


def swap(block):
    return lax.ppermute(block, "member", [(0, 1), (1, 0)])


def local(log_cond, potential, noise, source, parents, accept, weights):
    moves = noise.shape[0]
    width, ny, nz = source.shape
    reach = 2 * moves

    depth = tuple(reach - 2 * m for m in range(moves)) + (reach - 1,)
    pieces, noise, source, low_edge, high_edge = pack(
        weights, log_cond, potential, noise[:, 0], source, lax.axis_size("pairs"), depth
    )
    pieces = lax.all_to_all(pieces, "pairs", 0, 0, tiled=True)
    chosen, root = choose(parents, weights, pieces, swap(pieces))
    moved = lax.all_to_all(chosen, "pairs", 0, 0, tiled=True).reshape(2, width, ny, nz)
    low, high = exchange_halo(
        jnp.concatenate([moved[:, :reach].reshape(-1, ny, nz), low_edge]),
        jnp.concatenate([moved[:, width - reach:].reshape(-1, ny, nz), high_edge]),
    )
    conduct, pot, traces = run_moves(
        depth, accept[:, 0], root, moved, noise, source, low, high
    )

    rows = traces.shape[1] // (lax.axis_size("tile") * pair)
    member = lax.axis_index("member")
    piece = lax.all_gather(traces, "tile", axis=0, tiled=True)

    def product(owner):
        columns = lax.dynamic_slice_in_dim(
            piece, (lax.axis_index("tile") * pair + owner) * rows, rows, 1
        )
        return lax.dot_general(
            columns,
            piece,
            (((0,), (0,)), ((), ())),
            precision=lax.Precision.HIGHEST,
            preferred_element_type=jnp.float32,
        ).reshape(lax.axis_size("pairs"), -1, piece.shape[1])

    got = swap(product(1 - member))
    parts = lax.all_to_all(product(member) + got, "pairs", 0, 0, tiled=True)
    mine = lax.all_to_all(sum_copies(parts), "pairs", 0, 0, tiled=True)
    other = swap(mine).reshape(rows, -1)
    moments = put(other, False, (put(mine.reshape(rows, -1), True),))
    return (conduct[None], pot[None], moments)


def solution(mesh):
    tiles = mesh.shape["tile"]
    split = jax.sharding.Mesh(
        mesh.devices.reshape(-1, pair, tiles), ("pairs", "member", "tile")
    )
    placed = (
        P(group, "tile", None, None),
        P(group, "tile", None, None),
        P(None, group, "tile", None, None),
        P("tile", None, None),
        P(),
        P(None, group),
        P(group),
    )
    return jax.shard_map(
        local,
        mesh=split,
        in_specs=placed,
        out_specs=(P(group, "tile", None, None), P(group, "tile", None, None), P("tile", None)),
        check_vma=False,
    )
```

```python
import functools

import jax
import jax.numpy as jnp
from jax import lax
from jax.experimental import pallas as pl
from jax.experimental.pallas import tpu as pltpu
from jax.sharding import PartitionSpec as P

prior_keep = 0.8
prior_fresh = 0.6
relax_weight = 0.8
pair = 2
group = ("pairs", "member")

SMEM = pl.BlockSpec(memory_space=pltpu.SMEM)
VMEM = pl.BlockSpec(memory_space=pltpu.VMEM)
ANY = pl.BlockSpec(memory_space=pl.ANY)


def in_vmem(array):
    return pltpu.with_memory_space_constraint(array, pltpu.VMEM)


def pack_kernel(
    rows, depth, weight_ref, cond_ref, pot_ref, noise_ref, source_ref,
    pieces_ref, noise_out, source_out, low_ref, high_ref, sems,
):
    moves = noise_ref.shape[0]
    pairs = []
    for piece in range(pieces_ref.shape[0]):
        row = piece * rows
        field = cond_ref if row < cond_ref.shape[0] else pot_ref
        row %= cond_ref.shape[0]
        pairs.append((field.at[pl.ds(row, rows)], pieces_ref.at[piece, pl.ds(0, rows)]))
    pairs += [(noise_ref, noise_out), (source_ref, source_out)]
    at = 0
    for field, h in zip([noise_ref.at[m] for m in range(moves)] + [source_ref], depth):
        pairs.append((field.at[pl.ds(0, h)], low_ref.at[pl.ds(at, h)]))
        pairs.append((field.at[pl.ds(field.shape[0] - h, h)], high_ref.at[pl.ds(at, h)]))
        at += h
    copies = [
        pltpu.make_async_copy(here, there, sems.at[i]) for i, (here, there) in enumerate(pairs)
    ]
    for copy in copies:
        copy.start()
    weight = jnp.full((8, pieces_ref.shape[2]), weight_ref[0], jnp.float32)
    for piece in range(pieces_ref.shape[0]):
        pieces_ref[piece, rows:rows + 8] = weight
    for copy in copies:
        copy.wait()


def pack(weights, log_cond, potential, noise, source, pairs, depth):
    _, ny, nz = source.shape
    rows = 2 * log_cond.size // (pairs * nz)
    edge = pltpu.VMEM((sum(depth), ny, nz), jnp.float32)
    return pl.pallas_call(
        functools.partial(pack_kernel, rows, depth),
        out_shape=(
            pltpu.VMEM((pairs, rows + 8, nz), jnp.float32),
            pltpu.VMEM(noise.shape, jnp.float32),
            pltpu.VMEM(source.shape, jnp.float32),
            edge,
            edge,
        ),
        in_specs=[SMEM, ANY, ANY, ANY, ANY],
        out_specs=(VMEM,) * 5,
        scratch_shapes=[pltpu.SemaphoreType.DMA((pairs + 2 + 2 * len(depth),))],
        name="pack",
    )(weights, log_cond.reshape(-1, nz), potential.reshape(-1, nz), noise, source)


def choose_kernel(parents_ref, weight_ref, mine_ref, other_ref, chosen_ref, root_ref):
    member = lax.axis_index("member")
    rows = chosen_ref.shape[1]
    for place in range(chosen_ref.shape[0]):
        parent = parents_ref[place * pair + member]
        here = lax.rem(parent, pair) == member
        at = lax.div(parent, pair)
        chosen_ref[place] = jnp.where(
            here, mine_ref[at, pl.ds(0, rows)], other_ref[at, pl.ds(0, rows)]
        )
    total = jnp.zeros_like(root_ref)
    for place in range(chosen_ref.shape[0]):
        total += mine_ref[place, rows:rows + 8] + other_ref[place, rows:rows + 8]
    root_ref[...] = jnp.sqrt(weight_ref[0] / total)


def choose(parents, weights, mine, other):
    pairs, rows, nz = mine.shape
    return pl.pallas_call(
        choose_kernel,
        out_shape=(
            pltpu.VMEM((pairs, rows - 8, nz), jnp.float32),
            pltpu.VMEM((8, nz), jnp.float32),
        ),
        in_specs=[SMEM, SMEM, VMEM, VMEM],
        out_specs=(VMEM, VMEM),
        name="choose",
    )(parents, weights, in_vmem(mine), in_vmem(other))


def six_sum(before, here, after, edge):
    row = lax.broadcasted_iota(jnp.int32, here.shape, 0)
    lane = lax.broadcasted_iota(jnp.int32, here.shape, 1)
    ny, nz = here.shape
    down = jnp.where(row == 0, edge, pltpu.roll(here, 1, 0))
    up = jnp.where(row == ny - 1, edge, pltpu.roll(here, ny - 1, 0))
    left = jnp.where(lane == 0, edge, pltpu.roll(here, 1, 1))
    right = jnp.where(lane == nz - 1, edge, pltpu.roll(here, nz - 1, 1))
    return ((before + after) + (down + up)) + (left + right)


def moves_kernel(
    depth, accept_ref, root_ref, moved_ref, noise_ref, source_ref,
    low_ref, high_ref,
    cond_out, pot_out, traces_out, cond, pot, once, conductivity, gain,
):
    moves, width, _, nz = noise_ref.shape
    reach = 2 * moves
    span = width + 2 * reach
    tile = lax.axis_index("tile")
    first = tile == 0
    last = tile == lax.axis_size("tile") - 1

    def fetch(field, at, h, i):
        if i < 0:
            return low_ref[at + h + i]
        if i >= width:
            return high_ref[at + i - width]
        return field[i]

    def keep_inside(value, i):
        outside = (first & (i < reach)) | (last & (i >= reach + width))
        return jnp.where(outside, 0.0, value)

    for i in range(span):
        cond[i] = fetch(moved_ref.at[0], 0, reach, i - reach)
        pot[i] = fetch(moved_ref.at[1], reach, reach, i - reach)

    source_at = 2 * reach + sum(depth[:moves])
    for m in range(moves):
        start = 2 * m
        noise_at = 2 * reach + sum(depth[:m])
        accepted = accept_ref[m] > 0

        def sweep(old, lo, hi):
            for i in range(lo, hi):
                here, here_k = old[i], conductivity[i]
                before, after = old[i - 1], old[i + 1]
                plain = six_sum(before, here, after, 0.0)
                scaled = six_sum(
                    before * conductivity[i - 1], here * here_k, after * conductivity[i + 1], 0.0
                )
                source = fetch(
                    source_ref, source_at, depth[moves], i - reach
                )
                value = (1.0 - relax_weight) * here + (
                    2.0 * source + (here_k * plain + scaled)
                ) * gain[i]
                yield i, keep_inside(value, i)

        for i in range(start, span - start):
            proposal = prior_keep * cond[i] + prior_fresh * fetch(
                noise_ref.at[m], noise_at, depth[m], i - reach
            )
            conductivity[i] = jnp.exp(proposal)
            cond[i] = jnp.where(accepted, proposal, cond[i])
        for i in range(start + 1, span - start - 1):
            here_k = conductivity[i]
            gain[i] = relax_weight / (
                6.0 * here_k + six_sum(conductivity[i - 1], here_k, conductivity[i + 1], 1.0)
            )
        for i, value in sweep(pot, start + 1, span - start - 1):
            once[i] = value
        for i, value in sweep(once, start + 2, span - start - 2):
            pot[i] = jnp.where(accepted, value, pot[i])

    root = root_ref[0:1]
    for i in range(width):
        cond_out[i] = cond[i + reach]
        value = pot[i + reach]
        pot_out[i] = value
        scaled = value * root
        for place in range(traces_out.shape[0]):
            traces_out[place, :, i * nz:(i + 1) * nz] = scaled


def run_moves(depth, accept, root, *fields):
    moves, width, ny, nz = fields[1].shape
    span = width + 4 * moves
    return pl.pallas_call(
        functools.partial(moves_kernel, depth),
        out_shape=(
            pltpu.VMEM((width, ny, nz), jnp.float32),
            pltpu.VMEM((width, ny, nz), jnp.float32),
            pltpu.VMEM((lax.axis_size("tile"), ny, width * nz), jnp.float32),
        ),
        in_specs=[SMEM] + [VMEM] * (1 + len(fields)),
        out_specs=(VMEM, VMEM, VMEM),
        scratch_shapes=[pltpu.VMEM((span, ny, nz), jnp.float32)] * 5,
        name="moves",
    )(accept, in_vmem(root), *[in_vmem(field) for field in fields])


def sum_copies_kernel(parts_ref, copies_ref):
    total = parts_ref[0]
    for place in range(1, parts_ref.shape[0]):
        total += parts_ref[place]
    for place in range(copies_ref.shape[0]):
        copies_ref[place] = total


def sum_copies(parts):
    return pl.pallas_call(
        sum_copies_kernel,
        out_shape=pltpu.VMEM(parts.shape, jnp.float32),
        in_specs=[VMEM],
        out_specs=VMEM,
        name="sum_copies",
    )(in_vmem(parts))


def put_kernel(own, half_ref, *refs):
    out_ref, sem = refs[-2:]
    member = lax.axis_index("member")
    owner = member if own else 1 - member
    rows = half_ref.shape[0]
    copy = pltpu.make_async_copy(
        half_ref, out_ref.at[pl.ds(pl.multiple_of(owner * rows, rows), rows)], sem
    )
    copy.start()
    copy.wait()


def put(half, own, whole=()):
    return pl.pallas_call(
        functools.partial(put_kernel, own),
        out_shape=jax.ShapeDtypeStruct((pair * half.shape[0], half.shape[1]), jnp.float32),
        in_specs=[VMEM] + [ANY] * len(whole),
        out_specs=ANY,
        scratch_shapes=[pltpu.SemaphoreType.DMA],
        input_output_aliases={1: 0} if whole else {},
        name="put",
    )(in_vmem(half), *whole)


def exchange_halo(low_edge, high_edge):
    count = lax.axis_size("tile")
    forward = [(i, i + 1) for i in range(count - 1)]
    backward = [(target, source) for source, target in forward]
    low = lax.ppermute(high_edge, "tile", forward)
    high = lax.ppermute(low_edge, "tile", backward)
    return low, high


def swap(block):
    return lax.ppermute(block, "member", [(0, 1), (1, 0)])


def local(log_cond, potential, noise, source, parents, accept, weights):
    moves = noise.shape[0]
    width, ny, nz = source.shape
    reach = 2 * moves

    depth = tuple(reach - 2 * m for m in range(moves)) + (reach - 1,)
    pieces, noise, source, low_edge, high_edge = pack(
        weights, log_cond, potential, noise[:, 0], source, lax.axis_size("pairs"), depth
    )
    pieces = lax.all_to_all(pieces, "pairs", 0, 0, tiled=True)
    chosen, root = choose(parents, weights, pieces, swap(pieces))
    moved = lax.all_to_all(chosen, "pairs", 0, 0, tiled=True).reshape(2, width, ny, nz)
    low, high = exchange_halo(
        jnp.concatenate([moved[:, :reach].reshape(-1, ny, nz), low_edge]),
        jnp.concatenate([moved[:, width - reach:].reshape(-1, ny, nz), high_edge]),
    )
    conduct, pot, traces = run_moves(
        depth, accept[:, 0], root, moved, noise, source, low, high
    )

    rows = traces.shape[2] // (lax.axis_size("tile") * pair)
    member = lax.axis_index("member")
    piece = lax.all_to_all(traces, "tile", 0, 0, tiled=True).reshape(-1, traces.shape[2])

    def product(owner):
        columns = lax.dynamic_slice_in_dim(
            piece, (lax.axis_index("tile") * pair + owner) * rows, rows, 1
        )
        return lax.dot_general(
            columns,
            piece,
            (((0,), (0,)), ((), ())),
            precision=lax.Precision.HIGHEST,
            preferred_element_type=jnp.float32,
        ).reshape(lax.axis_size("pairs"), -1, piece.shape[1])

    got = swap(product(1 - member))
    parts = lax.all_to_all(product(member) + got, "pairs", 0, 0, tiled=True)
    mine = lax.all_to_all(sum_copies(parts), "pairs", 0, 0, tiled=True)
    other = swap(mine).reshape(rows, -1)
    moments = put(other, False, (put(mine.reshape(rows, -1), True),))
    return (conduct[None], pot[None], moments)


def solution(mesh):
    tiles = mesh.shape["tile"]
    split = jax.sharding.Mesh(
        mesh.devices.reshape(-1, pair, tiles), ("pairs", "member", "tile")
    )
    placed = (
        P(group, "tile", None, None),
        P(group, "tile", None, None),
        P(None, group, "tile", None, None),
        P("tile", None, None),
        P(),
        P(None, group),
        P(group),
    )
    return jax.shard_map(
        local,
        mesh=split,
        in_specs=placed,
        out_specs=(P(group, "tile", None, None), P(group, "tile", None, None), P("tile", None)),
        check_vma=False,
    )
```

```python
import functools

import jax
import jax.numpy as jnp
from jax import lax
from jax.experimental import pallas as pl
from jax.experimental.pallas import tpu as pltpu
from jax.sharding import PartitionSpec as P

prior_keep = 0.8
prior_fresh = 0.6
relax_weight = 0.8
pair = 2
group = ("pairs", "member")

SMEM = pl.BlockSpec(memory_space=pltpu.SMEM)
VMEM = pl.BlockSpec(memory_space=pltpu.VMEM)
ANY = pl.BlockSpec(memory_space=pl.ANY)


def in_vmem(array):
    return pltpu.with_memory_space_constraint(array, pltpu.VMEM)


def pack_kernel(
    depth, weight_ref, cond_ref, pot_ref, noise_ref, source_ref,
    copies_ref, noise_out, source_out, low_ref, high_ref, sems,
):
    moves = noise_ref.shape[0]
    rows = cond_ref.shape[0]
    pairs = []
    for place in range(copies_ref.shape[0]):
        pairs.append((cond_ref, copies_ref.at[place, pl.ds(0, rows)]))
        pairs.append((pot_ref, copies_ref.at[place, pl.ds(rows, rows)]))
    pairs += [(noise_ref, noise_out), (source_ref, source_out)]
    at = 0
    for field, h in zip([noise_ref.at[m] for m in range(moves)] + [source_ref], depth):
        pairs.append((field.at[pl.ds(0, h)], low_ref.at[pl.ds(at, h)]))
        pairs.append((field.at[pl.ds(field.shape[0] - h, h)], high_ref.at[pl.ds(at, h)]))
        at += h
    copies = [
        pltpu.make_async_copy(here, there, sems.at[i]) for i, (here, there) in enumerate(pairs)
    ]
    for copy in copies:
        copy.start()
    weight = jnp.full((8, copies_ref.shape[2]), weight_ref[0], jnp.float32)
    for place in range(copies_ref.shape[0]):
        copies_ref[place, 2 * rows:2 * rows + 8] = weight
    for copy in copies:
        copy.wait()


def pack(weights, log_cond, potential, noise, source, depth):
    _, ny, nz = source.shape
    pairs = lax.axis_size("pairs")
    rows = 2 * source.size // nz
    edge = pltpu.VMEM((sum(depth), ny, nz), jnp.float32)
    return pl.pallas_call(
        functools.partial(pack_kernel, depth),
        out_shape=(
            pltpu.VMEM((pairs, rows + 8, nz), jnp.float32),
            pltpu.VMEM(noise.shape, jnp.float32),
            pltpu.VMEM(source.shape, jnp.float32),
            edge,
            edge,
        ),
        in_specs=[SMEM, ANY, ANY, ANY, ANY],
        out_specs=(VMEM,) * 5,
        scratch_shapes=[pltpu.SemaphoreType.DMA((2 * pairs + 2 + 2 * len(depth),))],
        name="pack",
    )(weights, log_cond.reshape(-1, nz), potential.reshape(-1, nz), noise, source)


def pick_kernel(parents_ref, held_ref, keep_ref, give_ref):
    pairs, rows, _ = held_ref.shape
    rows -= 8
    member = lax.axis_index("member")
    first = lax.axis_index("pairs") * pair
    total = held_ref[0, rows:rows + 8]
    for place in range(1, pairs):
        total += held_ref[place, rows:rows + 8]
    for out_ref, device in [(keep_ref, first + member), (give_ref, first + 1 - member)]:
        out_ref[0:rows] = held_ref[lax.div(parents_ref[device], pair), 0:rows]
        out_ref[rows:rows + 8] = total


def pick(parents, held):
    out = pltpu.VMEM(held.shape[1:], jnp.float32)
    return pl.pallas_call(
        pick_kernel,
        out_shape=(out, out),
        in_specs=[SMEM, VMEM],
        out_specs=(VMEM, VMEM),
        name="pick",
    )(parents, in_vmem(held))


def settle_kernel(
    reach, parents_ref, weight_ref, keep_ref, got_ref, low_edge_ref, high_edge_ref,
    moved_ref, low_ref, high_ref, root_ref,
):
    _, width, ny, nz = moved_ref.shape
    member = lax.axis_index("member")
    parent = parents_ref[lax.axis_index("pairs") * pair + member]
    here = lax.rem(parent, pair) == member
    for field in range(2):
        for i in range(width):
            row = (field * width + i) * ny
            layer = jnp.where(here, keep_ref[row:row + ny], got_ref[row:row + ny])
            moved_ref[field, i] = layer
            if i < reach:
                low_ref[field * reach + i] = layer
            if i >= width - reach:
                high_ref[field * reach + i - width + reach] = layer
    low_ref[2 * reach:] = low_edge_ref[...]
    high_ref[2 * reach:] = high_edge_ref[...]
    rows = 2 * width * ny
    root_ref[...] = jnp.sqrt(
        weight_ref[0] / (keep_ref[rows:rows + 8] + got_ref[rows:rows + 8])
    )


def settle(reach, parents, weights, keep, got, low_edge, high_edge):
    depth, ny, nz = low_edge.shape
    edge = pltpu.VMEM((2 * reach + depth, ny, nz), jnp.float32)
    width = (keep.shape[0] - 8) // (2 * ny)
    return pl.pallas_call(
        functools.partial(settle_kernel, reach),
        out_shape=(
            pltpu.VMEM((2, width, ny, nz), jnp.float32),
            edge,
            edge,
            pltpu.VMEM((8, nz), jnp.float32),
        ),
        in_specs=[SMEM, SMEM] + [VMEM] * 4,
        out_specs=(VMEM,) * 4,
        name="settle",
    )(parents, weights, *[in_vmem(a) for a in (keep, got, low_edge, high_edge)])


def six_sum(before, here, after, edge):
    row = lax.broadcasted_iota(jnp.int32, here.shape, 0)
    lane = lax.broadcasted_iota(jnp.int32, here.shape, 1)
    ny, nz = here.shape
    down = jnp.where(row == 0, edge, pltpu.roll(here, 1, 0))
    up = jnp.where(row == ny - 1, edge, pltpu.roll(here, ny - 1, 0))
    left = jnp.where(lane == 0, edge, pltpu.roll(here, 1, 1))
    right = jnp.where(lane == nz - 1, edge, pltpu.roll(here, nz - 1, 1))
    return ((before + after) + (down + up)) + (left + right)


def moves_kernel(
    depth, accept_ref, root_ref, moved_ref, noise_ref, source_ref,
    low_ref, high_ref,
    cond_out, pot_out, traces_out, cond, pot, once, conductivity, gain,
):
    moves, width, _, nz = noise_ref.shape
    reach = 2 * moves
    span = width + 2 * reach
    tile = lax.axis_index("tile")
    first = tile == 0
    last = tile == lax.axis_size("tile") - 1

    def fetch(field, at, h, i):
        if i < 0:
            return low_ref[at + h + i]
        if i >= width:
            return high_ref[at + i - width]
        return field[i]

    def keep_inside(value, i):
        outside = (first & (i < reach)) | (last & (i >= reach + width))
        return jnp.where(outside, 0.0, value)

    for i in range(span):
        cond[i] = fetch(moved_ref.at[0], 0, reach, i - reach)
        pot[i] = fetch(moved_ref.at[1], reach, reach, i - reach)

    source_at = 2 * reach + sum(depth[:moves])
    for m in range(moves):
        start = 2 * m
        noise_at = 2 * reach + sum(depth[:m])
        accepted = accept_ref[m] > 0

        def sweep(old, lo, hi):
            for i in range(lo, hi):
                here, here_k = old[i], conductivity[i]
                before, after = old[i - 1], old[i + 1]
                plain = six_sum(before, here, after, 0.0)
                scaled = six_sum(
                    before * conductivity[i - 1], here * here_k, after * conductivity[i + 1], 0.0
                )
                source = fetch(
                    source_ref, source_at, depth[moves], i - reach
                )
                value = (1.0 - relax_weight) * here + (
                    2.0 * source + (here_k * plain + scaled)
                ) * gain[i]
                yield i, keep_inside(value, i)

        for i in range(start, span - start):
            proposal = prior_keep * cond[i] + prior_fresh * fetch(
                noise_ref.at[m], noise_at, depth[m], i - reach
            )
            conductivity[i] = jnp.exp(proposal)
            cond[i] = jnp.where(accepted, proposal, cond[i])
        for i in range(start + 1, span - start - 1):
            here_k = conductivity[i]
            gain[i] = relax_weight / (
                6.0 * here_k + six_sum(conductivity[i - 1], here_k, conductivity[i + 1], 1.0)
            )
        for i, value in sweep(pot, start + 1, span - start - 1):
            once[i] = value
        for i, value in sweep(once, start + 2, span - start - 2):
            pot[i] = jnp.where(accepted, value, pot[i])

    root = root_ref[0:1]
    for i in range(width):
        cond_out[i] = cond[i + reach]
        value = pot[i + reach]
        pot_out[i] = value
        traces_out[:, i * nz:(i + 1) * nz] = value * root


def run_moves(depth, accept, root, *fields):
    moves, width, ny, nz = fields[1].shape
    span = width + 4 * moves
    return pl.pallas_call(
        functools.partial(moves_kernel, depth),
        out_shape=(
            pltpu.VMEM((width, ny, nz), jnp.float32),
            pltpu.VMEM((width, ny, nz), jnp.float32),
            pltpu.VMEM((ny, width * nz), jnp.float32),
        ),
        in_specs=[SMEM] + [VMEM] * (1 + len(fields)),
        out_specs=(VMEM, VMEM, VMEM),
        scratch_shapes=[pltpu.VMEM((span, ny, nz), jnp.float32)] * 5,
        name="moves",
    )(accept, in_vmem(root), *[in_vmem(field) for field in fields])


def sum_copies_kernel(parts_ref, copies_ref):
    total = parts_ref[0]
    for place in range(1, parts_ref.shape[0]):
        total += parts_ref[place]
    for place in range(copies_ref.shape[0]):
        copies_ref[place] = total


def sum_copies(parts):
    return pl.pallas_call(
        sum_copies_kernel,
        out_shape=pltpu.VMEM(parts.shape, jnp.float32),
        in_specs=[VMEM],
        out_specs=VMEM,
        name="sum_copies",
    )(in_vmem(parts))


def put_kernel(own, half_ref, *refs):
    out_ref, sem = refs[-2:]
    member = lax.axis_index("member")
    owner = member if own else 1 - member
    rows = half_ref.shape[0]
    copy = pltpu.make_async_copy(
        half_ref, out_ref.at[pl.ds(pl.multiple_of(owner * rows, rows), rows)], sem
    )
    copy.start()
    copy.wait()


def put(half, own, whole=()):
    return pl.pallas_call(
        functools.partial(put_kernel, own),
        out_shape=jax.ShapeDtypeStruct((pair * half.shape[0], half.shape[1]), jnp.float32),
        in_specs=[VMEM] + [ANY] * len(whole),
        out_specs=ANY,
        scratch_shapes=[pltpu.SemaphoreType.DMA],
        input_output_aliases={1: 0} if whole else {},
        name="put",
    )(in_vmem(half), *whole)


def exchange_halo(low_edge, high_edge):
    count = lax.axis_size("tile")
    forward = [(i, i + 1) for i in range(count - 1)]
    backward = [(target, source) for source, target in forward]
    low = lax.ppermute(high_edge, "tile", forward)
    high = lax.ppermute(low_edge, "tile", backward)
    return low, high


def swap(block):
    return lax.ppermute(block, "member", [(0, 1), (1, 0)])


def local(log_cond, potential, noise, source, parents, accept, weights):
    moves = noise.shape[0]
    width, ny, nz = source.shape
    reach = 2 * moves

    depth = tuple(reach - 2 * m for m in range(moves)) + (reach - 1,)
    bundles, noise, source, low_edge, high_edge = pack(
        weights, log_cond, potential, noise[:, 0], source, depth
    )
    held = lax.all_to_all(bundles, "pairs", 0, 0, tiled=True)
    keep, give = pick(parents, held)
    moved, low_edge, high_edge, root = settle(
        reach, parents, weights, keep, swap(give), low_edge, high_edge
    )
    low, high = exchange_halo(low_edge, high_edge)
    conduct, pot, traces = run_moves(
        depth, accept[:, 0], root, moved, noise, source, low, high
    )

    rows = traces.shape[1] // (lax.axis_size("tile") * pair)
    member = lax.axis_index("member")
    piece = lax.all_gather(traces, "tile", axis=0, tiled=True)

    def product(owner):
        columns = lax.dynamic_slice_in_dim(
            piece, (lax.axis_index("tile") * pair + owner) * rows, rows, 1
        )
        return lax.dot_general(
            columns,
            piece,
            (((0,), (0,)), ((), ())),
            precision=lax.Precision.HIGHEST,
            preferred_element_type=jnp.float32,
        ).reshape(lax.axis_size("pairs"), -1, piece.shape[1])

    got = swap(product(1 - member))
    parts = lax.all_to_all(product(member) + got, "pairs", 0, 0, tiled=True)
    mine = lax.all_to_all(sum_copies(parts), "pairs", 0, 0, tiled=True)
    other = swap(mine).reshape(rows, -1)
    moments = put(other, False, (put(mine.reshape(rows, -1), True),))
    return (conduct[None], pot[None], moments)


def solution(mesh):
    tiles = mesh.shape["tile"]
    split = jax.sharding.Mesh(
        mesh.devices.reshape(-1, pair, tiles), ("pairs", "member", "tile")
    )
    placed = (
        P(group, "tile", None, None),
        P(group, "tile", None, None),
        P(None, group, "tile", None, None),
        P("tile", None, None),
        P(),
        P(None, group),
        P(group),
    )
    return jax.shard_map(
        local,
        mesh=split,
        in_specs=placed,
        out_specs=(P(group, "tile", None, None), P(group, "tile", None, None), P("tile", None)),
        check_vma=False,
    )
```

```python
import functools

import jax
import jax.numpy as jnp
from jax import lax
from jax.experimental import pallas as pl
from jax.experimental.pallas import tpu as pltpu
from jax.sharding import PartitionSpec as P

prior_keep = 0.8
prior_fresh = 0.6
relax_weight = 0.8
pair = 2
group = ("pairs", "member")

SMEM = pl.BlockSpec(memory_space=pltpu.SMEM)
VMEM = pl.BlockSpec(memory_space=pltpu.VMEM)
ANY = pl.BlockSpec(memory_space=pl.ANY)


def in_smem(array):
    return pltpu.with_memory_space_constraint(array, pltpu.SMEM)


def in_vmem(array):
    return pltpu.with_memory_space_constraint(array, pltpu.VMEM)


def pack_kernel(
    rows, depth, weight_ref, parents_ref, accept_ref, cond_ref, pot_ref, noise_ref, source_ref,
    weight_out, parents_out, accept_out, pieces_ref, noise_out, source_out, low_ref, high_ref, sems,
):
    moves = noise_ref.shape[0]
    pairs = [(weight_ref, weight_out), (parents_ref, parents_out), (accept_ref, accept_out)]
    for piece in range(pieces_ref.shape[0]):
        row = piece * rows
        field = cond_ref if row < cond_ref.shape[0] else pot_ref
        row %= cond_ref.shape[0]
        pairs.append((field.at[pl.ds(row, rows)], pieces_ref.at[piece, pl.ds(0, rows)]))
    pairs += [(noise_ref, noise_out), (source_ref, source_out)]
    at = 0
    for field, h in zip([noise_ref.at[m] for m in range(moves)] + [source_ref], depth):
        pairs.append((field.at[pl.ds(0, h)], low_ref.at[pl.ds(at, h)]))
        pairs.append((field.at[pl.ds(field.shape[0] - h, h)], high_ref.at[pl.ds(at, h)]))
        at += h
    copies = [
        pltpu.make_async_copy(here, there, sems.at[i]) for i, (here, there) in enumerate(pairs)
    ]
    for copy in copies:
        copy.start()
    for copy in copies:
        copy.wait()
    weight = jnp.full((8, pieces_ref.shape[2]), weight_out[0], jnp.float32)
    for piece in range(pieces_ref.shape[0]):
        pieces_ref[piece, rows:rows + 8] = weight


def pack(weights, parents, accept, log_cond, potential, noise, source, pairs, depth):
    _, ny, nz = source.shape
    rows = 2 * log_cond.size // (pairs * nz)
    edge = pltpu.VMEM((sum(depth), ny, nz), jnp.float32)
    return pl.pallas_call(
        functools.partial(pack_kernel, rows, depth),
        out_shape=(
            pltpu.SMEM(weights.shape, jnp.float32),
            pltpu.SMEM(parents.shape, jnp.int32),
            pltpu.SMEM(accept.shape, jnp.int32),
            pltpu.VMEM((pairs, rows + 8, nz), jnp.float32),
            pltpu.VMEM(noise.shape, jnp.float32),
            pltpu.VMEM(source.shape, jnp.float32),
            edge,
            edge,
        ),
        in_specs=[ANY] * 7,
        out_specs=(SMEM,) * 3 + (VMEM,) * 5,
        scratch_shapes=[pltpu.SemaphoreType.DMA((pairs + 5 + 2 * len(depth),))],
        name="pack",
    )(weights, parents, accept, log_cond.reshape(-1, nz), potential.reshape(-1, nz), noise, source)


def choose_kernel(parents_ref, weight_ref, mine_ref, other_ref, chosen_ref, root_ref):
    member = lax.axis_index("member")
    rows = chosen_ref.shape[1]
    for place in range(chosen_ref.shape[0]):
        parent = parents_ref[place * pair + member]
        here = lax.rem(parent, pair) == member
        at = lax.div(parent, pair)
        chosen_ref[place] = jnp.where(
            here, mine_ref[at, pl.ds(0, rows)], other_ref[at, pl.ds(0, rows)]
        )
    total = jnp.zeros_like(root_ref)
    for place in range(chosen_ref.shape[0]):
        total += mine_ref[place, rows:rows + 8] + other_ref[place, rows:rows + 8]
    root_ref[...] = jnp.sqrt(weight_ref[0] / total)


def choose(parents, weights, mine, other):
    pairs, rows, nz = mine.shape
    return pl.pallas_call(
        choose_kernel,
        out_shape=(
            pltpu.VMEM((pairs, rows - 8, nz), jnp.float32),
            pltpu.VMEM((8, nz), jnp.float32),
        ),
        in_specs=[SMEM, SMEM, VMEM, VMEM],
        out_specs=(VMEM, VMEM),
        name="choose",
    )(in_smem(parents), in_smem(weights), in_vmem(mine), in_vmem(other))


def six_sum(before, here, after, edge):
    row = lax.broadcasted_iota(jnp.int32, here.shape, 0)
    lane = lax.broadcasted_iota(jnp.int32, here.shape, 1)
    ny, nz = here.shape
    down = jnp.where(row == 0, edge, pltpu.roll(here, 1, 0))
    up = jnp.where(row == ny - 1, edge, pltpu.roll(here, ny - 1, 0))
    left = jnp.where(lane == 0, edge, pltpu.roll(here, 1, 1))
    right = jnp.where(lane == nz - 1, edge, pltpu.roll(here, nz - 1, 1))
    return ((before + after) + (down + up)) + (left + right)


def moves_kernel(
    depth, accept_ref, root_ref, moved_ref, noise_ref, source_ref,
    moved_low, moved_high, fixed_low, fixed_high,
    cond_out, pot_out, traces_out, cond, pot, once, conductivity, gain,
):
    moves, width, _, nz = noise_ref.shape
    reach = 2 * moves
    span = width + 2 * reach
    tile = lax.axis_index("tile")
    first = tile == 0
    last = tile == lax.axis_size("tile") - 1

    def fetch(field, low, high, at, h, i):
        if i < 0:
            return low[at + h + i]
        if i >= width:
            return high[at + i - width]
        return field[i]

    def keep_inside(value, i):
        outside = (first & (i < reach)) | (last & (i >= reach + width))
        return jnp.where(outside, 0.0, value)

    for i in range(span):
        cond[i] = fetch(moved_ref.at[0], moved_low, moved_high, 0, reach, i - reach)
        pot[i] = fetch(moved_ref.at[1], moved_low, moved_high, reach, reach, i - reach)

    source_at = sum(depth[:moves])
    for m in range(moves):
        start = 2 * m
        noise_at = sum(depth[:m])
        accepted = accept_ref[m] > 0

        def sweep(old, lo, hi):
            for i in range(lo, hi):
                here, here_k = old[i], conductivity[i]
                before, after = old[i - 1], old[i + 1]
                plain = six_sum(before, here, after, 0.0)
                scaled = six_sum(
                    before * conductivity[i - 1], here * here_k, after * conductivity[i + 1], 0.0
                )
                source = fetch(
                    source_ref, fixed_low, fixed_high, source_at, depth[moves], i - reach
                )
                value = (1.0 - relax_weight) * here + (
                    2.0 * source + (here_k * plain + scaled)
                ) * gain[i]
                yield i, keep_inside(value, i)

        for i in range(start, span - start):
            proposal = prior_keep * cond[i] + prior_fresh * fetch(
                noise_ref.at[m], fixed_low, fixed_high, noise_at, depth[m], i - reach
            )
            conductivity[i] = jnp.exp(proposal)
            cond[i] = jnp.where(accepted, proposal, cond[i])
        for i in range(start + 1, span - start - 1):
            here_k = conductivity[i]
            gain[i] = relax_weight / (
                6.0 * here_k + six_sum(conductivity[i - 1], here_k, conductivity[i + 1], 1.0)
            )
        for i, value in sweep(pot, start + 1, span - start - 1):
            once[i] = value
        for i, value in sweep(once, start + 2, span - start - 2):
            pot[i] = jnp.where(accepted, value, pot[i])

    root = root_ref[0:1]
    for i in range(width):
        cond_out[i] = cond[i + reach]
        value = pot[i + reach]
        pot_out[i] = value
        traces_out[:, i * nz:(i + 1) * nz] = value * root


def run_moves(depth, accept, root, *fields):
    moves, width, ny, nz = fields[1].shape
    span = width + 4 * moves
    return pl.pallas_call(
        functools.partial(moves_kernel, depth),
        out_shape=(
            pltpu.VMEM((width, ny, nz), jnp.float32),
            pltpu.VMEM((width, ny, nz), jnp.float32),
            pltpu.VMEM((ny, width * nz), jnp.float32),
        ),
        in_specs=[SMEM] + [VMEM] * (1 + len(fields)),
        out_specs=(VMEM, VMEM, VMEM),
        scratch_shapes=[pltpu.VMEM((span, ny, nz), jnp.float32)] * 5,
        name="moves",
    )(in_smem(accept), in_vmem(root), *[in_vmem(field) for field in fields])


def sum_copies_kernel(parts_ref, copies_ref):
    total = parts_ref[0]
    for place in range(1, parts_ref.shape[0]):
        total += parts_ref[place]
    for place in range(copies_ref.shape[0]):
        copies_ref[place] = total


def sum_copies(parts):
    return pl.pallas_call(
        sum_copies_kernel,
        out_shape=pltpu.VMEM(parts.shape, jnp.float32),
        in_specs=[VMEM],
        out_specs=VMEM,
        name="sum_copies",
    )(in_vmem(parts))


def own_rows(ref, rows, owner):
    return ref.at[pl.ds(pl.multiple_of(owner * rows, rows), rows)]


def store_kernel(cond_ref, pot_ref, half_ref, cond_out, pot_out, rows_out, sems):
    own = own_rows(rows_out, half_ref.shape[0], lax.axis_index("member"))
    pairs = [(cond_ref, cond_out), (pot_ref, pot_out), (half_ref, own)]
    copies = [
        pltpu.make_async_copy(here, there, sems.at[i]) for i, (here, there) in enumerate(pairs)
    ]
    for copy in copies:
        copy.start()
    for copy in copies:
        copy.wait()


def store(conduct, pot, half):
    return pl.pallas_call(
        store_kernel,
        out_shape=(
            jax.ShapeDtypeStruct(conduct.shape, jnp.float32),
            jax.ShapeDtypeStruct(pot.shape, jnp.float32),
            jax.ShapeDtypeStruct((pair * half.shape[0], half.shape[1]), jnp.float32),
        ),
        in_specs=[VMEM] * 3,
        out_specs=(ANY,) * 3,
        scratch_shapes=[pltpu.SemaphoreType.DMA((3,))],
        name="store",
    )(in_vmem(conduct), in_vmem(pot), in_vmem(half))


def store_other_kernel(half_ref, held_ref, rows_out, sem):
    other = own_rows(rows_out, half_ref.shape[0], 1 - lax.axis_index("member"))
    copy = pltpu.make_async_copy(half_ref, other, sem)
    copy.start()
    copy.wait()


def store_other(half, held):
    return pl.pallas_call(
        store_other_kernel,
        out_shape=jax.ShapeDtypeStruct(held.shape, jnp.float32),
        in_specs=[VMEM, ANY],
        out_specs=ANY,
        scratch_shapes=[pltpu.SemaphoreType.DMA],
        input_output_aliases={1: 0},
        name="store_other",
    )(in_vmem(half), held)


def exchange_halo(low_edge, high_edge):
    count = lax.axis_size("tile")
    forward = [(i, i + 1) for i in range(count - 1)]
    backward = [(target, source) for source, target in forward]
    low = lax.ppermute(high_edge, "tile", forward)
    high = lax.ppermute(low_edge, "tile", backward)
    return low, high


def swap(block):
    return lax.ppermute(block, "member", [(0, 1), (1, 0)])


def local(log_cond, potential, noise, source, parents, accept, weights):
    moves = noise.shape[0]
    width, ny, nz = source.shape
    reach = 2 * moves

    depth = tuple(reach - 2 * m for m in range(moves)) + (reach - 1,)
    weights, parents, accept, pieces, noise, source, low_edge, high_edge = pack(
        weights, parents, accept[:, 0], log_cond, potential, noise[:, 0], source,
        lax.axis_size("pairs"), depth,
    )
    pieces = lax.all_to_all(pieces, "pairs", 0, 0, tiled=True)
    fixed_low, fixed_high = exchange_halo(low_edge, high_edge)
    chosen, root = choose(parents, weights, pieces, swap(pieces))
    moved = lax.all_to_all(chosen, "pairs", 0, 0, tiled=True).reshape(2, width, ny, nz)
    moved_low, moved_high = exchange_halo(
        moved[:, :reach].reshape(-1, ny, nz), moved[:, width - reach:].reshape(-1, ny, nz)
    )
    conduct, pot, traces = run_moves(
        depth, accept, root, moved, noise, source, moved_low, moved_high, fixed_low, fixed_high
    )

    rows = traces.shape[1] // (lax.axis_size("tile") * pair)
    member = lax.axis_index("member")
    piece = lax.all_gather(traces, "tile", axis=0, tiled=True)

    def product(owner):
        columns = lax.dynamic_slice_in_dim(
            piece, (lax.axis_index("tile") * pair + owner) * rows, rows, 1
        )
        return lax.dot_general(
            columns,
            piece,
            (((0,), (0,)), ((), ())),
            precision=lax.Precision.HIGH,
            preferred_element_type=jnp.float32,
        ).reshape(lax.axis_size("pairs"), -1, piece.shape[1])

    got = swap(product(1 - member))
    parts = lax.all_to_all(product(member) + got, "pairs", 0, 0, tiled=True)
    mine = lax.all_to_all(sum_copies(parts), "pairs", 0, 0, tiled=True)
    other = swap(mine).reshape(rows, -1)
    conduct, pot, held = store(conduct, pot, mine.reshape(rows, -1))
    moments = store_other(other, held)
    return (conduct[None], pot[None], moments)


def solution(mesh):
    tiles = mesh.shape["tile"]
    split = jax.sharding.Mesh(
        mesh.devices.reshape(-1, pair, tiles), ("pairs", "member", "tile")
    )
    placed = (
        P(group, "tile", None, None),
        P(group, "tile", None, None),
        P(None, group, "tile", None, None),
        P("tile", None, None),
        P(),
        P(None, group),
        P(group),
    )
    return jax.shard_map(
        local,
        mesh=split,
        in_specs=placed,
        out_specs=(P(group, "tile", None, None), P(group, "tile", None, None), P("tile", None)),
        check_vma=False,
    )
```

```python
import functools

import jax
import jax.numpy as jnp
from jax import lax
from jax.experimental import pallas as pl
from jax.experimental.pallas import tpu as pltpu
from jax.sharding import PartitionSpec as P

prior_keep = 0.8
prior_fresh = 0.6
relax_weight = 0.8
pair = 2
group = ("pairs", "member")

SMEM = pl.BlockSpec(memory_space=pltpu.SMEM)
VMEM = pl.BlockSpec(memory_space=pltpu.VMEM)
ANY = pl.BlockSpec(memory_space=pl.ANY)


def in_smem(array):
    return pltpu.with_memory_space_constraint(array, pltpu.SMEM)


def in_vmem(array):
    return pltpu.with_memory_space_constraint(array, pltpu.VMEM)


def pack_kernel(
    rows, depth, weight_ref, parents_ref, accept_ref, cond_ref, pot_ref, noise_ref, source_ref,
    weight_out, parents_out, accept_out, pieces_ref, noise_out, source_out, low_ref, high_ref, sems,
):
    moves = noise_ref.shape[0]
    pairs = [(weight_ref, weight_out), (parents_ref, parents_out), (accept_ref, accept_out)]
    for piece in range(pieces_ref.shape[0]):
        row = piece * rows
        field = cond_ref if row < cond_ref.shape[0] else pot_ref
        row %= cond_ref.shape[0]
        pairs.append((field.at[pl.ds(row, rows)], pieces_ref.at[piece, pl.ds(0, rows)]))
    pairs += [(noise_ref, noise_out), (source_ref, source_out)]
    at = 0
    for field, h in zip([noise_ref.at[m] for m in range(moves)] + [source_ref], depth):
        pairs.append((field.at[pl.ds(0, h)], low_ref.at[pl.ds(at, h)]))
        pairs.append((field.at[pl.ds(field.shape[0] - h, h)], high_ref.at[pl.ds(at, h)]))
        at += h
    copies = [
        pltpu.make_async_copy(here, there, sems.at[i]) for i, (here, there) in enumerate(pairs)
    ]
    for copy in copies:
        copy.start()
    for copy in copies:
        copy.wait()
    weight = jnp.full((8, pieces_ref.shape[2]), weight_out[0], jnp.float32)
    for piece in range(pieces_ref.shape[0]):
        pieces_ref[piece, rows:rows + 8] = weight


def pack(weights, parents, accept, log_cond, potential, noise, source, pairs, depth):
    _, ny, nz = source.shape
    rows = 2 * log_cond.size // (pairs * nz)
    edge = pltpu.VMEM((sum(depth), ny, nz), jnp.float32)
    return pl.pallas_call(
        functools.partial(pack_kernel, rows, depth),
        out_shape=(
            pltpu.SMEM(weights.shape, jnp.float32),
            pltpu.SMEM(parents.shape, jnp.int32),
            pltpu.SMEM(accept.shape, jnp.int32),
            pltpu.VMEM((pairs, rows + 8, nz), jnp.float32),
            pltpu.VMEM(noise.shape, jnp.float32),
            pltpu.VMEM(source.shape, jnp.float32),
            edge,
            edge,
        ),
        in_specs=[ANY] * 7,
        out_specs=(SMEM,) * 3 + (VMEM,) * 5,
        scratch_shapes=[pltpu.SemaphoreType.DMA((pairs + 5 + 2 * len(depth),))],
        name="pack",
    )(weights, parents, accept, log_cond.reshape(-1, nz), potential.reshape(-1, nz), noise, source)


def choose_kernel(parents_ref, weight_ref, mine_ref, other_ref, chosen_ref, root_ref):
    member = lax.axis_index("member")
    rows = chosen_ref.shape[1]
    for place in range(chosen_ref.shape[0]):
        parent = parents_ref[place * pair + member]
        here = lax.rem(parent, pair) == member
        at = lax.div(parent, pair)
        chosen_ref[place] = jnp.where(
            here, mine_ref[at, pl.ds(0, rows)], other_ref[at, pl.ds(0, rows)]
        )
    total = jnp.zeros_like(root_ref)
    for place in range(chosen_ref.shape[0]):
        total += mine_ref[place, rows:rows + 8] + other_ref[place, rows:rows + 8]
    root_ref[...] = jnp.sqrt(weight_ref[0] / total)


def choose(parents, weights, mine, other):
    pairs, rows, nz = mine.shape
    return pl.pallas_call(
        choose_kernel,
        out_shape=(
            pltpu.VMEM((pairs, rows - 8, nz), jnp.float32),
            pltpu.VMEM((8, nz), jnp.float32),
        ),
        in_specs=[SMEM, SMEM, VMEM, VMEM],
        out_specs=(VMEM, VMEM),
        name="choose",
    )(in_smem(parents), in_smem(weights), in_vmem(mine), in_vmem(other))


def six_sum(before, here, after, edge):
    row = lax.broadcasted_iota(jnp.int32, here.shape, 0)
    lane = lax.broadcasted_iota(jnp.int32, here.shape, 1)
    ny, nz = here.shape
    down = jnp.where(row == 0, edge, pltpu.roll(here, 1, 0))
    up = jnp.where(row == ny - 1, edge, pltpu.roll(here, ny - 1, 0))
    left = jnp.where(lane == 0, edge, pltpu.roll(here, 1, 1))
    right = jnp.where(lane == nz - 1, edge, pltpu.roll(here, nz - 1, 1))
    return ((before + after) + (down + up)) + (left + right)


def moves_kernel(
    depth, accept_ref, root_ref, moved_ref, noise_ref, source_ref,
    moved_first, moved_second, fixed_first, fixed_second,
    cond_out, pot_out, traces_out, cond, pot, once, conductivity, gain,
):
    moves, width, _, nz = noise_ref.shape
    reach = 2 * moves
    span = width + 2 * reach
    tile = lax.axis_index("tile")
    first = tile == 0
    last = tile == lax.axis_size("tile") - 1

    even = lax.axis_index("member") == 0

    def fetch(field, first, second, at, h, i):
        if 0 <= i < width:
            return field[i]
        place = at + h + i if i < 0 else at + i - width
        return jnp.where(even == (i < 0), first[place], second[place])

    def keep_inside(value, i):
        outside = (first & (i < reach)) | (last & (i >= reach + width))
        return jnp.where(outside, 0.0, value)

    for i in range(span):
        cond[i] = fetch(moved_ref.at[0], moved_first, moved_second, 0, reach, i - reach)
        pot[i] = fetch(moved_ref.at[1], moved_first, moved_second, reach, reach, i - reach)

    source_at = sum(depth[:moves])
    for m in range(moves):
        start = 2 * m
        noise_at = sum(depth[:m])
        accepted = accept_ref[m] > 0

        def sweep(old, lo, hi):
            for i in range(lo, hi):
                here, here_k = old[i], conductivity[i]
                before, after = old[i - 1], old[i + 1]
                plain = six_sum(before, here, after, 0.0)
                scaled = six_sum(
                    before * conductivity[i - 1], here * here_k, after * conductivity[i + 1], 0.0
                )
                source = fetch(
                    source_ref, fixed_first, fixed_second, source_at, depth[moves], i - reach
                )
                value = (1.0 - relax_weight) * here + (
                    2.0 * source + (here_k * plain + scaled)
                ) * gain[i]
                yield i, keep_inside(value, i)

        for i in range(start, span - start):
            proposal = prior_keep * cond[i] + prior_fresh * fetch(
                noise_ref.at[m], fixed_first, fixed_second, noise_at, depth[m], i - reach
            )
            conductivity[i] = jnp.exp(proposal)
            cond[i] = jnp.where(accepted, proposal, cond[i])
        for i in range(start + 1, span - start - 1):
            here_k = conductivity[i]
            gain[i] = relax_weight / (
                6.0 * here_k + six_sum(conductivity[i - 1], here_k, conductivity[i + 1], 1.0)
            )
        for i, value in sweep(pot, start + 1, span - start - 1):
            once[i] = value
        for i, value in sweep(once, start + 2, span - start - 2):
            pot[i] = jnp.where(accepted, value, pot[i])

    root = root_ref[0:1]
    for i in range(width):
        cond_out[i] = cond[i + reach]
        value = pot[i + reach]
        pot_out[i] = value
        traces_out[0, :, i * nz:(i + 1) * nz] = value * root


def run_moves(depth, accept, root, *fields):
    moves, width, ny, nz = fields[1].shape
    span = width + 4 * moves
    return pl.pallas_call(
        functools.partial(moves_kernel, depth),
        out_shape=(
            pltpu.VMEM((width, ny, nz), jnp.float32),
            pltpu.VMEM((width, ny, nz), jnp.float32),
            pltpu.VMEM((1, ny, width * nz), jnp.float32),
        ),
        in_specs=[SMEM] + [VMEM] * (1 + len(fields)),
        out_specs=(VMEM, VMEM, VMEM),
        scratch_shapes=[pltpu.VMEM((span, ny, nz), jnp.float32)] * 5,
        name="moves",
    )(in_smem(accept), in_vmem(root), *[in_vmem(field) for field in fields])


def sum_copies_kernel(parts_ref, copies_ref):
    total = parts_ref[0]
    for place in range(1, parts_ref.shape[0]):
        total += parts_ref[place]
    for place in range(copies_ref.shape[0]):
        copies_ref[place] = total


def sum_copies(parts):
    return pl.pallas_call(
        sum_copies_kernel,
        out_shape=pltpu.VMEM(parts.shape, jnp.float32),
        in_specs=[VMEM],
        out_specs=VMEM,
        name="sum_copies",
    )(in_vmem(parts))


def own_rows(ref, rows, owner):
    return ref.at[pl.ds(pl.multiple_of(owner * rows, rows), rows)]


def store_kernel(cond_ref, pot_ref, half_ref, cond_out, pot_out, rows_out, sems):
    own = own_rows(rows_out, half_ref.shape[0], lax.axis_index("member"))
    pairs = [(cond_ref, cond_out), (pot_ref, pot_out), (half_ref, own)]
    copies = [
        pltpu.make_async_copy(here, there, sems.at[i]) for i, (here, there) in enumerate(pairs)
    ]
    for copy in copies:
        copy.start()
    for copy in copies:
        copy.wait()


def store(conduct, pot, half):
    return pl.pallas_call(
        store_kernel,
        out_shape=(
            jax.ShapeDtypeStruct(conduct.shape, jnp.float32),
            jax.ShapeDtypeStruct(pot.shape, jnp.float32),
            jax.ShapeDtypeStruct((pair * half.shape[0], half.shape[1]), jnp.float32),
        ),
        in_specs=[VMEM] * 3,
        out_specs=(ANY,) * 3,
        scratch_shapes=[pltpu.SemaphoreType.DMA((3,))],
        name="store",
    )(in_vmem(conduct), in_vmem(pot), in_vmem(half))


def store_other_kernel(half_ref, held_ref, rows_out, sem):
    other = own_rows(rows_out, half_ref.shape[0], 1 - lax.axis_index("member"))
    copy = pltpu.make_async_copy(half_ref, other, sem)
    copy.start()
    copy.wait()


def store_other(half, held):
    return pl.pallas_call(
        store_other_kernel,
        out_shape=jax.ShapeDtypeStruct(held.shape, jnp.float32),
        in_specs=[VMEM, ANY],
        out_specs=ANY,
        scratch_shapes=[pltpu.SemaphoreType.DMA],
        input_output_aliases={1: 0},
        name="store_other",
    )(in_vmem(half), held)


def exchange_halo(low_edge, high_edge):
    count = lax.axis_size("tile")
    up = [(i, i + 1) for i in range(count - 1)]
    down = [(target, source) for source, target in up]

    def turn(member_0, member_1):
        return member_0 + [(count + source, count + target) for source, target in member_1]

    even = lax.axis_index("member") == 0
    first = lax.ppermute(
        jnp.where(even, high_edge, low_edge), ("member", "tile"), turn(up, down)
    )
    second = lax.ppermute(
        jnp.where(even, low_edge, high_edge), ("member", "tile"), turn(down, up)
    )
    return first, second


def swap(block):
    return lax.ppermute(block, "member", [(0, 1), (1, 0)])


def local(log_cond, potential, noise, source, parents, accept, weights):
    moves = noise.shape[0]
    width, ny, nz = source.shape
    reach = 2 * moves

    depth = tuple(reach - 2 * m for m in range(moves)) + (reach - 1,)
    weights, parents, accept, pieces, noise, source, low_edge, high_edge = pack(
        weights, parents, accept[:, 0], log_cond, potential, noise[:, 0], source,
        lax.axis_size("pairs"), depth,
    )
    pieces = lax.all_to_all(pieces, "pairs", 0, 0, tiled=True)
    fixed_first, fixed_second = exchange_halo(low_edge, high_edge)
    chosen, root = choose(parents, weights, pieces, swap(pieces))
    moved = lax.all_to_all(chosen, "pairs", 0, 0, tiled=True).reshape(2, width, ny, nz)
    moved_first, moved_second = exchange_halo(
        moved[:, :reach].reshape(-1, ny, nz), moved[:, width - reach:].reshape(-1, ny, nz)
    )
    conduct, pot, traces = run_moves(
        depth, accept, root, moved, noise, source, moved_first, moved_second, fixed_first, fixed_second
    )

    rows = traces.shape[2] // (lax.axis_size("tile") * pair)
    member = lax.axis_index("member")
    piece = lax.all_gather(traces, "tile", axis=0, tiled=True).reshape(-1, traces.shape[2])

    def product(owner):
        columns = lax.dynamic_slice_in_dim(
            piece, (lax.axis_index("tile") * pair + owner) * rows, rows, 1
        )
        return lax.dot_general(
            columns,
            piece,
            (((0,), (0,)), ((), ())),
            precision=lax.Precision.HIGH,
            preferred_element_type=jnp.float32,
        ).reshape(lax.axis_size("pairs"), -1, piece.shape[1])

    got = swap(product(1 - member))
    parts = lax.all_to_all(product(member) + got, "pairs", 0, 0, tiled=True)
    mine = lax.all_to_all(sum_copies(parts), "pairs", 0, 0, tiled=True)
    other = swap(mine).reshape(rows, -1)
    conduct, pot, held = store(conduct, pot, mine.reshape(rows, -1))
    moments = store_other(other, held)
    return (conduct[None], pot[None], moments)


def solution(mesh):
    tiles = mesh.shape["tile"]
    split = jax.sharding.Mesh(
        mesh.devices.reshape(-1, pair, tiles), ("pairs", "member", "tile")
    )
    placed = (
        P(group, "tile", None, None),
        P(group, "tile", None, None),
        P(None, group, "tile", None, None),
        P("tile", None, None),
        P(),
        P(None, group),
        P(group),
    )
    return jax.shard_map(
        local,
        mesh=split,
        in_specs=placed,
        out_specs=(P(group, "tile", None, None), P(group, "tile", None, None), P("tile", None)),
        check_vma=False,
    )
```

```python
import functools

import jax
import jax.numpy as jnp
from jax import lax
from jax.experimental import pallas as pl
from jax.experimental.pallas import tpu as pltpu
from jax.sharding import PartitionSpec as P

prior_keep = 0.8
prior_fresh = 0.6
relax_weight = 0.8
pair = 2
group = ("pairs", "member")

SMEM = pl.BlockSpec(memory_space=pltpu.SMEM)
VMEM = pl.BlockSpec(memory_space=pltpu.VMEM)
ANY = pl.BlockSpec(memory_space=pl.ANY)


def in_smem(array):
    return pltpu.with_memory_space_constraint(array, pltpu.SMEM)


def in_vmem(array):
    return pltpu.with_memory_space_constraint(array, pltpu.VMEM)


def pack_kernel(
    rows, depth, weight_ref, parents_ref, accept_ref, cond_ref, pot_ref, noise_ref, source_ref,
    weight_out, parents_out, accept_out, pieces_ref, noise_out, source_out, low_ref, high_ref, sems,
):
    moves = noise_ref.shape[0]
    pairs = [(weight_ref, weight_out), (parents_ref, parents_out), (accept_ref, accept_out)]
    for piece in range(pieces_ref.shape[0]):
        row = piece * rows
        field = cond_ref if row < cond_ref.shape[0] else pot_ref
        row %= cond_ref.shape[0]
        pairs.append((field.at[pl.ds(row, rows)], pieces_ref.at[piece, pl.ds(0, rows)]))
    pairs += [(noise_ref, noise_out), (source_ref, source_out)]
    at = 0
    for field, h in zip([noise_ref.at[m] for m in range(moves)] + [source_ref], depth):
        pairs.append((field.at[pl.ds(0, h)], low_ref.at[pl.ds(at, h)]))
        pairs.append((field.at[pl.ds(field.shape[0] - h, h)], high_ref.at[pl.ds(at, h)]))
        at += h
    copies = [
        pltpu.make_async_copy(here, there, sems.at[i]) for i, (here, there) in enumerate(pairs)
    ]
    for copy in copies:
        copy.start()
    for copy in copies:
        copy.wait()
    weight = jnp.full((8, pieces_ref.shape[2]), weight_out[0], jnp.float32)
    for piece in range(pieces_ref.shape[0]):
        pieces_ref[piece, rows:rows + 8] = weight


def pack(weights, parents, accept, log_cond, potential, noise, source, pairs, depth):
    _, ny, nz = source.shape
    rows = 2 * log_cond.size // (pairs * nz)
    edge = pltpu.VMEM((sum(depth), ny, nz), jnp.float32)
    return pl.pallas_call(
        functools.partial(pack_kernel, rows, depth),
        out_shape=(
            pltpu.SMEM(weights.shape, jnp.float32),
            pltpu.SMEM(parents.shape, jnp.int32),
            pltpu.SMEM(accept.shape, jnp.int32),
            pltpu.VMEM((pairs, rows + 8, nz), jnp.float32),
            pltpu.VMEM(noise.shape, jnp.float32),
            pltpu.VMEM(source.shape, jnp.float32),
            edge,
            edge,
        ),
        in_specs=[ANY] * 7,
        out_specs=(SMEM,) * 3 + (VMEM,) * 5,
        scratch_shapes=[pltpu.SemaphoreType.DMA((pairs + 5 + 2 * len(depth),))],
        name="pack",
    )(weights, parents, accept, log_cond.reshape(-1, nz), potential.reshape(-1, nz), noise, source)


def choose_kernel(parents_ref, weight_ref, mine_ref, other_ref, chosen_ref, root_ref):
    member = lax.axis_index("member")
    rows = chosen_ref.shape[1]
    for place in range(chosen_ref.shape[0]):
        parent = parents_ref[place * pair + member]
        here = lax.rem(parent, pair) == member
        at = lax.div(parent, pair)
        chosen_ref[place] = jnp.where(
            here, mine_ref[at, pl.ds(0, rows)], other_ref[at, pl.ds(0, rows)]
        )
    total = jnp.zeros_like(root_ref)
    for place in range(chosen_ref.shape[0]):
        total += mine_ref[place, rows:rows + 8] + other_ref[place, rows:rows + 8]
    root_ref[...] = jnp.sqrt(weight_ref[0] / total)


def choose(parents, weights, mine, other):
    pairs, rows, nz = mine.shape
    return pl.pallas_call(
        choose_kernel,
        out_shape=(
            pltpu.VMEM((pairs, rows - 8, nz), jnp.float32),
            pltpu.VMEM((8, nz), jnp.float32),
        ),
        in_specs=[SMEM, SMEM, VMEM, VMEM],
        out_specs=(VMEM, VMEM),
        name="choose",
    )(in_smem(parents), in_smem(weights), in_vmem(mine), in_vmem(other))


def six_sum(before, here, after, edge):
    row = lax.broadcasted_iota(jnp.int32, here.shape, 0)
    lane = lax.broadcasted_iota(jnp.int32, here.shape, 1)
    ny, nz = here.shape
    down = jnp.where(row == 0, edge, pltpu.roll(here, 1, 0))
    up = jnp.where(row == ny - 1, edge, pltpu.roll(here, ny - 1, 0))
    left = jnp.where(lane == 0, edge, pltpu.roll(here, 1, 1))
    right = jnp.where(lane == nz - 1, edge, pltpu.roll(here, nz - 1, 1))
    return ((before + after) + (down + up)) + (left + right)


def moves_kernel(
    depth, accept_ref, root_ref, moved_ref, noise_ref, source_ref,
    moved_low, moved_high, fixed_low, fixed_high,
    cond_out, pot_out, traces_out, cond, pot, once, conductivity, gain,
):
    moves, width, _, nz = noise_ref.shape
    reach = 2 * moves
    span = width + 2 * reach
    tile = lax.axis_index("tile")
    first = tile == 0
    last = tile == lax.axis_size("tile") - 1

    def fetch(field, low, high, at, h, i):
        if i < 0:
            return low[at + h + i]
        if i >= width:
            return high[at + i - width]
        return field[i]

    def keep_inside(value, i):
        outside = (first & (i < reach)) | (last & (i >= reach + width))
        return jnp.where(outside, 0.0, value)

    for i in range(span):
        cond[i] = fetch(moved_ref.at[0], moved_low, moved_high, 0, reach, i - reach)
        pot[i] = fetch(moved_ref.at[1], moved_low, moved_high, reach, reach, i - reach)

    source_at = sum(depth[:moves])
    for m in range(moves):
        start = 2 * m
        noise_at = sum(depth[:m])
        accepted = accept_ref[m] > 0

        def sweep(old, lo, hi):
            for i in range(lo, hi):
                here, here_k = old[i], conductivity[i]
                before, after = old[i - 1], old[i + 1]
                plain = six_sum(before, here, after, 0.0)
                scaled = six_sum(
                    before * conductivity[i - 1], here * here_k, after * conductivity[i + 1], 0.0
                )
                source = fetch(
                    source_ref, fixed_low, fixed_high, source_at, depth[moves], i - reach
                )
                value = (1.0 - relax_weight) * here + (
                    2.0 * source + (here_k * plain + scaled)
                ) * gain[i]
                yield i, keep_inside(value, i)

        for i in range(start, span - start):
            proposal = prior_keep * cond[i] + prior_fresh * fetch(
                noise_ref.at[m], fixed_low, fixed_high, noise_at, depth[m], i - reach
            )
            conductivity[i] = jnp.exp(proposal)
            cond[i] = jnp.where(accepted, proposal, cond[i])
        for i in range(start + 1, span - start - 1):
            here_k = conductivity[i]
            gain[i] = relax_weight / (
                6.0 * here_k + six_sum(conductivity[i - 1], here_k, conductivity[i + 1], 1.0)
            )
        for i, value in sweep(pot, start + 1, span - start - 1):
            once[i] = value
        for i, value in sweep(once, start + 2, span - start - 2):
            pot[i] = jnp.where(accepted, value, pot[i])

    root = root_ref[0:1]
    for i in range(width):
        cond_out[i] = cond[i + reach]
        value = pot[i + reach]
        pot_out[i] = value
        traces_out[:, i * nz:(i + 1) * nz] = value * root


def run_moves(depth, accept, root, *fields):
    moves, width, ny, nz = fields[1].shape
    span = width + 4 * moves
    return pl.pallas_call(
        functools.partial(moves_kernel, depth),
        out_shape=(
            pltpu.VMEM((width, ny, nz), jnp.float32),
            pltpu.VMEM((width, ny, nz), jnp.float32),
            pltpu.VMEM((ny, width * nz), jnp.float32),
        ),
        in_specs=[SMEM] + [VMEM] * (1 + len(fields)),
        out_specs=(VMEM, VMEM, VMEM),
        scratch_shapes=[pltpu.VMEM((span, ny, nz), jnp.float32)] * 5,
        name="moves",
    )(in_smem(accept), in_vmem(root), *[in_vmem(field) for field in fields])


def own_rows(ref, rows, owner):
    return ref.at[pl.ds(pl.multiple_of(owner * rows, rows), rows)]


def store_kernel(cond_ref, pot_ref, half_ref, cond_out, pot_out, rows_out, sems):
    own = own_rows(rows_out, half_ref.shape[0], lax.axis_index("member"))
    pairs = [(cond_ref, cond_out), (pot_ref, pot_out), (half_ref, own)]
    copies = [
        pltpu.make_async_copy(here, there, sems.at[i]) for i, (here, there) in enumerate(pairs)
    ]
    for copy in copies:
        copy.start()
    for copy in copies:
        copy.wait()


def store(conduct, pot, half):
    return pl.pallas_call(
        store_kernel,
        out_shape=(
            jax.ShapeDtypeStruct(conduct.shape, jnp.float32),
            jax.ShapeDtypeStruct(pot.shape, jnp.float32),
            jax.ShapeDtypeStruct((pair * half.shape[0], half.shape[1]), jnp.float32),
        ),
        in_specs=[VMEM] * 3,
        out_specs=(ANY,) * 3,
        scratch_shapes=[pltpu.SemaphoreType.DMA((3,))],
        name="store",
    )(in_vmem(conduct), in_vmem(pot), in_vmem(half))


def store_other_kernel(half_ref, held_ref, rows_out, sem):
    other = own_rows(rows_out, half_ref.shape[0], 1 - lax.axis_index("member"))
    copy = pltpu.make_async_copy(half_ref, other, sem)
    copy.start()
    copy.wait()


def store_other(half, held):
    return pl.pallas_call(
        store_other_kernel,
        out_shape=jax.ShapeDtypeStruct(held.shape, jnp.float32),
        in_specs=[VMEM, ANY],
        out_specs=ANY,
        scratch_shapes=[pltpu.SemaphoreType.DMA],
        input_output_aliases={1: 0},
        name="store_other",
    )(in_vmem(half), held)


def exchange_halo(low_edge, high_edge):
    count = lax.axis_size("tile")
    forward = [(i, i + 1) for i in range(count - 1)]
    backward = [(target, source) for source, target in forward]
    low = lax.ppermute(high_edge, "tile", forward)
    high = lax.ppermute(low_edge, "tile", backward)
    return low, high


def swap(block):
    return lax.ppermute(block, "member", [(0, 1), (1, 0)])


def local(log_cond, potential, noise, source, parents, accept, weights):
    moves = noise.shape[0]
    width, ny, nz = source.shape
    reach = 2 * moves

    depth = tuple(reach - 2 * m for m in range(moves)) + (reach - 1,)
    weights, parents, accept, pieces, noise, source, low_edge, high_edge = pack(
        weights, parents, accept[:, 0], log_cond, potential, noise[:, 0], source,
        lax.axis_size("pairs"), depth,
    )
    pieces = lax.all_to_all(pieces, "pairs", 0, 0, tiled=True)
    fixed_low, fixed_high = exchange_halo(low_edge, high_edge)
    chosen, root = choose(parents, weights, pieces, swap(pieces))
    moved = lax.all_to_all(chosen, "pairs", 0, 0, tiled=True).reshape(2, width, ny, nz)
    moved_low, moved_high = exchange_halo(
        moved[:, :reach].reshape(-1, ny, nz), moved[:, width - reach:].reshape(-1, ny, nz)
    )
    conduct, pot, traces = run_moves(
        depth, accept, root, moved, noise, source, moved_low, moved_high, fixed_low, fixed_high
    )

    rows = traces.shape[1] // (lax.axis_size("tile") * pair)
    member = lax.axis_index("member")
    piece = lax.all_gather(traces, "tile", axis=0, tiled=True)

    def product(owner):
        columns = lax.dynamic_slice_in_dim(
            piece, (lax.axis_index("tile") * pair + owner) * rows, rows, 1
        )
        return lax.dot_general(
            columns,
            piece,
            (((0,), (0,)), ((), ())),
            precision=lax.Precision.HIGH,
            preferred_element_type=jnp.float32,
        ).reshape(lax.axis_size("pairs"), -1, piece.shape[1])

    got = swap(product(1 - member))
    mine = lax.psum(product(member) + got, "pairs")
    other = swap(mine).reshape(rows, -1)
    conduct, pot, held = store(conduct, pot, mine.reshape(rows, -1))
    moments = store_other(other, held)
    return (conduct[None], pot[None], moments)


def solution(mesh):
    tiles = mesh.shape["tile"]
    split = jax.sharding.Mesh(
        mesh.devices.reshape(-1, pair, tiles), ("pairs", "member", "tile")
    )
    placed = (
        P(group, "tile", None, None),
        P(group, "tile", None, None),
        P(None, group, "tile", None, None),
        P("tile", None, None),
        P(),
        P(None, group),
        P(group),
    )
    return jax.shard_map(
        local,
        mesh=split,
        in_specs=placed,
        out_specs=(P(group, "tile", None, None), P(group, "tile", None, None), P("tile", None)),
        check_vma=False,
    )
```

```python
import functools

import jax
import jax.numpy as jnp
from jax import lax
from jax.experimental import pallas as pl
from jax.experimental.pallas import tpu as pltpu
from jax.sharding import PartitionSpec as P

prior_keep = 0.8
prior_fresh = 0.6
relax_weight = 0.8
pair = 2
group = ("pairs", "member")

SMEM = pl.BlockSpec(memory_space=pltpu.SMEM)
VMEM = pl.BlockSpec(memory_space=pltpu.VMEM)
ANY = pl.BlockSpec(memory_space=pl.ANY)


def in_smem(array):
    return pltpu.with_memory_space_constraint(array, pltpu.SMEM)


def in_vmem(array):
    return pltpu.with_memory_space_constraint(array, pltpu.VMEM)


def pack_kernel(
    rows, depth, weight_ref, parents_ref, accept_ref, cond_ref, pot_ref, noise_ref, source_ref,
    weight_out, parents_out, accept_out, pieces_ref, noise_out, source_out, low_ref, high_ref, sems,
):
    moves = noise_ref.shape[0]
    pairs = [(weight_ref, weight_out), (parents_ref, parents_out), (accept_ref, accept_out)]
    for piece in range(pieces_ref.shape[0]):
        row = piece * rows
        field = cond_ref if row < cond_ref.shape[0] else pot_ref
        row %= cond_ref.shape[0]
        pairs.append((field.at[pl.ds(row, rows)], pieces_ref.at[piece, pl.ds(0, rows)]))
    pairs += [(noise_ref, noise_out), (source_ref, source_out)]
    at = 0
    for field, h in zip([noise_ref.at[m] for m in range(moves)] + [source_ref], depth):
        pairs.append((field.at[pl.ds(0, h)], low_ref.at[pl.ds(at, h)]))
        pairs.append((field.at[pl.ds(field.shape[0] - h, h)], high_ref.at[pl.ds(at, h)]))
        at += h
    copies = [
        pltpu.make_async_copy(here, there, sems.at[i]) for i, (here, there) in enumerate(pairs)
    ]
    for copy in copies:
        copy.start()
    for copy in copies:
        copy.wait()
    weight = jnp.full((8, pieces_ref.shape[2]), weight_out[0], jnp.float32)
    for piece in range(pieces_ref.shape[0]):
        pieces_ref[piece, rows:rows + 8] = weight


def pack(weights, parents, accept, log_cond, potential, noise, source, pairs, depth):
    _, ny, nz = source.shape
    rows = 2 * log_cond.size // (pairs * nz)
    edge = pltpu.VMEM((sum(depth), ny, nz), jnp.float32)
    return pl.pallas_call(
        functools.partial(pack_kernel, rows, depth),
        out_shape=(
            pltpu.SMEM(weights.shape, jnp.float32),
            pltpu.SMEM(parents.shape, jnp.int32),
            pltpu.SMEM(accept.shape, jnp.int32),
            pltpu.VMEM((pairs, rows + 8, nz), jnp.float32),
            pltpu.VMEM(noise.shape, jnp.float32),
            pltpu.VMEM(source.shape, jnp.float32),
            edge,
            edge,
        ),
        in_specs=[ANY] * 7,
        out_specs=(SMEM,) * 3 + (VMEM,) * 5,
        scratch_shapes=[pltpu.SemaphoreType.DMA((pairs + 5 + 2 * len(depth),))],
        name="pack",
    )(weights, parents, accept, log_cond.reshape(-1, nz), potential.reshape(-1, nz), noise, source)


def choose_kernel(parents_ref, weight_ref, mine_ref, other_ref, chosen_ref, root_ref):
    member = lax.axis_index("member")
    rows = chosen_ref.shape[1]
    for place in range(chosen_ref.shape[0]):
        parent = parents_ref[place * pair + member]
        here = lax.rem(parent, pair) == member
        at = lax.div(parent, pair)
        chosen_ref[place] = jnp.where(
            here, mine_ref[at, pl.ds(0, rows)], other_ref[at, pl.ds(0, rows)]
        )
    total = jnp.zeros_like(root_ref)
    for place in range(chosen_ref.shape[0]):
        total += mine_ref[place, rows:rows + 8] + other_ref[place, rows:rows + 8]
    root_ref[...] = jnp.sqrt(weight_ref[0] / total)


def choose(parents, weights, mine, other):
    pairs, rows, nz = mine.shape
    return pl.pallas_call(
        choose_kernel,
        out_shape=(
            pltpu.VMEM((pairs, rows - 8, nz), jnp.float32),
            pltpu.VMEM((8, nz), jnp.float32),
        ),
        in_specs=[SMEM, SMEM, VMEM, VMEM],
        out_specs=(VMEM, VMEM),
        name="choose",
    )(in_smem(parents), in_smem(weights), in_vmem(mine), in_vmem(other))


def six_sum(before, here, after, edge):
    row = lax.broadcasted_iota(jnp.int32, here.shape, 0)
    lane = lax.broadcasted_iota(jnp.int32, here.shape, 1)
    ny, nz = here.shape
    down = jnp.where(row == 0, edge, pltpu.roll(here, 1, 0))
    up = jnp.where(row == ny - 1, edge, pltpu.roll(here, ny - 1, 0))
    left = jnp.where(lane == 0, edge, pltpu.roll(here, 1, 1))
    right = jnp.where(lane == nz - 1, edge, pltpu.roll(here, nz - 1, 1))
    return ((before + after) + (down + up)) + (left + right)


def moves_kernel(
    depth, accept_ref, root_ref, moved_ref, noise_ref, source_ref,
    moved_low, moved_high, fixed_own, fixed_other,
    cond_out, pot_out, traces_out, cond, pot, once, conductivity, gain,
):
    moves, width, _, nz = noise_ref.shape
    reach = 2 * moves
    span = width + 2 * reach
    tile = lax.axis_index("tile")
    first = tile == 0
    last = tile == lax.axis_size("tile") - 1

    even = lax.axis_index("member") == 0

    def fetch_moved(field, at, i):
        if i < 0:
            return moved_low[at + reach + i]
        if i >= width:
            return moved_high[at + i - width]
        return moved_ref[field, i]

    def fetch(field, at, h, i):
        if 0 <= i < width:
            return field[i]
        place = at + h + i if i < 0 else at + i - width
        return jnp.where(even == (i < 0), fixed_own[place], fixed_other[place])

    def keep_inside(value, i):
        outside = (first & (i < reach)) | (last & (i >= reach + width))
        return jnp.where(outside, 0.0, value)

    for i in range(span):
        cond[i] = fetch_moved(0, 0, i - reach)
        pot[i] = fetch_moved(1, reach, i - reach)

    source_at = sum(depth[:moves])
    for m in range(moves):
        start = 2 * m
        noise_at = sum(depth[:m])
        accepted = accept_ref[m] > 0

        def sweep(old, lo, hi):
            for i in range(lo, hi):
                here, here_k = old[i], conductivity[i]
                before, after = old[i - 1], old[i + 1]
                plain = six_sum(before, here, after, 0.0)
                scaled = six_sum(
                    before * conductivity[i - 1], here * here_k, after * conductivity[i + 1], 0.0
                )
                source = fetch(
                    source_ref, source_at, depth[moves], i - reach
                )
                value = (1.0 - relax_weight) * here + (
                    2.0 * source + (here_k * plain + scaled)
                ) * gain[i]
                yield i, keep_inside(value, i)

        for i in range(start, span - start):
            proposal = prior_keep * cond[i] + prior_fresh * fetch(
                noise_ref.at[m], noise_at, depth[m], i - reach
            )
            conductivity[i] = jnp.exp(proposal)
            cond[i] = jnp.where(accepted, proposal, cond[i])
        for i in range(start + 1, span - start - 1):
            here_k = conductivity[i]
            gain[i] = relax_weight / (
                6.0 * here_k + six_sum(conductivity[i - 1], here_k, conductivity[i + 1], 1.0)
            )
        for i, value in sweep(pot, start + 1, span - start - 1):
            once[i] = value
        for i, value in sweep(once, start + 2, span - start - 2):
            pot[i] = jnp.where(accepted, value, pot[i])

    root = root_ref[0:1]
    for i in range(width):
        cond_out[i] = cond[i + reach]
        value = pot[i + reach]
        pot_out[i] = value
        traces_out[:, i * nz:(i + 1) * nz] = value * root


def run_moves(depth, accept, root, *fields):
    moves, width, ny, nz = fields[1].shape
    span = width + 4 * moves
    return pl.pallas_call(
        functools.partial(moves_kernel, depth),
        out_shape=(
            pltpu.VMEM((width, ny, nz), jnp.float32),
            pltpu.VMEM((width, ny, nz), jnp.float32),
            pltpu.VMEM((ny, width * nz), jnp.float32),
        ),
        in_specs=[SMEM] + [VMEM] * (1 + len(fields)),
        out_specs=(VMEM, VMEM, VMEM),
        scratch_shapes=[pltpu.VMEM((span, ny, nz), jnp.float32)] * 5,
        name="moves",
    )(in_smem(accept), in_vmem(root), *[in_vmem(field) for field in fields])


def sum_copies_kernel(parts_ref, copies_ref):
    total = parts_ref[0]
    for place in range(1, parts_ref.shape[0]):
        total += parts_ref[place]
    for place in range(copies_ref.shape[0]):
        copies_ref[place] = total


def sum_copies(parts):
    return pl.pallas_call(
        sum_copies_kernel,
        out_shape=pltpu.VMEM(parts.shape, jnp.float32),
        in_specs=[VMEM],
        out_specs=VMEM,
        name="sum_copies",
    )(in_vmem(parts))


def own_rows(ref, rows, owner):
    return ref.at[pl.ds(pl.multiple_of(owner * rows, rows), rows)]


def store_kernel(cond_ref, pot_ref, half_ref, cond_out, pot_out, rows_out, sems):
    own = own_rows(rows_out, half_ref.shape[0], lax.axis_index("member"))
    pairs = [(cond_ref, cond_out), (pot_ref, pot_out), (half_ref, own)]
    copies = [
        pltpu.make_async_copy(here, there, sems.at[i]) for i, (here, there) in enumerate(pairs)
    ]
    for copy in copies:
        copy.start()
    for copy in copies:
        copy.wait()


def store(conduct, pot, half):
    return pl.pallas_call(
        store_kernel,
        out_shape=(
            jax.ShapeDtypeStruct(conduct.shape, jnp.float32),
            jax.ShapeDtypeStruct(pot.shape, jnp.float32),
            jax.ShapeDtypeStruct((pair * half.shape[0], half.shape[1]), jnp.float32),
        ),
        in_specs=[VMEM] * 3,
        out_specs=(ANY,) * 3,
        scratch_shapes=[pltpu.SemaphoreType.DMA((3,))],
        name="store",
    )(in_vmem(conduct), in_vmem(pot), in_vmem(half))


def store_other_kernel(half_ref, held_ref, rows_out, sem):
    other = own_rows(rows_out, half_ref.shape[0], 1 - lax.axis_index("member"))
    copy = pltpu.make_async_copy(half_ref, other, sem)
    copy.start()
    copy.wait()


def store_other(half, held):
    return pl.pallas_call(
        store_other_kernel,
        out_shape=jax.ShapeDtypeStruct(held.shape, jnp.float32),
        in_specs=[VMEM, ANY],
        out_specs=ANY,
        scratch_shapes=[pltpu.SemaphoreType.DMA],
        input_output_aliases={1: 0},
        name="store_other",
    )(in_vmem(half), held)


def exchange_halo(low_edge, high_edge):
    count = lax.axis_size("tile")
    forward = [(i, i + 1) for i in range(count - 1)]
    backward = [(target, source) for source, target in forward]
    low = lax.ppermute(high_edge, "tile", forward)
    high = lax.ppermute(low_edge, "tile", backward)
    return low, high


def swap(block):
    return lax.ppermute(block, "member", [(0, 1), (1, 0)])


def exchange_by_member(low_edge, high_edge):
    count = lax.axis_size("tile")
    up = [(i, i + 1) for i in range(count - 1)]
    down = [(count + target, count + source) for source, target in up]
    even = lax.axis_index("member") == 0
    got = swap(jnp.where(even, low_edge, high_edge))
    lane = jnp.concatenate([jnp.where(even, high_edge, low_edge), got])
    came = lax.ppermute(lane, ("member", "tile"), up + down)
    return came[:low_edge.shape[0]], swap(came[low_edge.shape[0]:])


def local(log_cond, potential, noise, source, parents, accept, weights):
    moves = noise.shape[0]
    width, ny, nz = source.shape
    reach = 2 * moves

    depth = tuple(reach - 2 * m for m in range(moves)) + (reach - 1,)
    weights, parents, accept, pieces, noise, source, low_edge, high_edge = pack(
        weights, parents, accept[:, 0], log_cond, potential, noise[:, 0], source,
        lax.axis_size("pairs"), depth,
    )
    pieces = lax.all_to_all(pieces, "pairs", 0, 0, tiled=True)
    fixed_own, fixed_other = exchange_by_member(low_edge, high_edge)
    chosen, root = choose(parents, weights, pieces, swap(pieces))
    moved = lax.all_to_all(chosen, "pairs", 0, 0, tiled=True).reshape(2, width, ny, nz)
    moved_low, moved_high = exchange_halo(
        moved[:, :reach].reshape(-1, ny, nz), moved[:, width - reach:].reshape(-1, ny, nz)
    )
    conduct, pot, traces = run_moves(
        depth, accept, root, moved, noise, source, moved_low, moved_high, fixed_own, fixed_other
    )

    rows = traces.shape[1] // (lax.axis_size("tile") * pair)
    member = lax.axis_index("member")
    piece = lax.all_gather(traces, "tile", axis=0, tiled=True)

    def product(owner):
        columns = lax.dynamic_slice_in_dim(
            piece, (lax.axis_index("tile") * pair + owner) * rows, rows, 1
        )
        return lax.dot_general(
            columns,
            piece,
            (((0,), (0,)), ((), ())),
            precision=lax.Precision.HIGH,
            preferred_element_type=jnp.float32,
        ).reshape(lax.axis_size("pairs"), -1, piece.shape[1])

    got = swap(product(1 - member))
    parts = lax.all_to_all(product(member) + got, "pairs", 0, 0, tiled=True)
    mine = lax.all_to_all(sum_copies(parts), "pairs", 0, 0, tiled=True)
    other = swap(mine).reshape(rows, -1)
    conduct, pot, held = store(conduct, pot, mine.reshape(rows, -1))
    moments = store_other(other, held)
    return (conduct[None], pot[None], moments)


def solution(mesh):
    tiles = mesh.shape["tile"]
    split = jax.sharding.Mesh(
        mesh.devices.reshape(-1, pair, tiles), ("pairs", "member", "tile")
    )
    placed = (
        P(group, "tile", None, None),
        P(group, "tile", None, None),
        P(None, group, "tile", None, None),
        P("tile", None, None),
        P(),
        P(None, group),
        P(group),
    )
    return jax.shard_map(
        local,
        mesh=split,
        in_specs=placed,
        out_specs=(P(group, "tile", None, None), P(group, "tile", None, None), P("tile", None)),
        check_vma=False,
    )
```

```python
import functools

import jax
import jax.numpy as jnp
from jax import lax
from jax.experimental import pallas as pl
from jax.experimental.pallas import tpu as pltpu
from jax.sharding import PartitionSpec as P

prior_keep = 0.8
prior_fresh = 0.6
relax_weight = 0.8
pair = 2
group = ("pairs", "member")

SMEM = pl.BlockSpec(memory_space=pltpu.SMEM)
VMEM = pl.BlockSpec(memory_space=pltpu.VMEM)
ANY = pl.BlockSpec(memory_space=pl.ANY)


def in_smem(array):
    return pltpu.with_memory_space_constraint(array, pltpu.SMEM)


def in_vmem(array):
    return pltpu.with_memory_space_constraint(array, pltpu.VMEM)


def pack_kernel(
    rows, depth, weight_ref, parents_ref, accept_ref, cond_ref, pot_ref, noise_ref, source_ref,
    weight_out, parents_out, accept_out, pieces_ref, noise_out, source_out, low_ref, high_ref,
    weight_rows, sems,
):
    moves = noise_ref.shape[0]
    fetch_weight = pltpu.make_async_copy(weight_ref, weight_out, sems.at[0])
    fetch_weight.start()
    pairs = [(parents_ref, parents_out), (accept_ref, accept_out)]
    for piece in range(pieces_ref.shape[0]):
        row = piece * rows
        field = cond_ref if row < cond_ref.shape[0] else pot_ref
        row %= cond_ref.shape[0]
        pairs.append((field.at[pl.ds(row, rows)], pieces_ref.at[piece, pl.ds(0, rows)]))
    pairs += [(noise_ref, noise_out), (source_ref, source_out)]
    at = 0
    for field, h in zip([noise_ref.at[m] for m in range(moves)] + [source_ref], depth):
        pairs.append((field.at[pl.ds(0, h)], low_ref.at[pl.ds(at, h)]))
        pairs.append((field.at[pl.ds(field.shape[0] - h, h)], high_ref.at[pl.ds(at, h)]))
        at += h
    copies = [
        pltpu.make_async_copy(here, there, sems.at[1 + i]) for i, (here, there) in enumerate(pairs)
    ]
    for copy in copies:
        copy.start()
    fetch_weight.wait()
    weight_rows[...] = jnp.full(weight_rows.shape, weight_out[0], jnp.float32)
    weights = pltpu.make_async_copy(
        weight_rows, pieces_ref.at[:, pl.ds(rows, 8)], sems.at[1 + len(pairs)]
    )
    weights.start()
    for copy in copies + [weights]:
        copy.wait()


def pack(weights, parents, accept, log_cond, potential, noise, source, pairs, depth):
    _, ny, nz = source.shape
    rows = 2 * log_cond.size // (pairs * nz)
    edge = pltpu.VMEM((sum(depth), ny, nz), jnp.float32)
    return pl.pallas_call(
        functools.partial(pack_kernel, rows, depth),
        out_shape=(
            pltpu.SMEM(weights.shape, jnp.float32),
            pltpu.SMEM(parents.shape, jnp.int32),
            pltpu.SMEM(accept.shape, jnp.int32),
            jax.ShapeDtypeStruct((pairs, rows + 8, nz), jnp.float32),
            pltpu.VMEM(noise.shape, jnp.float32),
            pltpu.VMEM(source.shape, jnp.float32),
            edge,
            edge,
        ),
        in_specs=[ANY] * 7,
        out_specs=(SMEM,) * 3 + (ANY,) + (VMEM,) * 4,
        scratch_shapes=[
            pltpu.VMEM((pairs, 8, nz), jnp.float32),
            pltpu.SemaphoreType.DMA((pairs + 6 + 2 * len(depth),)),
        ],
        name="pack",
    )(weights, parents, accept, log_cond.reshape(-1, nz), potential.reshape(-1, nz), noise, source)


def choose_kernel(parents_ref, weight_ref, mine_ref, other_ref, chosen_ref, root_ref):
    member = lax.axis_index("member")
    rows = chosen_ref.shape[1]
    for place in range(chosen_ref.shape[0]):
        parent = parents_ref[place * pair + member]
        here = lax.rem(parent, pair) == member
        at = lax.div(parent, pair)
        chosen_ref[place] = jnp.where(
            here, mine_ref[at, pl.ds(0, rows)], other_ref[at, pl.ds(0, rows)]
        )
    total = jnp.zeros_like(root_ref)
    for place in range(chosen_ref.shape[0]):
        total += mine_ref[place, rows:rows + 8] + other_ref[place, rows:rows + 8]
    root_ref[...] = jnp.sqrt(weight_ref[0] / total)


def choose(parents, weights, mine, other):
    pairs, rows, nz = mine.shape
    return pl.pallas_call(
        choose_kernel,
        out_shape=(
            pltpu.VMEM((pairs, rows - 8, nz), jnp.float32),
            pltpu.VMEM((8, nz), jnp.float32),
        ),
        in_specs=[SMEM, SMEM, VMEM, VMEM],
        out_specs=(VMEM, VMEM),
        name="choose",
    )(in_smem(parents), in_smem(weights), in_vmem(mine), in_vmem(other))


def cut_kernel(moved_ref, came_ref, low_ref, high_ref, pass_ref):
    reach = low_ref.shape[0] // 2
    width = moved_ref.shape[1]
    for field in range(2):
        at = field * reach
        low_ref[at:at + reach] = moved_ref[field, 0:reach]
        high_ref[at:at + reach] = moved_ref[field, width - reach:width]
    pass_ref[...] = came_ref[came_ref.shape[0] - pass_ref.shape[0]:]


def cut(reach, moved, came):
    layer = moved.shape[2:]
    edge = pltpu.VMEM((2 * reach,) + layer, jnp.float32)
    return pl.pallas_call(
        cut_kernel,
        out_shape=(edge, edge, pltpu.VMEM((came.shape[0] // 2,) + layer, jnp.float32)),
        in_specs=[VMEM] * 2,
        out_specs=(VMEM,) * 3,
        name="cut",
    )(in_vmem(moved), in_vmem(came))


def six_sum(before, here, after, edge):
    row = lax.broadcasted_iota(jnp.int32, here.shape, 0)
    lane = lax.broadcasted_iota(jnp.int32, here.shape, 1)
    ny, nz = here.shape
    down = jnp.where(row == 0, edge, pltpu.roll(here, 1, 0))
    up = jnp.where(row == ny - 1, edge, pltpu.roll(here, ny - 1, 0))
    left = jnp.where(lane == 0, edge, pltpu.roll(here, 1, 1))
    right = jnp.where(lane == nz - 1, edge, pltpu.roll(here, nz - 1, 1))
    return ((before + after) + (down + up)) + (left + right)


def moves_kernel(
    depth, accept_ref, root_ref, moved_ref, noise_ref, source_ref,
    moved_low, moved_high, fixed_own, fixed_other,
    cond_out, pot_out, traces_out, cond, pot, once, conductivity, gain,
):
    moves, width, _, nz = noise_ref.shape
    reach = 2 * moves
    span = width + 2 * reach
    tile = lax.axis_index("tile")
    first = tile == 0
    last = tile == lax.axis_size("tile") - 1

    even = lax.axis_index("member") == 0

    def fetch_moved(field, at, i):
        if i < 0:
            return moved_low[at + reach + i]
        if i >= width:
            return moved_high[at + i - width]
        return moved_ref[field, i]

    def fetch(field, at, h, i):
        if 0 <= i < width:
            return field[i]
        place = at + h + i if i < 0 else at + i - width
        return jnp.where(even == (i < 0), fixed_own[place], fixed_other[place])

    def keep_inside(value, i):
        outside = (first & (i < reach)) | (last & (i >= reach + width))
        return jnp.where(outside, 0.0, value)

    for i in range(span):
        cond[i] = fetch_moved(0, 0, i - reach)
        pot[i] = fetch_moved(1, reach, i - reach)

    source_at = sum(depth[:moves])
    for m in range(moves):
        start = 2 * m
        noise_at = sum(depth[:m])
        accepted = accept_ref[m] > 0

        def sweep(old, lo, hi):
            for i in range(lo, hi):
                here, here_k = old[i], conductivity[i]
                before, after = old[i - 1], old[i + 1]
                plain = six_sum(before, here, after, 0.0)
                scaled = six_sum(
                    before * conductivity[i - 1], here * here_k, after * conductivity[i + 1], 0.0
                )
                source = fetch(
                    source_ref, source_at, depth[moves], i - reach
                )
                value = (1.0 - relax_weight) * here + (
                    2.0 * source + (here_k * plain + scaled)
                ) * gain[i]
                yield i, keep_inside(value, i)

        for i in range(start, span - start):
            proposal = prior_keep * cond[i] + prior_fresh * fetch(
                noise_ref.at[m], noise_at, depth[m], i - reach
            )
            conductivity[i] = jnp.exp(proposal)
            cond[i] = jnp.where(accepted, proposal, cond[i])
        for i in range(start + 1, span - start - 1):
            here_k = conductivity[i]
            gain[i] = relax_weight / (
                6.0 * here_k + six_sum(conductivity[i - 1], here_k, conductivity[i + 1], 1.0)
            )
        for i, value in sweep(pot, start + 1, span - start - 1):
            once[i] = value
        for i, value in sweep(once, start + 2, span - start - 2):
            pot[i] = jnp.where(accepted, value, pot[i])

    root = root_ref[0:1]
    for i in range(width):
        cond_out[i] = cond[i + reach]
        value = pot[i + reach]
        pot_out[i] = value
        traces_out[:, i * nz:(i + 1) * nz] = value * root


def run_moves(depth, accept, root, *fields):
    moves, width, ny, nz = fields[1].shape
    span = width + 4 * moves
    return pl.pallas_call(
        functools.partial(moves_kernel, depth),
        out_shape=(
            pltpu.VMEM((width, ny, nz), jnp.float32),
            pltpu.VMEM((width, ny, nz), jnp.float32),
            pltpu.VMEM((ny, width * nz), jnp.float32),
        ),
        in_specs=[SMEM] + [VMEM] * (1 + len(fields)),
        out_specs=(VMEM, VMEM, VMEM),
        scratch_shapes=[pltpu.VMEM((span, ny, nz), jnp.float32)] * 5,
        name="moves",
    )(in_smem(accept), in_vmem(root), *[in_vmem(field) for field in fields])


def sum_copies_kernel(parts_ref, copies_ref):
    total = parts_ref[0]
    for place in range(1, parts_ref.shape[0]):
        total += parts_ref[place]
    for place in range(copies_ref.shape[0]):
        copies_ref[place] = total


def sum_copies(parts):
    return pl.pallas_call(
        sum_copies_kernel,
        out_shape=pltpu.VMEM(parts.shape, jnp.float32),
        in_specs=[VMEM],
        out_specs=VMEM,
        name="sum_copies",
    )(in_vmem(parts))


def own_rows(ref, rows, owner):
    return ref.at[pl.ds(pl.multiple_of(owner * rows, rows), rows)]


def store_kernel(cond_ref, pot_ref, half_ref, cond_out, pot_out, rows_out, sems):
    own = own_rows(rows_out, half_ref.shape[0], lax.axis_index("member"))
    pairs = [(cond_ref, cond_out), (pot_ref, pot_out), (half_ref, own)]
    copies = [
        pltpu.make_async_copy(here, there, sems.at[i]) for i, (here, there) in enumerate(pairs)
    ]
    for copy in copies:
        copy.start()
    for copy in copies:
        copy.wait()


def store(conduct, pot, half):
    return pl.pallas_call(
        store_kernel,
        out_shape=(
            jax.ShapeDtypeStruct(conduct.shape, jnp.float32),
            jax.ShapeDtypeStruct(pot.shape, jnp.float32),
            jax.ShapeDtypeStruct((pair * half.shape[0], half.shape[1]), jnp.float32),
        ),
        in_specs=[VMEM] * 3,
        out_specs=(ANY,) * 3,
        scratch_shapes=[pltpu.SemaphoreType.DMA((3,))],
        name="store",
    )(in_vmem(conduct), in_vmem(pot), in_vmem(half))


def store_other_kernel(half_ref, held_ref, rows_out, sem):
    other = own_rows(rows_out, half_ref.shape[0], 1 - lax.axis_index("member"))
    copy = pltpu.make_async_copy(half_ref, other, sem)
    copy.start()
    copy.wait()


def store_other(half, held):
    return pl.pallas_call(
        store_other_kernel,
        out_shape=jax.ShapeDtypeStruct(held.shape, jnp.float32),
        in_specs=[VMEM, ANY],
        out_specs=ANY,
        scratch_shapes=[pltpu.SemaphoreType.DMA],
        input_output_aliases={1: 0},
        name="store_other",
    )(in_vmem(half), held)


def exchange_halo(low_edge, high_edge):
    count = lax.axis_size("tile")
    forward = [(i, i + 1) for i in range(count - 1)]
    backward = [(target, source) for source, target in forward]
    low = lax.ppermute(high_edge, "tile", forward)
    high = lax.ppermute(low_edge, "tile", backward)
    return low, high


def swap(block):
    return lax.ppermute(block, "member", [(0, 1), (1, 0)])


def exchange_by_member(low_edge, high_edge):
    count = lax.axis_size("tile")
    up = [(i, i + 1) for i in range(count - 1)]
    down = [(count + target, count + source) for source, target in up]
    even = lax.axis_index("member") == 0
    got = swap(jnp.where(even, low_edge, high_edge))
    lane = jnp.concatenate([jnp.where(even, high_edge, low_edge), got])
    return lax.ppermute(lane, ("member", "tile"), up + down)


def local(log_cond, potential, noise, source, parents, accept, weights):
    moves = noise.shape[0]
    width, ny, nz = source.shape
    reach = 2 * moves

    depth = tuple(reach - 2 * m for m in range(moves)) + (reach - 1,)
    weights, parents, accept, pieces, noise, source, low_edge, high_edge = pack(
        weights, parents, accept[:, 0], log_cond, potential, noise[:, 0], source,
        lax.axis_size("pairs"), depth,
    )
    pieces = lax.all_to_all(pieces, "pairs", 0, 0, tiled=True)
    came = exchange_by_member(low_edge, high_edge)
    chosen, root = choose(parents, weights, pieces, swap(pieces))
    moved = lax.all_to_all(chosen, "pairs", 0, 0, tiled=True).reshape(2, width, ny, nz)
    low_edge, high_edge, other = cut(reach, moved, came)
    moved_low, moved_high = exchange_halo(low_edge, high_edge)
    conduct, pot, traces = run_moves(
        depth, accept, root, moved, noise, source, moved_low, moved_high, came, swap(other)
    )

    rows = traces.shape[1] // (lax.axis_size("tile") * pair)
    member = lax.axis_index("member")
    piece = lax.all_gather(traces, "tile", axis=0, tiled=True)

    def product(owner):
        columns = lax.dynamic_slice_in_dim(
            piece, (lax.axis_index("tile") * pair + owner) * rows, rows, 1
        )
        return lax.dot_general(
            columns,
            piece,
            (((0,), (0,)), ((), ())),
            precision=lax.Precision.HIGH,
            preferred_element_type=jnp.float32,
        ).reshape(lax.axis_size("pairs"), -1, piece.shape[1])

    got = swap(product(1 - member))
    parts = lax.all_to_all(product(member) + got, "pairs", 0, 0, tiled=True)
    mine = lax.all_to_all(sum_copies(parts), "pairs", 0, 0, tiled=True)
    other = swap(mine).reshape(rows, -1)
    conduct, pot, held = store(conduct, pot, mine.reshape(rows, -1))
    moments = store_other(other, held)
    return (conduct[None], pot[None], moments)


def solution(mesh):
    tiles = mesh.shape["tile"]
    split = jax.sharding.Mesh(
        mesh.devices.reshape(-1, pair, tiles), ("pairs", "member", "tile")
    )
    placed = (
        P(group, "tile", None, None),
        P(group, "tile", None, None),
        P(None, group, "tile", None, None),
        P("tile", None, None),
        P(),
        P(None, group),
        P(group),
    )
    return jax.shard_map(
        local,
        mesh=split,
        in_specs=placed,
        out_specs=(P(group, "tile", None, None), P(group, "tile", None, None), P("tile", None)),
        check_vma=False,
    )
```

```python
import functools

import jax
import jax.numpy as jnp
from jax import lax
from jax.experimental import pallas as pl
from jax.experimental.pallas import tpu as pltpu
from jax.sharding import PartitionSpec as P

prior_keep = 0.8
prior_fresh = 0.6
relax_weight = 0.8
pair = 2
group = ("pairs", "member")

SMEM = pl.BlockSpec(memory_space=pltpu.SMEM)
VMEM = pl.BlockSpec(memory_space=pltpu.VMEM)
ANY = pl.BlockSpec(memory_space=pl.ANY)


def in_smem(array):
    return pltpu.with_memory_space_constraint(array, pltpu.SMEM)


def in_vmem(array):
    return pltpu.with_memory_space_constraint(array, pltpu.VMEM)


def pack_kernel(
    rows, weight_ref, parents_ref, accept_ref, cond_ref, pot_ref, noise_ref, source_ref,
    weight_out, parents_out, accept_out, pieces_ref, noise_out, source_out, sems,
):
    pairs = [(weight_ref, weight_out), (parents_ref, parents_out), (accept_ref, accept_out)]
    for piece in range(pieces_ref.shape[0]):
        row = piece * rows
        field = cond_ref if row < cond_ref.shape[0] else pot_ref
        row %= cond_ref.shape[0]
        pairs.append((field.at[pl.ds(row, rows)], pieces_ref.at[piece, pl.ds(0, rows)]))
    pairs += [(noise_ref, noise_out), (source_ref, source_out)]
    copies = [
        pltpu.make_async_copy(here, there, sems.at[i]) for i, (here, there) in enumerate(pairs)
    ]
    for copy in copies:
        copy.start()
    for copy in copies:
        copy.wait()
    weight = jnp.full((8, pieces_ref.shape[2]), weight_out[0], jnp.float32)
    for piece in range(pieces_ref.shape[0]):
        pieces_ref[piece, rows:rows + 8] = weight


def pack(weights, parents, accept, log_cond, potential, noise, source, pairs):
    nz = source.shape[2]
    rows = 2 * log_cond.size // (pairs * nz)
    return pl.pallas_call(
        functools.partial(pack_kernel, rows),
        out_shape=(
            pltpu.SMEM(weights.shape, jnp.float32),
            pltpu.SMEM(parents.shape, jnp.int32),
            pltpu.SMEM(accept.shape, jnp.int32),
            pltpu.VMEM((pairs, rows + 8, nz), jnp.float32),
            pltpu.VMEM(noise.shape, jnp.float32),
            pltpu.VMEM(source.shape, jnp.float32),
        ),
        in_specs=[ANY] * 7,
        out_specs=(SMEM,) * 3 + (VMEM,) * 3,
        scratch_shapes=[pltpu.SemaphoreType.DMA((pairs + 5,))],
        name="pack",
    )(weights, parents, accept, log_cond.reshape(-1, nz), potential.reshape(-1, nz), noise, source)


def choose_kernel(parents_ref, weight_ref, mine_ref, other_ref, chosen_ref, root_ref):
    member = lax.axis_index("member")
    rows = chosen_ref.shape[1]
    for place in range(chosen_ref.shape[0]):
        parent = parents_ref[place * pair + member]
        here = lax.rem(parent, pair) == member
        at = lax.div(parent, pair)
        chosen_ref[place] = jnp.where(
            here, mine_ref[at, pl.ds(0, rows)], other_ref[at, pl.ds(0, rows)]
        )
    total = jnp.zeros_like(root_ref)
    for place in range(chosen_ref.shape[0]):
        total += mine_ref[place, rows:rows + 8] + other_ref[place, rows:rows + 8]
    root_ref[...] = jnp.sqrt(weight_ref[0] / total)


def choose(parents, weights, mine, other):
    pairs, rows, nz = mine.shape
    return pl.pallas_call(
        choose_kernel,
        out_shape=(
            pltpu.VMEM((pairs, rows - 8, nz), jnp.float32),
            pltpu.VMEM((8, nz), jnp.float32),
        ),
        in_specs=[SMEM, SMEM, VMEM, VMEM],
        out_specs=(VMEM, VMEM),
        name="choose",
    )(in_smem(parents), in_smem(weights), in_vmem(mine), in_vmem(other))


def six_sum(before, here, after, edge):
    row = lax.broadcasted_iota(jnp.int32, here.shape, 0)
    lane = lax.broadcasted_iota(jnp.int32, here.shape, 1)
    ny, nz = here.shape
    down = jnp.where(row == 0, edge, pltpu.roll(here, 1, 0))
    up = jnp.where(row == ny - 1, edge, pltpu.roll(here, ny - 1, 0))
    left = jnp.where(lane == 0, edge, pltpu.roll(here, 1, 1))
    right = jnp.where(lane == nz - 1, edge, pltpu.roll(here, nz - 1, 1))
    return ((before + after) + (down + up)) + (left + right)


def layout(moves):
    reach = 2 * moves
    depth = [reach] + [reach - 2 * m for m in range(moves)] + [reach - 1]
    return [sum(depth[:i]) for i in range(len(depth))], depth


def edges_kernel(accept_ref, moved_ref, noise_ref, source_ref, low_ref, high_ref):
    moves, width = noise_ref.shape[:2]
    at, depth = layout(moves)
    for out_ref, place in [(low_ref, lambda h, i: i), (high_ref, lambda h, i: width - h + i)]:
        for i in range(depth[0]):
            out_ref[at[0] + i] = moved_ref[1, place(depth[0], i)]
        for i in range(depth[-1]):
            out_ref[at[-1] + i] = source_ref[place(depth[-1], i)]
        conduct = {place(depth[1], i): moved_ref[0, place(depth[1], i)] for i in range(depth[1])}
        for m in range(moves):
            accepted = accept_ref[m] > 0
            for i in range(depth[1 + m]):
                layer = place(depth[1 + m], i)
                proposal = prior_keep * conduct[layer] + prior_fresh * noise_ref[m, layer]
                out_ref[at[1 + m] + i] = proposal
                conduct[layer] = jnp.where(accepted, proposal, conduct[layer])


def edges(accept, moved, noise, source):
    at, depth = layout(noise.shape[0])
    out = pltpu.VMEM((sum(depth),) + source.shape[1:], jnp.float32)
    return pl.pallas_call(
        edges_kernel,
        out_shape=(out, out),
        in_specs=[SMEM] + [VMEM] * 3,
        out_specs=(VMEM, VMEM),
        name="edges",
    )(in_smem(accept), *[in_vmem(field) for field in (moved, noise, source)])


def moves_kernel(
    accept_ref, root_ref, moved_ref, noise_ref, source_ref, low_ref, high_ref,
    cond_out, pot_out, traces_out, pot, once, conductivity, gain,
):
    moves, width, _, nz = noise_ref.shape
    reach = 2 * moves
    span = width + 2 * reach
    at, depth = layout(moves)
    tile = lax.axis_index("tile")
    first = tile == 0
    last = tile == lax.axis_size("tile") - 1

    def halo(number, i):
        if i < 0:
            return low_ref[at[number] + depth[number] + i]
        return high_ref[at[number] + i - width]

    def own(i):
        return 0 <= i < width

    def keep_inside(value, i):
        outside = (first & (i < reach)) | (last & (i >= reach + width))
        return jnp.where(outside, 0.0, value)

    def sweep(old, lo, hi):
        for i in range(lo, hi):
            here, here_k = old[i], conductivity[i]
            before, after = old[i - 1], old[i + 1]
            plain = six_sum(before, here, after, 0.0)
            scaled = six_sum(
                before * conductivity[i - 1], here * here_k, after * conductivity[i + 1], 0.0
            )
            x = i - reach
            source = source_ref[x] if own(x) else halo(1 + moves, x)
            value = (1.0 - relax_weight) * here + (
                2.0 * source + (here_k * plain + scaled)
            ) * gain[i]
            yield i, keep_inside(value, i)

    for i in range(span):
        x = i - reach
        pot[i] = moved_ref[1, x] if own(x) else halo(0, x)
        if own(x):
            cond_out[x] = moved_ref[0, x]

    for m in range(moves):
        start = 2 * m
        accepted = accept_ref[m] > 0
        for i in range(start, span - start):
            x = i - reach
            if own(x):
                conduct = cond_out[x]
                proposal = prior_keep * conduct + prior_fresh * noise_ref[m, x]
                cond_out[x] = jnp.where(accepted, proposal, conduct)
            else:
                proposal = halo(1 + m, x)
            conductivity[i] = jnp.exp(proposal)
        for i in range(start + 1, span - start - 1):
            here_k = conductivity[i]
            gain[i] = relax_weight / (
                6.0 * here_k + six_sum(conductivity[i - 1], here_k, conductivity[i + 1], 1.0)
            )
        for i, value in sweep(pot, start + 1, span - start - 1):
            once[i] = value
        for i, value in sweep(once, start + 2, span - start - 2):
            pot[i] = jnp.where(accepted, value, pot[i])

    root = root_ref[0:1]
    for x in range(width):
        value = pot[x + reach]
        pot_out[x] = value
        traces_out[:, x * nz:(x + 1) * nz] = value * root


def run_moves(accept, root, *fields):
    moves, width, ny, nz = fields[1].shape
    span = width + 4 * moves
    return pl.pallas_call(
        moves_kernel,
        out_shape=(
            pltpu.VMEM((width, ny, nz), jnp.float32),
            pltpu.VMEM((width, ny, nz), jnp.float32),
            pltpu.VMEM((ny, width * nz), jnp.float32),
        ),
        in_specs=[SMEM] + [VMEM] * (1 + len(fields)),
        out_specs=(VMEM, VMEM, VMEM),
        scratch_shapes=[pltpu.VMEM((span, ny, nz), jnp.float32)] * 4,
        name="moves",
    )(in_smem(accept), in_vmem(root), *[in_vmem(field) for field in fields])


def sum_copies_kernel(parts_ref, copies_ref):
    total = parts_ref[0]
    for place in range(1, parts_ref.shape[0]):
        total += parts_ref[place]
    for place in range(copies_ref.shape[0]):
        copies_ref[place] = total


def sum_copies(parts):
    return pl.pallas_call(
        sum_copies_kernel,
        out_shape=pltpu.VMEM(parts.shape, jnp.float32),
        in_specs=[VMEM],
        out_specs=VMEM,
        name="sum_copies",
    )(in_vmem(parts))


def own_rows(ref, rows, owner):
    return ref.at[pl.ds(pl.multiple_of(owner * rows, rows), rows)]


def store_kernel(cond_ref, pot_ref, half_ref, cond_out, pot_out, rows_out, sems):
    own = own_rows(rows_out, half_ref.shape[0], lax.axis_index("member"))
    pairs = [(cond_ref, cond_out), (pot_ref, pot_out), (half_ref, own)]
    copies = [
        pltpu.make_async_copy(here, there, sems.at[i]) for i, (here, there) in enumerate(pairs)
    ]
    for copy in copies:
        copy.start()
    for copy in copies:
        copy.wait()


def store(conduct, pot, half):
    return pl.pallas_call(
        store_kernel,
        out_shape=(
            jax.ShapeDtypeStruct(conduct.shape, jnp.float32),
            jax.ShapeDtypeStruct(pot.shape, jnp.float32),
            jax.ShapeDtypeStruct((pair * half.shape[0], half.shape[1]), jnp.float32),
        ),
        in_specs=[VMEM] * 3,
        out_specs=(ANY,) * 3,
        scratch_shapes=[pltpu.SemaphoreType.DMA((3,))],
        name="store",
    )(in_vmem(conduct), in_vmem(pot), in_vmem(half))


def store_other_kernel(half_ref, held_ref, rows_out, sem):
    other = own_rows(rows_out, half_ref.shape[0], 1 - lax.axis_index("member"))
    copy = pltpu.make_async_copy(half_ref, other, sem)
    copy.start()
    copy.wait()


def store_other(half, held):
    return pl.pallas_call(
        store_other_kernel,
        out_shape=jax.ShapeDtypeStruct(held.shape, jnp.float32),
        in_specs=[VMEM, ANY],
        out_specs=ANY,
        scratch_shapes=[pltpu.SemaphoreType.DMA],
        input_output_aliases={1: 0},
        name="store_other",
    )(in_vmem(half), held)


def exchange_halo(low_edge, high_edge):
    count = lax.axis_size("tile")
    forward = [(i, i + 1) for i in range(count - 1)]
    backward = [(target, source) for source, target in forward]
    low = lax.ppermute(high_edge, "tile", forward)
    high = lax.ppermute(low_edge, "tile", backward)
    return low, high


def swap(block):
    return lax.ppermute(block, "member", [(0, 1), (1, 0)])


def local(log_cond, potential, noise, source, parents, accept, weights):
    width, ny, nz = source.shape

    weights, parents, accept, pieces, noise, source = pack(
        weights, parents, accept[:, 0], log_cond, potential, noise[:, 0], source,
        lax.axis_size("pairs"),
    )
    pieces = lax.all_to_all(pieces, "pairs", 0, 0, tiled=True)
    chosen, root = choose(parents, weights, pieces, swap(pieces))
    moved = lax.all_to_all(chosen, "pairs", 0, 0, tiled=True).reshape(2, width, ny, nz)
    low, high = exchange_halo(*edges(accept, moved, noise, source))
    conduct, pot, traces = run_moves(accept, root, moved, noise, source, low, high)

    rows = traces.shape[1] // (lax.axis_size("tile") * pair)
    member = lax.axis_index("member")
    piece = lax.all_gather(traces, "tile", axis=0, tiled=True)

    def product(owner):
        columns = lax.dynamic_slice_in_dim(
            piece, (lax.axis_index("tile") * pair + owner) * rows, rows, 1
        )
        return lax.dot_general(
            columns,
            piece,
            (((0,), (0,)), ((), ())),
            precision=lax.Precision.HIGH,
            preferred_element_type=jnp.float32,
        ).reshape(lax.axis_size("pairs"), -1, piece.shape[1])

    got = swap(product(1 - member))
    parts = lax.all_to_all(product(member) + got, "pairs", 0, 0, tiled=True)
    mine = lax.all_to_all(sum_copies(parts), "pairs", 0, 0, tiled=True)
    other = swap(mine).reshape(rows, -1)
    conduct, pot, held = store(conduct, pot, mine.reshape(rows, -1))
    moments = store_other(other, held)
    return (conduct[None], pot[None], moments)


def solution(mesh):
    tiles = mesh.shape["tile"]
    split = jax.sharding.Mesh(
        mesh.devices.reshape(-1, pair, tiles), ("pairs", "member", "tile")
    )
    placed = (
        P(group, "tile", None, None),
        P(group, "tile", None, None),
        P(None, group, "tile", None, None),
        P("tile", None, None),
        P(),
        P(None, group),
        P(group),
    )
    return jax.shard_map(
        local,
        mesh=split,
        in_specs=placed,
        out_specs=(P(group, "tile", None, None), P(group, "tile", None, None), P("tile", None)),
        check_vma=False,
    )
```

```python
import functools

import jax
import jax.numpy as jnp
from jax import lax
from jax.experimental import pallas as pl
from jax.experimental.pallas import tpu as pltpu
from jax.sharding import PartitionSpec as P

prior_keep = 0.8
prior_fresh = 0.6
relax_weight = 0.8
pair = 2
group = ("pairs", "member")

SMEM = pl.BlockSpec(memory_space=pltpu.SMEM)
VMEM = pl.BlockSpec(memory_space=pltpu.VMEM)
ANY = pl.BlockSpec(memory_space=pl.ANY)


def in_smem(array):
    return pltpu.with_memory_space_constraint(array, pltpu.SMEM)


def in_vmem(array):
    return pltpu.with_memory_space_constraint(array, pltpu.VMEM)


def pack_kernel(
    rows, weight_ref, parents_ref, accept_ref, cond_ref, pot_ref, noise_ref, source_ref,
    weight_out, parents_out, accept_out, pieces_ref, noise_out, source_out, sems,
):
    pairs = [(weight_ref, weight_out), (parents_ref, parents_out), (accept_ref, accept_out)]
    for piece in range(pieces_ref.shape[0]):
        row = piece * rows
        field = cond_ref if row < cond_ref.shape[0] else pot_ref
        row %= cond_ref.shape[0]
        pairs.append((field.at[pl.ds(row, rows)], pieces_ref.at[piece, pl.ds(0, rows)]))
    pairs += [(noise_ref, noise_out), (source_ref, source_out)]
    copies = [
        pltpu.make_async_copy(here, there, sems.at[i]) for i, (here, there) in enumerate(pairs)
    ]
    for copy in copies:
        copy.start()
    for copy in copies:
        copy.wait()
    weight = jnp.full((8, pieces_ref.shape[2]), weight_out[0], jnp.float32)
    for piece in range(pieces_ref.shape[0]):
        pieces_ref[piece, rows:rows + 8] = weight


def pack(weights, parents, accept, log_cond, potential, noise, source, pairs):
    nz = source.shape[2]
    rows = 2 * log_cond.size // (pairs * nz)
    return pl.pallas_call(
        functools.partial(pack_kernel, rows),
        out_shape=(
            pltpu.SMEM(weights.shape, jnp.float32),
            pltpu.SMEM(parents.shape, jnp.int32),
            pltpu.SMEM(accept.shape, jnp.int32),
            pltpu.VMEM((pairs, rows + 8, nz), jnp.float32),
            pltpu.VMEM(noise.shape, jnp.float32),
            pltpu.VMEM(source.shape, jnp.float32),
        ),
        in_specs=[ANY] * 7,
        out_specs=(SMEM,) * 3 + (VMEM,) * 3,
        scratch_shapes=[pltpu.SemaphoreType.DMA((pairs + 5,))],
        name="pack",
    )(weights, parents, accept, log_cond.reshape(-1, nz), potential.reshape(-1, nz), noise, source)


def choose_kernel(parents_ref, weight_ref, mine_ref, other_ref, chosen_ref, root_ref):
    member = lax.axis_index("member")
    rows = chosen_ref.shape[1]
    for place in range(chosen_ref.shape[0]):
        parent = parents_ref[place * pair + member]
        here = lax.rem(parent, pair) == member
        at = lax.div(parent, pair)
        chosen_ref[place] = jnp.where(
            here, mine_ref[at, pl.ds(0, rows)], other_ref[at, pl.ds(0, rows)]
        )
    total = jnp.zeros_like(root_ref)
    for place in range(chosen_ref.shape[0]):
        total += mine_ref[place, rows:rows + 8] + other_ref[place, rows:rows + 8]
    root_ref[...] = jnp.sqrt(weight_ref[0] / total)


def choose(parents, weights, mine, other):
    pairs, rows, nz = mine.shape
    return pl.pallas_call(
        choose_kernel,
        out_shape=(
            pltpu.VMEM((pairs, rows - 8, nz), jnp.float32),
            pltpu.VMEM((8, nz), jnp.float32),
        ),
        in_specs=[SMEM, SMEM, VMEM, VMEM],
        out_specs=(VMEM, VMEM),
        name="choose",
    )(in_smem(parents), in_smem(weights), in_vmem(mine), in_vmem(other))


def shifts(here):
    ny, nz = here.shape
    return [pltpu.roll(here, by, axis) for by, axis in [(1, 0), (ny - 1, 0), (1, 1), (nz - 1, 1)]]


def outer(shape):
    row = lax.broadcasted_iota(jnp.int32, shape, 0)
    lane = lax.broadcasted_iota(jnp.int32, shape, 1)
    return [row == 0, row == shape[0] - 1, lane == 0, lane == shape[1] - 1]


def layout(moves):
    reach = 2 * moves
    depth = [reach] + [reach - 2 * m for m in range(moves)] + [reach - 1]
    return [sum(depth[:i]) for i in range(len(depth))], depth


def edges_kernel(accept_ref, moved_ref, noise_ref, source_ref, low_ref, high_ref):
    moves, width = noise_ref.shape[:2]
    at, depth = layout(moves)
    for out_ref, place in [(low_ref, lambda h, i: i), (high_ref, lambda h, i: width - h + i)]:
        for i in range(depth[0]):
            out_ref[at[0] + i] = moved_ref[1, place(depth[0], i)]
        for i in range(depth[-1]):
            out_ref[at[-1] + i] = source_ref[place(depth[-1], i)]
        conduct = {place(depth[1], i): moved_ref[0, place(depth[1], i)] for i in range(depth[1])}
        for m in range(moves):
            accepted = accept_ref[m] > 0
            for i in range(depth[1 + m]):
                layer = place(depth[1 + m], i)
                proposal = prior_keep * conduct[layer] + prior_fresh * noise_ref[m, layer]
                out_ref[at[1 + m] + i] = proposal
                conduct[layer] = jnp.where(accepted, proposal, conduct[layer])


def edges(accept, moved, noise, source):
    at, depth = layout(noise.shape[0])
    out = pltpu.VMEM((sum(depth),) + source.shape[1:], jnp.float32)
    return pl.pallas_call(
        edges_kernel,
        out_shape=(out, out),
        in_specs=[SMEM] + [VMEM] * 3,
        out_specs=(VMEM, VMEM),
        name="edges",
    )(in_smem(accept), *[in_vmem(field) for field in (moved, noise, source)])


def moves_kernel(
    accept_ref, root_ref, moved_ref, noise_ref, source_ref, low_ref, high_ref,
    cond_out, pot_out, traces_out, pot, once, conductivity, gain, faces,
):
    moves, width, ny, nz = noise_ref.shape
    reach = 2 * moves
    span = width + 2 * reach
    at, depth = layout(moves)
    tile = lax.axis_index("tile")
    first = tile == 0
    last = tile == lax.axis_size("tile") - 1

    def halo(number, i):
        if i < 0:
            return low_ref[at[number] + depth[number] + i]
        return high_ref[at[number] + i - width]

    def own(i):
        return 0 <= i < width

    def keep_inside(value, i):
        outside = (first & (i < reach)) | (last & (i >= reach + width))
        return jnp.where(outside, 0.0, value)

    def sweep(old, lo, hi):
        for i in range(lo, hi):
            here, here_k = old[i], conductivity[i]
            flux = (here_k + conductivity[i - 1]) * old[i - 1] + (
                here_k + conductivity[i + 1]
            ) * old[i + 1]
            for side, near in enumerate(shifts(here)):
                flux += faces[side, i] * near
            x = i - reach
            source = source_ref[x] if own(x) else halo(1 + moves, x)
            value = (1.0 - relax_weight) * here + (
                2.0 * source + flux
            ) * gain[i]
            yield i, keep_inside(value, i)

    for i in range(span):
        x = i - reach
        pot[i] = moved_ref[1, x] if own(x) else halo(0, x)
        if own(x):
            cond_out[x] = moved_ref[0, x]

    for m in range(moves):
        start = 2 * m
        accepted = accept_ref[m] > 0
        for i in range(start, span - start):
            x = i - reach
            if own(x):
                conduct = cond_out[x]
                proposal = prior_keep * conduct + prior_fresh * noise_ref[m, x]
                cond_out[x] = jnp.where(accepted, proposal, conduct)
            else:
                proposal = halo(1 + m, x)
            conductivity[i] = jnp.exp(proposal)
        for i in range(start + 1, span - start - 1):
            here_k = conductivity[i]
            total = 6.0 * here_k + conductivity[i - 1] + conductivity[i + 1]
            for side, (near, outside) in enumerate(zip(shifts(here_k), outer((ny, nz)))):
                total += jnp.where(outside, 1.0, near)
                faces[side, i] = jnp.where(outside, 0.0, here_k + near)
            gain[i] = relax_weight / total
        for i, value in sweep(pot, start + 1, span - start - 1):
            once[i] = value
        for i, value in sweep(once, start + 2, span - start - 2):
            pot[i] = jnp.where(accepted, value, pot[i])

    root = root_ref[0:1]
    for x in range(width):
        value = pot[x + reach]
        pot_out[x] = value
        traces_out[:, x * nz:(x + 1) * nz] = value * root


def run_moves(accept, root, *fields):
    moves, width, ny, nz = fields[1].shape
    span = width + 4 * moves
    return pl.pallas_call(
        moves_kernel,
        out_shape=(
            pltpu.VMEM((width, ny, nz), jnp.float32),
            pltpu.VMEM((width, ny, nz), jnp.float32),
            pltpu.VMEM((ny, width * nz), jnp.float32),
        ),
        in_specs=[SMEM] + [VMEM] * (1 + len(fields)),
        out_specs=(VMEM, VMEM, VMEM),
        scratch_shapes=[pltpu.VMEM((span, ny, nz), jnp.float32)] * 4
        + [pltpu.VMEM((4, span, ny, nz), jnp.float32)],
        name="moves",
    )(in_smem(accept), in_vmem(root), *[in_vmem(field) for field in fields])


def sum_copies_kernel(parts_ref, copies_ref):
    total = parts_ref[0]
    for place in range(1, parts_ref.shape[0]):
        total += parts_ref[place]
    for place in range(copies_ref.shape[0]):
        copies_ref[place] = total


def sum_copies(parts):
    return pl.pallas_call(
        sum_copies_kernel,
        out_shape=pltpu.VMEM(parts.shape, jnp.float32),
        in_specs=[VMEM],
        out_specs=VMEM,
        name="sum_copies",
    )(in_vmem(parts))


def own_rows(ref, rows, owner):
    return ref.at[pl.ds(pl.multiple_of(owner * rows, rows), rows)]


def store_kernel(cond_ref, pot_ref, half_ref, cond_out, pot_out, rows_out, sems):
    own = own_rows(rows_out, half_ref.shape[0], lax.axis_index("member"))
    pairs = [(cond_ref, cond_out), (pot_ref, pot_out), (half_ref, own)]
    copies = [
        pltpu.make_async_copy(here, there, sems.at[i]) for i, (here, there) in enumerate(pairs)
    ]
    for copy in copies:
        copy.start()
    for copy in copies:
        copy.wait()


def store(conduct, pot, half):
    return pl.pallas_call(
        store_kernel,
        out_shape=(
            jax.ShapeDtypeStruct(conduct.shape, jnp.float32),
            jax.ShapeDtypeStruct(pot.shape, jnp.float32),
            jax.ShapeDtypeStruct((pair * half.shape[0], half.shape[1]), jnp.float32),
        ),
        in_specs=[VMEM] * 3,
        out_specs=(ANY,) * 3,
        scratch_shapes=[pltpu.SemaphoreType.DMA((3,))],
        name="store",
    )(in_vmem(conduct), in_vmem(pot), in_vmem(half))


def store_other_kernel(half_ref, held_ref, rows_out, sem):
    other = own_rows(rows_out, half_ref.shape[0], 1 - lax.axis_index("member"))
    copy = pltpu.make_async_copy(half_ref, other, sem)
    copy.start()
    copy.wait()


def store_other(half, held):
    return pl.pallas_call(
        store_other_kernel,
        out_shape=jax.ShapeDtypeStruct(held.shape, jnp.float32),
        in_specs=[VMEM, ANY],
        out_specs=ANY,
        scratch_shapes=[pltpu.SemaphoreType.DMA],
        input_output_aliases={1: 0},
        name="store_other",
    )(in_vmem(half), held)


def exchange_halo(low_edge, high_edge):
    count = lax.axis_size("tile")
    forward = [(i, i + 1) for i in range(count - 1)]
    backward = [(target, source) for source, target in forward]
    low = lax.ppermute(high_edge, "tile", forward)
    high = lax.ppermute(low_edge, "tile", backward)
    return low, high


def swap(block):
    return lax.ppermute(block, "member", [(0, 1), (1, 0)])


def local(log_cond, potential, noise, source, parents, accept, weights):
    width, ny, nz = source.shape

    weights, parents, accept, pieces, noise, source = pack(
        weights, parents, accept[:, 0], log_cond, potential, noise[:, 0], source,
        lax.axis_size("pairs"),
    )
    pieces = lax.all_to_all(pieces, "pairs", 0, 0, tiled=True)
    chosen, root = choose(parents, weights, pieces, swap(pieces))
    moved = lax.all_to_all(chosen, "pairs", 0, 0, tiled=True).reshape(2, width, ny, nz)
    low, high = exchange_halo(*edges(accept, moved, noise, source))
    conduct, pot, traces = run_moves(accept, root, moved, noise, source, low, high)

    rows = traces.shape[1] // (lax.axis_size("tile") * pair)
    member = lax.axis_index("member")
    piece = lax.all_gather(traces, "tile", axis=0, tiled=True)

    def product(owner):
        columns = lax.dynamic_slice_in_dim(
            piece, (lax.axis_index("tile") * pair + owner) * rows, rows, 1
        )
        return lax.dot_general(
            columns,
            piece,
            (((0,), (0,)), ((), ())),
            precision=lax.Precision.HIGH,
            preferred_element_type=jnp.float32,
        ).reshape(lax.axis_size("pairs"), -1, piece.shape[1])

    got = swap(product(1 - member))
    parts = lax.all_to_all(product(member) + got, "pairs", 0, 0, tiled=True)
    mine = lax.all_to_all(sum_copies(parts), "pairs", 0, 0, tiled=True)
    other = swap(mine).reshape(rows, -1)
    conduct, pot, held = store(conduct, pot, mine.reshape(rows, -1))
    moments = store_other(other, held)
    return (conduct[None], pot[None], moments)


def solution(mesh):
    tiles = mesh.shape["tile"]
    split = jax.sharding.Mesh(
        mesh.devices.reshape(-1, pair, tiles), ("pairs", "member", "tile")
    )
    placed = (
        P(group, "tile", None, None),
        P(group, "tile", None, None),
        P(None, group, "tile", None, None),
        P("tile", None, None),
        P(),
        P(None, group),
        P(group),
    )
    return jax.shard_map(
        local,
        mesh=split,
        in_specs=placed,
        out_specs=(P(group, "tile", None, None), P(group, "tile", None, None), P("tile", None)),
        check_vma=False,
    )
```

```python
import functools

import jax
import jax.numpy as jnp
from jax import lax
from jax.experimental import pallas as pl
from jax.experimental.pallas import tpu as pltpu
from jax.sharding import PartitionSpec as P

prior_keep = 0.8
prior_fresh = 0.6
relax_weight = 0.8
pair = 2
group = ("pairs", "member")

SMEM = pl.BlockSpec(memory_space=pltpu.SMEM)
VMEM = pl.BlockSpec(memory_space=pltpu.VMEM)
ANY = pl.BlockSpec(memory_space=pl.ANY)


def in_smem(array):
    return pltpu.with_memory_space_constraint(array, pltpu.SMEM)


def in_vmem(array):
    return pltpu.with_memory_space_constraint(array, pltpu.VMEM)


def quarters(here, there):
    layers = max(1, here.shape[0] // 4)
    return [
        (here.at[pl.ds(i, layers)], there.at[pl.ds(i, layers)])
        for i in range(0, here.shape[0], layers)
    ]


def pack_kernel(
    rows, weight_ref, parents_ref, accept_ref, cond_ref, pot_ref, noise_ref, source_ref,
    weight_out, parents_out, accept_out, pieces_ref, noise_out, source_out, sems,
):
    pairs = [(weight_ref, weight_out), (parents_ref, parents_out), (accept_ref, accept_out)]
    for piece in range(pieces_ref.shape[0]):
        row = piece * rows
        field = cond_ref if row < cond_ref.shape[0] else pot_ref
        row %= cond_ref.shape[0]
        pairs.append((field.at[pl.ds(row, rows)], pieces_ref.at[piece, pl.ds(0, rows)]))
    for move in range(noise_ref.shape[0]):
        pairs += quarters(noise_ref.at[move], noise_out.at[move])
    pairs += quarters(source_ref, source_out)
    copies = [
        pltpu.make_async_copy(here, there, sems.at[i]) for i, (here, there) in enumerate(pairs)
    ]
    for copy in copies:
        copy.start()
    for copy in copies:
        copy.wait()
    weight = jnp.full((8, pieces_ref.shape[2]), weight_out[0], jnp.float32)
    for piece in range(pieces_ref.shape[0]):
        pieces_ref[piece, rows:rows + 8] = weight


def pack(weights, parents, accept, log_cond, potential, noise, source, pairs):
    nz = source.shape[2]
    rows = 2 * log_cond.size // (pairs * nz)
    return pl.pallas_call(
        functools.partial(pack_kernel, rows),
        out_shape=(
            pltpu.SMEM(weights.shape, jnp.float32),
            pltpu.SMEM(parents.shape, jnp.int32),
            pltpu.SMEM(accept.shape, jnp.int32),
            pltpu.VMEM((pairs, rows + 8, nz), jnp.float32),
            pltpu.VMEM(noise.shape, jnp.float32),
            pltpu.VMEM(source.shape, jnp.float32),
        ),
        in_specs=[ANY] * 7,
        out_specs=(SMEM,) * 3 + (VMEM,) * 3,
        scratch_shapes=[pltpu.SemaphoreType.DMA((pairs + 3 + 8 * (1 + noise.shape[0]),))],
        name="pack",
    )(weights, parents, accept, log_cond.reshape(-1, nz), potential.reshape(-1, nz), noise, source)


def choose_kernel(parents_ref, weight_ref, mine_ref, other_ref, chosen_ref, root_ref):
    member = lax.axis_index("member")
    rows = chosen_ref.shape[1]
    for place in range(chosen_ref.shape[0]):
        parent = parents_ref[place * pair + member]
        here = lax.rem(parent, pair) == member
        at = lax.div(parent, pair)
        chosen_ref[place] = jnp.where(
            here, mine_ref[at, pl.ds(0, rows)], other_ref[at, pl.ds(0, rows)]
        )
    total = jnp.zeros_like(root_ref)
    for place in range(chosen_ref.shape[0]):
        total += mine_ref[place, rows:rows + 8] + other_ref[place, rows:rows + 8]
    root_ref[...] = jnp.sqrt(weight_ref[0] / total)


def choose(parents, weights, mine, other):
    pairs, rows, nz = mine.shape
    return pl.pallas_call(
        choose_kernel,
        out_shape=(
            pltpu.VMEM((pairs, rows - 8, nz), jnp.float32),
            pltpu.VMEM((8, nz), jnp.float32),
        ),
        in_specs=[SMEM, SMEM, VMEM, VMEM],
        out_specs=(VMEM, VMEM),
        name="choose",
    )(in_smem(parents), in_smem(weights), in_vmem(mine), in_vmem(other))


def shifts(here):
    ny, nz = here.shape
    return [pltpu.roll(here, by, axis) for by, axis in [(1, 0), (ny - 1, 0), (1, 1), (nz - 1, 1)]]


def outer(shape):
    row = lax.broadcasted_iota(jnp.int32, shape, 0)
    lane = lax.broadcasted_iota(jnp.int32, shape, 1)
    return [row == 0, row == shape[0] - 1, lane == 0, lane == shape[1] - 1]


def layout(moves):
    reach = 2 * moves
    depth = [reach] + [reach - 2 * m for m in range(moves)] + [reach - 1]
    return [sum(depth[:i]) for i in range(len(depth))], depth


def edges_kernel(accept_ref, moved_ref, noise_ref, source_ref, low_ref, high_ref):
    moves, width = noise_ref.shape[:2]
    at, depth = layout(moves)
    for out_ref, place in [(low_ref, lambda h, i: i), (high_ref, lambda h, i: width - h + i)]:
        for i in range(depth[0]):
            out_ref[at[0] + i] = moved_ref[1, place(depth[0], i)]
        for i in range(depth[-1]):
            out_ref[at[-1] + i] = source_ref[place(depth[-1], i)]
        conduct = {place(depth[1], i): moved_ref[0, place(depth[1], i)] for i in range(depth[1])}
        for m in range(moves):
            accepted = accept_ref[m] > 0
            for i in range(depth[1 + m]):
                layer = place(depth[1 + m], i)
                proposal = prior_keep * conduct[layer] + prior_fresh * noise_ref[m, layer]
                out_ref[at[1 + m] + i] = proposal
                conduct[layer] = jnp.where(accepted, proposal, conduct[layer])


def edges(accept, moved, noise, source):
    at, depth = layout(noise.shape[0])
    out = pltpu.VMEM((sum(depth),) + source.shape[1:], jnp.float32)
    return pl.pallas_call(
        edges_kernel,
        out_shape=(out, out),
        in_specs=[SMEM] + [VMEM] * 3,
        out_specs=(VMEM, VMEM),
        name="edges",
    )(in_smem(accept), *[in_vmem(field) for field in (moved, noise, source)])


def moves_kernel(
    accept_ref, root_ref, moved_ref, noise_ref, source_ref, low_ref, high_ref,
    cond_out, pot_out, traces_out, pot, once, conductivity, gain, faces,
):
    moves, width, ny, nz = noise_ref.shape
    reach = 2 * moves
    span = width + 2 * reach
    at, depth = layout(moves)
    tile = lax.axis_index("tile")
    first = tile == 0
    last = tile == lax.axis_size("tile") - 1

    def halo(number, i):
        if i < 0:
            return low_ref[at[number] + depth[number] + i]
        return high_ref[at[number] + i - width]

    def own(i):
        return 0 <= i < width

    def keep_inside(value, i):
        outside = (first & (i < reach)) | (last & (i >= reach + width))
        return jnp.where(outside, 0.0, value)

    def sweep(old, lo, hi):
        for i in range(lo, hi):
            here, here_k = old[i], conductivity[i]
            flux = (here_k + conductivity[i - 1]) * old[i - 1] + (
                here_k + conductivity[i + 1]
            ) * old[i + 1]
            for side, near in enumerate(shifts(here)):
                flux += faces[side, i] * near
            x = i - reach
            source = source_ref[x] if own(x) else halo(1 + moves, x)
            value = (1.0 - relax_weight) * here + (
                2.0 * source + flux
            ) * gain[i]
            yield i, keep_inside(value, i)

    for i in range(span):
        x = i - reach
        pot[i] = moved_ref[1, x] if own(x) else halo(0, x)
        if own(x):
            cond_out[x] = moved_ref[0, x]

    for m in range(moves):
        start = 2 * m
        accepted = accept_ref[m] > 0
        for i in range(start, span - start):
            x = i - reach
            if own(x):
                conduct = cond_out[x]
                proposal = prior_keep * conduct + prior_fresh * noise_ref[m, x]
                cond_out[x] = jnp.where(accepted, proposal, conduct)
            else:
                proposal = halo(1 + m, x)
            conductivity[i] = jnp.exp(proposal)
        for i in range(start + 1, span - start - 1):
            here_k = conductivity[i]
            total = 6.0 * here_k + conductivity[i - 1] + conductivity[i + 1]
            for side, (near, outside) in enumerate(zip(shifts(here_k), outer((ny, nz)))):
                total += jnp.where(outside, 1.0, near)
                faces[side, i] = jnp.where(outside, 0.0, here_k + near)
            gain[i] = relax_weight / total
        for i, value in sweep(pot, start + 1, span - start - 1):
            once[i] = value
        for i, value in sweep(once, start + 2, span - start - 2):
            pot[i] = jnp.where(accepted, value, pot[i])

    root = root_ref[0:1]
    for x in range(width):
        value = pot[x + reach]
        pot_out[x] = value
        traces_out[:, x * nz:(x + 1) * nz] = value * root


def run_moves(accept, root, *fields):
    moves, width, ny, nz = fields[1].shape
    span = width + 4 * moves
    return pl.pallas_call(
        moves_kernel,
        out_shape=(
            pltpu.VMEM((width, ny, nz), jnp.float32),
            pltpu.VMEM((width, ny, nz), jnp.float32),
            pltpu.VMEM((ny, width * nz), jnp.float32),
        ),
        in_specs=[SMEM] + [VMEM] * (1 + len(fields)),
        out_specs=(VMEM, VMEM, VMEM),
        scratch_shapes=[pltpu.VMEM((span, ny, nz), jnp.float32)] * 4
        + [pltpu.VMEM((4, span, ny, nz), jnp.float32)],
        name="moves",
    )(in_smem(accept), in_vmem(root), *[in_vmem(field) for field in fields])


def sum_copies_kernel(parts_ref, copies_ref):
    total = parts_ref[0]
    for place in range(1, parts_ref.shape[0]):
        total += parts_ref[place]
    for place in range(copies_ref.shape[0]):
        copies_ref[place] = total


def sum_copies(parts):
    return pl.pallas_call(
        sum_copies_kernel,
        out_shape=pltpu.VMEM(parts.shape, jnp.float32),
        in_specs=[VMEM],
        out_specs=VMEM,
        name="sum_copies",
    )(in_vmem(parts))


def own_rows(ref, rows, owner):
    return ref.at[pl.ds(pl.multiple_of(owner * rows, rows), rows)]


def store_kernel(cond_ref, pot_ref, half_ref, cond_out, pot_out, rows_out, sems):
    own = own_rows(rows_out, half_ref.shape[0], lax.axis_index("member"))
    pairs = [(cond_ref, cond_out), (pot_ref, pot_out), (half_ref, own)]
    copies = [
        pltpu.make_async_copy(here, there, sems.at[i]) for i, (here, there) in enumerate(pairs)
    ]
    for copy in copies:
        copy.start()
    for copy in copies:
        copy.wait()


def store(conduct, pot, half):
    return pl.pallas_call(
        store_kernel,
        out_shape=(
            jax.ShapeDtypeStruct(conduct.shape, jnp.float32),
            jax.ShapeDtypeStruct(pot.shape, jnp.float32),
            jax.ShapeDtypeStruct((pair * half.shape[0], half.shape[1]), jnp.float32),
        ),
        in_specs=[VMEM] * 3,
        out_specs=(ANY,) * 3,
        scratch_shapes=[pltpu.SemaphoreType.DMA((3,))],
        name="store",
    )(in_vmem(conduct), in_vmem(pot), in_vmem(half))


def store_other_kernel(half_ref, held_ref, rows_out, sems):
    other = own_rows(rows_out, half_ref.shape[0], 1 - lax.axis_index("member"))
    rows = half_ref.shape[0] // sems.shape[0]
    copies = [
        pltpu.make_async_copy(
            half_ref.at[pl.ds(i * rows, rows)], other.at[pl.ds(i * rows, rows)], sems.at[i]
        )
        for i in range(sems.shape[0])
    ]
    for copy in copies:
        copy.start()
    for copy in copies:
        copy.wait()


def store_other(half, held):
    return pl.pallas_call(
        store_other_kernel,
        out_shape=jax.ShapeDtypeStruct(held.shape, jnp.float32),
        in_specs=[VMEM, ANY],
        out_specs=ANY,
        scratch_shapes=[pltpu.SemaphoreType.DMA((max(1, half.shape[0] // 16),))],
        input_output_aliases={1: 0},
        name="store_other",
    )(in_vmem(half), held)


def exchange_halo(low_edge, high_edge):
    count = lax.axis_size("tile")
    forward = [(i, i + 1) for i in range(count - 1)]
    backward = [(target, source) for source, target in forward]
    low = lax.ppermute(high_edge, "tile", forward)
    high = lax.ppermute(low_edge, "tile", backward)
    return low, high


def swap(block):
    return lax.ppermute(block, "member", [(0, 1), (1, 0)])


def local(log_cond, potential, noise, source, parents, accept, weights):
    width, ny, nz = source.shape

    weights, parents, accept, pieces, noise, source = pack(
        weights, parents, accept[:, 0], log_cond, potential, noise[:, 0], source,
        lax.axis_size("pairs"),
    )
    pieces = lax.all_to_all(pieces, "pairs", 0, 0, tiled=True)
    chosen, root = choose(parents, weights, pieces, swap(pieces))
    moved = lax.all_to_all(chosen, "pairs", 0, 0, tiled=True).reshape(2, width, ny, nz)
    low, high = exchange_halo(*edges(accept, moved, noise, source))
    conduct, pot, traces = run_moves(accept, root, moved, noise, source, low, high)

    rows = traces.shape[1] // (lax.axis_size("tile") * pair)
    member = lax.axis_index("member")
    piece = lax.all_gather(traces, "tile", axis=0, tiled=True)

    def product(owner):
        columns = lax.dynamic_slice_in_dim(
            piece, (lax.axis_index("tile") * pair + owner) * rows, rows, 1
        )
        return lax.dot_general(
            columns,
            piece,
            (((0,), (0,)), ((), ())),
            precision=lax.Precision.HIGH,
            preferred_element_type=jnp.float32,
        ).reshape(lax.axis_size("pairs"), -1, piece.shape[1])

    got = swap(product(1 - member))
    parts = lax.all_to_all(product(member) + got, "pairs", 0, 0, tiled=True)
    mine = lax.all_to_all(sum_copies(parts), "pairs", 0, 0, tiled=True)
    other = swap(mine).reshape(rows, -1)
    conduct, pot, held = store(conduct, pot, mine.reshape(rows, -1))
    moments = store_other(other, held)
    return (conduct[None], pot[None], moments)


def solution(mesh):
    tiles = mesh.shape["tile"]
    split = jax.sharding.Mesh(
        mesh.devices.reshape(-1, pair, tiles), ("pairs", "member", "tile")
    )
    placed = (
        P(group, "tile", None, None),
        P(group, "tile", None, None),
        P(None, group, "tile", None, None),
        P("tile", None, None),
        P(),
        P(None, group),
        P(group),
    )
    return jax.shard_map(
        local,
        mesh=split,
        in_specs=placed,
        out_specs=(P(group, "tile", None, None), P(group, "tile", None, None), P("tile", None)),
        check_vma=False,
    )
```

```python
import functools

import jax
import jax.numpy as jnp
from jax import lax
from jax.experimental import pallas as pl
from jax.experimental.pallas import tpu as pltpu
from jax.sharding import PartitionSpec as P

prior_keep = 0.8
prior_fresh = 0.6
relax_weight = 0.8
pair = 2
group = ("pairs", "member")

SMEM = pl.BlockSpec(memory_space=pltpu.SMEM)
VMEM = pl.BlockSpec(memory_space=pltpu.VMEM)
ANY = pl.BlockSpec(memory_space=pl.ANY)


def in_smem(array):
    return pltpu.with_memory_space_constraint(array, pltpu.SMEM)


def in_vmem(array):
    return pltpu.with_memory_space_constraint(array, pltpu.VMEM)


def pack_kernel(
    rows, weight_ref, parents_ref, accept_ref, cond_ref, pot_ref, noise_ref, source_ref,
    weight_out, parents_out, accept_out, pieces_ref, noise_out, source_out, sems,
):
    pairs = [(weight_ref, weight_out), (parents_ref, parents_out), (accept_ref, accept_out)]
    for piece in range(pieces_ref.shape[0]):
        row = piece * rows
        field = cond_ref if row < cond_ref.shape[0] else pot_ref
        row %= cond_ref.shape[0]
        pairs.append((field.at[pl.ds(row, rows)], pieces_ref.at[piece, pl.ds(0, rows)]))
    pairs += [(noise_ref, noise_out), (source_ref, source_out)]
    copies = [
        pltpu.make_async_copy(here, there, sems.at[i]) for i, (here, there) in enumerate(pairs)
    ]
    for copy in copies:
        copy.start()
    for copy in copies:
        copy.wait()
    weight = jnp.full((8, pieces_ref.shape[2]), weight_out[0], jnp.float32)
    for piece in range(pieces_ref.shape[0]):
        pieces_ref[piece, rows:rows + 8] = weight


def pack(weights, parents, accept, log_cond, potential, noise, source, pairs):
    nz = source.shape[2]
    rows = 2 * log_cond.size // (pairs * nz)
    return pl.pallas_call(
        functools.partial(pack_kernel, rows),
        out_shape=(
            pltpu.SMEM(weights.shape, jnp.float32),
            pltpu.SMEM(parents.shape, jnp.int32),
            pltpu.SMEM(accept.shape, jnp.int32),
            pltpu.VMEM((pairs, rows + 8, nz), jnp.float32),
            pltpu.VMEM(noise.shape, jnp.float32),
            pltpu.VMEM(source.shape, jnp.float32),
        ),
        in_specs=[ANY] * 7,
        out_specs=(SMEM,) * 3 + (VMEM,) * 3,
        scratch_shapes=[pltpu.SemaphoreType.DMA((pairs + 5,))],
        name="pack",
    )(weights, parents, accept, log_cond.reshape(-1, nz), potential.reshape(-1, nz), noise, source)


def choose_kernel(parents_ref, weight_ref, mine_ref, other_ref, chosen_ref, root_ref):
    member = lax.axis_index("member")
    rows = chosen_ref.shape[1]
    for place in range(chosen_ref.shape[0]):
        parent = parents_ref[place * pair + member]
        here = lax.rem(parent, pair) == member
        at = lax.div(parent, pair)
        chosen_ref[place] = jnp.where(
            here, mine_ref[at, pl.ds(0, rows)], other_ref[at, pl.ds(0, rows)]
        )
    total = jnp.zeros_like(root_ref)
    for place in range(chosen_ref.shape[0]):
        total += mine_ref[place, rows:rows + 8] + other_ref[place, rows:rows + 8]
    root_ref[...] = jnp.sqrt(weight_ref[0] / total)


def choose(parents, weights, mine, other):
    pairs, rows, nz = mine.shape
    return pl.pallas_call(
        choose_kernel,
        out_shape=(
            pltpu.VMEM((pairs, rows - 8, nz), jnp.float32),
            pltpu.VMEM((8, nz), jnp.float32),
        ),
        in_specs=[SMEM, SMEM, VMEM, VMEM],
        out_specs=(VMEM, VMEM),
        name="choose",
    )(in_smem(parents), in_smem(weights), in_vmem(mine), in_vmem(other))


def shifts(here):
    ny, nz = here.shape
    return [pltpu.roll(here, by, axis) for by, axis in [(1, 0), (ny - 1, 0), (1, 1), (nz - 1, 1)]]


def outer(shape):
    row = lax.broadcasted_iota(jnp.int32, shape, 0)
    lane = lax.broadcasted_iota(jnp.int32, shape, 1)
    return [row == 0, row == shape[0] - 1, lane == 0, lane == shape[1] - 1]


def layout(moves):
    reach = 2 * moves
    depth = [reach] + [reach - 2 * m for m in range(moves)] + [reach - 1]
    return [sum(depth[:i]) for i in range(len(depth))], depth


def edges_kernel(accept_ref, moved_ref, noise_ref, source_ref, low_ref, high_ref):
    moves, width = noise_ref.shape[:2]
    at, depth = layout(moves)
    for out_ref, place in [(low_ref, lambda h, i: i), (high_ref, lambda h, i: width - h + i)]:
        for i in range(depth[0]):
            out_ref[at[0] + i] = moved_ref[1, place(depth[0], i)]
        for i in range(depth[-1]):
            out_ref[at[-1] + i] = source_ref[place(depth[-1], i)]
        conduct = {place(depth[1], i): moved_ref[0, place(depth[1], i)] for i in range(depth[1])}
        for m in range(moves):
            accepted = accept_ref[m] > 0
            for i in range(depth[1 + m]):
                layer = place(depth[1 + m], i)
                proposal = prior_keep * conduct[layer] + prior_fresh * noise_ref[m, layer]
                out_ref[at[1 + m] + i] = proposal
                conduct[layer] = jnp.where(accepted, proposal, conduct[layer])


def edges(accept, moved, noise, source):
    at, depth = layout(noise.shape[0])
    out = pltpu.VMEM((sum(depth),) + source.shape[1:], jnp.float32)
    return pl.pallas_call(
        edges_kernel,
        out_shape=(out, out),
        in_specs=[SMEM] + [VMEM] * 3,
        out_specs=(VMEM, VMEM),
        name="edges",
    )(in_smem(accept), *[in_vmem(field) for field in (moved, noise, source)])


def moves_kernel(
    accept_ref, root_ref, moved_ref, noise_ref, source_ref, low_ref, high_ref,
    cond_out, pot_out, traces_out, pot, once, conductivity, gain, faces,
):
    moves, width, ny, nz = noise_ref.shape
    reach = 2 * moves
    span = width + 2 * reach
    at, depth = layout(moves)
    tile = lax.axis_index("tile")
    first = tile == 0
    last = tile == lax.axis_size("tile") - 1

    def halo(number, i):
        if i < 0:
            return low_ref[at[number] + depth[number] + i]
        return high_ref[at[number] + i - width]

    def own(i):
        return 0 <= i < width

    def keep_inside(value, i):
        outside = (first & (i < reach)) | (last & (i >= reach + width))
        return jnp.where(outside, 0.0, value)

    def sweep(old, lo, hi):
        for i in range(lo, hi):
            here, here_k = old[i], conductivity[i]
            flux = (here_k + conductivity[i - 1]) * old[i - 1] + (
                here_k + conductivity[i + 1]
            ) * old[i + 1]
            for side, near in enumerate(shifts(here)):
                flux += faces[side, i] * near
            x = i - reach
            source = source_ref[x] if own(x) else halo(1 + moves, x)
            value = (1.0 - relax_weight) * here + (
                2.0 * source + flux
            ) * gain[i]
            yield i, keep_inside(value, i)

    for i in range(span):
        x = i - reach
        pot[i] = moved_ref[1, x] if own(x) else halo(0, x)
        if own(x):
            cond_out[x] = moved_ref[0, x]

    for m in range(moves):
        start = 2 * m
        accepted = accept_ref[m] > 0
        for i in range(start, span - start):
            x = i - reach
            if own(x):
                conduct = cond_out[x]
                proposal = prior_keep * conduct + prior_fresh * noise_ref[m, x]
                cond_out[x] = jnp.where(accepted, proposal, conduct)
            else:
                proposal = halo(1 + m, x)
            conductivity[i] = jnp.exp(proposal)
        for i in range(start + 1, span - start - 1):
            here_k = conductivity[i]
            total = 6.0 * here_k + conductivity[i - 1] + conductivity[i + 1]
            for side, (near, outside) in enumerate(zip(shifts(here_k), outer((ny, nz)))):
                total += jnp.where(outside, 1.0, near)
                faces[side, i] = jnp.where(outside, 0.0, here_k + near)
            gain[i] = relax_weight / total
        for i, value in sweep(pot, start + 1, span - start - 1):
            once[i] = value
        for i, value in sweep(once, start + 2, span - start - 2):
            pot[i] = jnp.where(accepted, value, pot[i])

    root = root_ref[0:1]
    for x in range(width):
        value = pot[x + reach]
        pot_out[x] = value
        traces_out[:, x * nz:(x + 1) * nz] = value * root


def run_moves(accept, root, *fields):
    moves, width, ny, nz = fields[1].shape
    span = width + 4 * moves
    return pl.pallas_call(
        moves_kernel,
        out_shape=(
            pltpu.VMEM((width, ny, nz), jnp.float32),
            pltpu.VMEM((width, ny, nz), jnp.float32),
            pltpu.VMEM((ny, width * nz), jnp.float32),
        ),
        in_specs=[SMEM] + [VMEM] * (1 + len(fields)),
        out_specs=(VMEM, VMEM, VMEM),
        scratch_shapes=[pltpu.VMEM((span, ny, nz), jnp.float32)] * 4
        + [pltpu.VMEM((4, span, ny, nz), jnp.float32)],
        name="moves",
    )(in_smem(accept), in_vmem(root), *[in_vmem(field) for field in fields])


def sum_parts_kernel(parts_ref, total_ref):
    total = parts_ref[0]
    for place in range(1, parts_ref.shape[0]):
        total += parts_ref[place]
    total_ref[...] = total


def sum_parts(parts):
    return pl.pallas_call(
        sum_parts_kernel,
        out_shape=pltpu.VMEM(parts.shape[1:], jnp.float32),
        in_specs=[VMEM],
        out_specs=VMEM,
        name="sum_parts",
    )(in_vmem(parts))


def own_rows(ref, rows, owner):
    return ref.at[pl.ds(pl.multiple_of(owner * rows, rows), rows)]


def store_kernel(cond_ref, pot_ref, half_ref, cond_out, pot_out, rows_out, sems):
    own = own_rows(rows_out, half_ref.shape[0], lax.axis_index("member"))
    pairs = [(cond_ref, cond_out), (pot_ref, pot_out), (half_ref, own)]
    copies = [
        pltpu.make_async_copy(here, there, sems.at[i]) for i, (here, there) in enumerate(pairs)
    ]
    for copy in copies:
        copy.start()
    for copy in copies:
        copy.wait()


def store(conduct, pot, half):
    return pl.pallas_call(
        store_kernel,
        out_shape=(
            jax.ShapeDtypeStruct(conduct.shape, jnp.float32),
            jax.ShapeDtypeStruct(pot.shape, jnp.float32),
            jax.ShapeDtypeStruct((pair * half.shape[0], half.shape[1]), jnp.float32),
        ),
        in_specs=[VMEM] * 3,
        out_specs=(ANY,) * 3,
        scratch_shapes=[pltpu.SemaphoreType.DMA((3,))],
        name="store",
    )(in_vmem(conduct), in_vmem(pot), in_vmem(half))


def store_other_kernel(half_ref, held_ref, rows_out, sem):
    other = own_rows(rows_out, half_ref.shape[0], 1 - lax.axis_index("member"))
    copy = pltpu.make_async_copy(half_ref, other, sem)
    copy.start()
    copy.wait()


def store_other(half, held):
    return pl.pallas_call(
        store_other_kernel,
        out_shape=jax.ShapeDtypeStruct(held.shape, jnp.float32),
        in_specs=[VMEM, ANY],
        out_specs=ANY,
        scratch_shapes=[pltpu.SemaphoreType.DMA],
        input_output_aliases={1: 0},
        name="store_other",
    )(in_vmem(half), held)


def exchange_halo(low_edge, high_edge):
    count = lax.axis_size("tile")
    forward = [(i, i + 1) for i in range(count - 1)]
    backward = [(target, source) for source, target in forward]
    low = lax.ppermute(high_edge, "tile", forward)
    high = lax.ppermute(low_edge, "tile", backward)
    return low, high


def swap(block):
    return lax.ppermute(block, "member", [(0, 1), (1, 0)])


def local(log_cond, potential, noise, source, parents, accept, weights):
    width, ny, nz = source.shape

    weights, parents, accept, pieces, noise, source = pack(
        weights, parents, accept[:, 0], log_cond, potential, noise[:, 0], source,
        lax.axis_size("pairs"),
    )
    pieces = lax.all_to_all(pieces, "pairs", 0, 0, tiled=True)
    chosen, root = choose(parents, weights, pieces, swap(pieces))
    moved = lax.all_to_all(chosen, "pairs", 0, 0, tiled=True).reshape(2, width, ny, nz)
    low, high = exchange_halo(*edges(accept, moved, noise, source))
    conduct, pot, traces = run_moves(accept, root, moved, noise, source, low, high)

    rows = traces.shape[1] // (lax.axis_size("tile") * pair)
    member = lax.axis_index("member")
    piece = lax.all_gather(traces, "tile", axis=0, tiled=True)

    def product(owner):
        columns = lax.dynamic_slice_in_dim(
            piece, (lax.axis_index("tile") * pair + owner) * rows, rows, 1
        )
        return lax.dot_general(
            columns,
            piece,
            (((0,), (0,)), ((), ())),
            precision=lax.Precision.HIGH,
            preferred_element_type=jnp.float32,
        ).reshape(lax.axis_size("pairs"), -1, piece.shape[1])

    got = swap(product(1 - member))
    parts = lax.all_to_all(product(member) + got, "pairs", 0, 0, tiled=True)
    mine = lax.all_gather(sum_parts(parts), "pairs", axis=0, tiled=True)
    other = swap(mine).reshape(rows, -1)
    conduct, pot, held = store(conduct, pot, mine.reshape(rows, -1))
    moments = store_other(other, held)
    return (conduct[None], pot[None], moments)


def solution(mesh):
    tiles = mesh.shape["tile"]
    split = jax.sharding.Mesh(
        mesh.devices.reshape(-1, pair, tiles), ("pairs", "member", "tile")
    )
    placed = (
        P(group, "tile", None, None),
        P(group, "tile", None, None),
        P(None, group, "tile", None, None),
        P("tile", None, None),
        P(),
        P(None, group),
        P(group),
    )
    return jax.shard_map(
        local,
        mesh=split,
        in_specs=placed,
        out_specs=(P(group, "tile", None, None), P(group, "tile", None, None), P("tile", None)),
        check_vma=False,
    )
```

```python
import functools

import jax
import jax.numpy as jnp
from jax import lax
from jax.experimental import pallas as pl
from jax.experimental.pallas import tpu as pltpu
from jax.sharding import PartitionSpec as P

prior_keep = 0.8
prior_fresh = 0.6
relax_weight = 0.8
pair = 2
group = ("pairs", "member")

SMEM = pl.BlockSpec(memory_space=pltpu.SMEM)
VMEM = pl.BlockSpec(memory_space=pltpu.VMEM)
ANY = pl.BlockSpec(memory_space=pl.ANY)


def in_smem(array):
    return pltpu.with_memory_space_constraint(array, pltpu.SMEM)


def in_vmem(array):
    return pltpu.with_memory_space_constraint(array, pltpu.VMEM)


def pack_kernel(
    rows, weight_ref, parents_ref, accept_ref, cond_ref, pot_ref, noise_ref, source_ref,
    weight_out, parents_out, accept_out, pieces_ref, noise_out, source_out, sems,
):
    pairs = [(weight_ref, weight_out), (parents_ref, parents_out), (accept_ref, accept_out)]
    half = rows // 2
    for i, field in enumerate([cond_ref, pot_ref]):
        pairs.append((field, pieces_ref.at[0, pl.ds(i * half, half)]))
    pairs += [(noise_ref, noise_out), (source_ref, source_out)]
    copies = [
        pltpu.make_async_copy(here, there, sems.at[i]) for i, (here, there) in enumerate(pairs)
    ]
    for copy in copies:
        copy.start()
    for copy in copies:
        copy.wait()
    weight = jnp.full((8, pieces_ref.shape[2]), weight_out[0], jnp.float32)
    for piece in range(pieces_ref.shape[0]):
        pieces_ref[piece, rows:rows + 8] = weight


def pack(weights, parents, accept, log_cond, potential, noise, source, pairs):
    nz = source.shape[2]
    rows = 2 * log_cond.size // (pairs * nz)
    return pl.pallas_call(
        functools.partial(pack_kernel, rows),
        out_shape=(
            pltpu.SMEM(weights.shape, jnp.float32),
            pltpu.SMEM(parents.shape, jnp.int32),
            pltpu.SMEM(accept.shape, jnp.int32),
            pltpu.VMEM((pairs, rows + 8, nz), jnp.float32),
            pltpu.VMEM(noise.shape, jnp.float32),
            pltpu.VMEM(source.shape, jnp.float32),
        ),
        in_specs=[ANY] * 7,
        out_specs=(SMEM,) * 3 + (VMEM,) * 3,
        scratch_shapes=[pltpu.SemaphoreType.DMA((7,))],
        name="pack",
    )(weights, parents, accept, log_cond.reshape(-1, nz), potential.reshape(-1, nz), noise, source)


def pick_kernel(parents_ref, held_ref, keep_ref, give_ref):
    pairs, rows, _ = held_ref.shape
    rows -= 8
    member = lax.axis_index("member")
    first = lax.axis_index("pairs") * pair
    total = held_ref[0, rows:rows + 8]
    for place in range(1, pairs):
        total += held_ref[place, rows:rows + 8]
    for out_ref, device in [(keep_ref, first + member), (give_ref, first + 1 - member)]:
        out_ref[0:rows] = held_ref[lax.div(parents_ref[device], pair), 0:rows]
        out_ref[rows:rows + 8] = total


def pick(parents, held):
    out = pltpu.VMEM(held.shape[1:], jnp.float32)
    return pl.pallas_call(
        pick_kernel,
        out_shape=(out, out),
        in_specs=[SMEM, VMEM],
        out_specs=(VMEM, VMEM),
        name="pick",
    )(in_smem(parents), in_vmem(held))


def settle_kernel(parents_ref, weight_ref, keep_ref, got_ref, moved_ref, root_ref):
    member = lax.axis_index("member")
    parent = parents_ref[lax.axis_index("pairs") * pair + member]
    here = lax.rem(parent, pair) == member
    rows = moved_ref.shape[0]
    moved_ref[...] = jnp.where(here, keep_ref[0:rows], got_ref[0:rows])
    root_ref[...] = jnp.sqrt(
        weight_ref[0] / (keep_ref[rows:rows + 8] + got_ref[rows:rows + 8])
    )


def settle(parents, weights, keep, got):
    rows, nz = keep.shape
    return pl.pallas_call(
        settle_kernel,
        out_shape=(
            pltpu.VMEM((rows - 8, nz), jnp.float32),
            pltpu.VMEM((8, nz), jnp.float32),
        ),
        in_specs=[SMEM, SMEM, VMEM, VMEM],
        out_specs=(VMEM, VMEM),
        name="settle",
    )(in_smem(parents), in_smem(weights), in_vmem(keep), in_vmem(got))


def shifts(here):
    ny, nz = here.shape
    return [pltpu.roll(here, by, axis) for by, axis in [(1, 0), (ny - 1, 0), (1, 1), (nz - 1, 1)]]


def outer(shape):
    row = lax.broadcasted_iota(jnp.int32, shape, 0)
    lane = lax.broadcasted_iota(jnp.int32, shape, 1)
    return [row == 0, row == shape[0] - 1, lane == 0, lane == shape[1] - 1]


def layout(moves):
    reach = 2 * moves
    depth = [reach] + [reach - 2 * m for m in range(moves)] + [reach - 1]
    return [sum(depth[:i]) for i in range(len(depth))], depth


def edges_kernel(accept_ref, moved_ref, noise_ref, source_ref, low_ref, high_ref):
    moves, width = noise_ref.shape[:2]
    at, depth = layout(moves)
    for out_ref, place in [(low_ref, lambda h, i: i), (high_ref, lambda h, i: width - h + i)]:
        for i in range(depth[0]):
            out_ref[at[0] + i] = moved_ref[1, place(depth[0], i)]
        for i in range(depth[-1]):
            out_ref[at[-1] + i] = source_ref[place(depth[-1], i)]
        conduct = {place(depth[1], i): moved_ref[0, place(depth[1], i)] for i in range(depth[1])}
        for m in range(moves):
            accepted = accept_ref[m] > 0
            for i in range(depth[1 + m]):
                layer = place(depth[1 + m], i)
                proposal = prior_keep * conduct[layer] + prior_fresh * noise_ref[m, layer]
                out_ref[at[1 + m] + i] = proposal
                conduct[layer] = jnp.where(accepted, proposal, conduct[layer])


def edges(accept, moved, noise, source):
    at, depth = layout(noise.shape[0])
    out = pltpu.VMEM((sum(depth),) + source.shape[1:], jnp.float32)
    return pl.pallas_call(
        edges_kernel,
        out_shape=(out, out),
        in_specs=[SMEM] + [VMEM] * 3,
        out_specs=(VMEM, VMEM),
        name="edges",
    )(in_smem(accept), *[in_vmem(field) for field in (moved, noise, source)])


def moves_kernel(
    accept_ref, root_ref, moved_ref, noise_ref, source_ref, low_ref, high_ref,
    cond_out, pot_out, traces_out, pot, once, conductivity, gain, faces,
):
    moves, width, ny, nz = noise_ref.shape
    reach = 2 * moves
    span = width + 2 * reach
    at, depth = layout(moves)
    tile = lax.axis_index("tile")
    first = tile == 0
    last = tile == lax.axis_size("tile") - 1

    def halo(number, i):
        if i < 0:
            return low_ref[at[number] + depth[number] + i]
        return high_ref[at[number] + i - width]

    def own(i):
        return 0 <= i < width

    def keep_inside(value, i):
        outside = (first & (i < reach)) | (last & (i >= reach + width))
        return jnp.where(outside, 0.0, value)

    def sweep(old, lo, hi):
        for i in range(lo, hi):
            here, here_k = old[i], conductivity[i]
            flux = (here_k + conductivity[i - 1]) * old[i - 1] + (
                here_k + conductivity[i + 1]
            ) * old[i + 1]
            for side, near in enumerate(shifts(here)):
                flux += faces[side, i] * near
            x = i - reach
            source = source_ref[x] if own(x) else halo(1 + moves, x)
            value = (1.0 - relax_weight) * here + (
                2.0 * source + flux
            ) * gain[i]
            yield i, keep_inside(value, i)

    for i in range(span):
        x = i - reach
        pot[i] = moved_ref[1, x] if own(x) else halo(0, x)
        if own(x):
            cond_out[x] = moved_ref[0, x]

    for m in range(moves):
        start = 2 * m
        accepted = accept_ref[m] > 0
        for i in range(start, span - start):
            x = i - reach
            if own(x):
                conduct = cond_out[x]
                proposal = prior_keep * conduct + prior_fresh * noise_ref[m, x]
                cond_out[x] = jnp.where(accepted, proposal, conduct)
            else:
                proposal = halo(1 + m, x)
            conductivity[i] = jnp.exp(proposal)
        for i in range(start + 1, span - start - 1):
            here_k = conductivity[i]
            total = 6.0 * here_k + conductivity[i - 1] + conductivity[i + 1]
            for side, (near, outside) in enumerate(zip(shifts(here_k), outer((ny, nz)))):
                total += jnp.where(outside, 1.0, near)
                faces[side, i] = jnp.where(outside, 0.0, here_k + near)
            gain[i] = relax_weight / total
        for i, value in sweep(pot, start + 1, span - start - 1):
            once[i] = value
        for i, value in sweep(once, start + 2, span - start - 2):
            pot[i] = jnp.where(accepted, value, pot[i])

    root = root_ref[0:1]
    for x in range(width):
        value = pot[x + reach]
        pot_out[x] = value
        traces_out[:, x * nz:(x + 1) * nz] = value * root


def run_moves(accept, root, *fields):
    moves, width, ny, nz = fields[1].shape
    span = width + 4 * moves
    return pl.pallas_call(
        moves_kernel,
        out_shape=(
            pltpu.VMEM((width, ny, nz), jnp.float32),
            pltpu.VMEM((width, ny, nz), jnp.float32),
            pltpu.VMEM((ny, width * nz), jnp.float32),
        ),
        in_specs=[SMEM] + [VMEM] * (1 + len(fields)),
        out_specs=(VMEM, VMEM, VMEM),
        scratch_shapes=[pltpu.VMEM((span, ny, nz), jnp.float32)] * 4
        + [pltpu.VMEM((4, span, ny, nz), jnp.float32)],
        name="moves",
    )(in_smem(accept), in_vmem(root), *[in_vmem(field) for field in fields])


def sum_parts_kernel(parts_ref, total_ref):
    total = parts_ref[0]
    for place in range(1, parts_ref.shape[0]):
        total += parts_ref[place]
    total_ref[...] = total


def sum_parts(parts):
    return pl.pallas_call(
        sum_parts_kernel,
        out_shape=pltpu.VMEM(parts.shape[1:], jnp.float32),
        in_specs=[VMEM],
        out_specs=VMEM,
        name="sum_parts",
    )(in_vmem(parts))


def own_rows(ref, rows, owner):
    return ref.at[pl.ds(pl.multiple_of(owner * rows, rows), rows)]


def store_kernel(cond_ref, pot_ref, half_ref, cond_out, pot_out, rows_out, sems):
    own = own_rows(rows_out, half_ref.shape[0], lax.axis_index("member"))
    pairs = [(cond_ref, cond_out), (pot_ref, pot_out), (half_ref, own)]
    copies = [
        pltpu.make_async_copy(here, there, sems.at[i]) for i, (here, there) in enumerate(pairs)
    ]
    for copy in copies:
        copy.start()
    for copy in copies:
        copy.wait()


def store(conduct, pot, half):
    return pl.pallas_call(
        store_kernel,
        out_shape=(
            jax.ShapeDtypeStruct(conduct.shape, jnp.float32),
            jax.ShapeDtypeStruct(pot.shape, jnp.float32),
            jax.ShapeDtypeStruct((pair * half.shape[0], half.shape[1]), jnp.float32),
        ),
        in_specs=[VMEM] * 3,
        out_specs=(ANY,) * 3,
        scratch_shapes=[pltpu.SemaphoreType.DMA((3,))],
        name="store",
    )(in_vmem(conduct), in_vmem(pot), in_vmem(half))


def store_other_kernel(half_ref, held_ref, rows_out, sem):
    other = own_rows(rows_out, half_ref.shape[0], 1 - lax.axis_index("member"))
    copy = pltpu.make_async_copy(half_ref, other, sem)
    copy.start()
    copy.wait()


def store_other(half, held):
    return pl.pallas_call(
        store_other_kernel,
        out_shape=jax.ShapeDtypeStruct(held.shape, jnp.float32),
        in_specs=[VMEM, ANY],
        out_specs=ANY,
        scratch_shapes=[pltpu.SemaphoreType.DMA],
        input_output_aliases={1: 0},
        name="store_other",
    )(in_vmem(half), held)


def exchange_halo(low_edge, high_edge):
    count = lax.axis_size("tile")
    forward = [(i, i + 1) for i in range(count - 1)]
    backward = [(target, source) for source, target in forward]
    low = lax.ppermute(high_edge, "tile", forward)
    high = lax.ppermute(low_edge, "tile", backward)
    return low, high


def swap(block):
    return lax.ppermute(block, "member", [(0, 1), (1, 0)])


def local(log_cond, potential, noise, source, parents, accept, weights):
    width, ny, nz = source.shape

    weights, parents, accept, bundle, noise, source = pack(
        weights, parents, accept[:, 0], log_cond, potential, noise[:, 0], source, 1
    )
    held = lax.all_gather(bundle, "pairs", axis=0, tiled=True)
    keep, give = pick(parents, held)
    moved, root = settle(parents, weights, keep, swap(give))
    moved = moved.reshape(2, width, ny, nz)
    low, high = exchange_halo(*edges(accept, moved, noise, source))
    conduct, pot, traces = run_moves(accept, root, moved, noise, source, low, high)

    rows = traces.shape[1] // (lax.axis_size("tile") * pair)
    member = lax.axis_index("member")
    piece = lax.all_gather(traces, "tile", axis=0, tiled=True)

    def product(owner):
        columns = lax.dynamic_slice_in_dim(
            piece, (lax.axis_index("tile") * pair + owner) * rows, rows, 1
        )
        return lax.dot_general(
            columns,
            piece,
            (((0,), (0,)), ((), ())),
            precision=lax.Precision.HIGH,
            preferred_element_type=jnp.float32,
        ).reshape(lax.axis_size("pairs"), -1, piece.shape[1])

    got = swap(product(1 - member))
    parts = lax.all_to_all(product(member) + got, "pairs", 0, 0, tiled=True)
    mine = lax.all_gather(sum_parts(parts), "pairs", axis=0, tiled=True)
    other = swap(mine).reshape(rows, -1)
    conduct, pot, held = store(conduct, pot, mine.reshape(rows, -1))
    moments = store_other(other, held)
    return (conduct[None], pot[None], moments)


def solution(mesh):
    tiles = mesh.shape["tile"]
    split = jax.sharding.Mesh(
        mesh.devices.reshape(-1, pair, tiles), ("pairs", "member", "tile")
    )
    placed = (
        P(group, "tile", None, None),
        P(group, "tile", None, None),
        P(None, group, "tile", None, None),
        P("tile", None, None),
        P(),
        P(None, group),
        P(group),
    )
    return jax.shard_map(
        local,
        mesh=split,
        in_specs=placed,
        out_specs=(P(group, "tile", None, None), P(group, "tile", None, None), P("tile", None)),
        check_vma=False,
    )
```

```python
import functools

import jax
import jax.numpy as jnp
from jax import lax
from jax.experimental import pallas as pl
from jax.experimental.pallas import tpu as pltpu
from jax.sharding import PartitionSpec as P

prior_keep = 0.8
prior_fresh = 0.6
relax_weight = 0.8
pair = 2
group = ("pairs", "member")

SMEM = pl.BlockSpec(memory_space=pltpu.SMEM)
VMEM = pl.BlockSpec(memory_space=pltpu.VMEM)
ANY = pl.BlockSpec(memory_space=pl.ANY)


def in_smem(array):
    return pltpu.with_memory_space_constraint(array, pltpu.SMEM)


def in_vmem(array):
    return pltpu.with_memory_space_constraint(array, pltpu.VMEM)


def pack_kernel(
    rows, weight_ref, parents_ref, accept_ref, cond_ref, pot_ref, noise_ref, source_ref,
    weight_out, parents_out, accept_out, pieces_ref, noise_out, source_out, sems,
):
    pairs = [(weight_ref, weight_out), (parents_ref, parents_out), (accept_ref, accept_out)]
    for piece in range(pieces_ref.shape[0]):
        row = piece * rows
        field = cond_ref if row < cond_ref.shape[0] else pot_ref
        row %= cond_ref.shape[0]
        pairs.append((field.at[pl.ds(row, rows)], pieces_ref.at[piece, pl.ds(0, rows)]))
    pairs += [(noise_ref, noise_out), (source_ref, source_out)]
    copies = [
        pltpu.make_async_copy(here, there, sems.at[i]) for i, (here, there) in enumerate(pairs)
    ]
    for copy in copies:
        copy.start()
    for copy in copies:
        copy.wait()
    weight = jnp.full((8, pieces_ref.shape[2]), weight_out[0], jnp.float32)
    for piece in range(pieces_ref.shape[0]):
        pieces_ref[piece, rows:rows + 8] = weight


def pack(weights, parents, accept, log_cond, potential, noise, source, pairs):
    nz = source.shape[2]
    rows = 2 * log_cond.size // (pairs * nz)
    return pl.pallas_call(
        functools.partial(pack_kernel, rows),
        out_shape=(
            pltpu.SMEM(weights.shape, jnp.float32),
            pltpu.SMEM(parents.shape, jnp.int32),
            pltpu.SMEM(accept.shape, jnp.int32),
            pltpu.VMEM((pairs, rows + 8, nz), jnp.float32),
            pltpu.VMEM(noise.shape, jnp.float32),
            pltpu.VMEM(source.shape, jnp.float32),
        ),
        in_specs=[ANY] * 7,
        out_specs=(SMEM,) * 3 + (VMEM,) * 3,
        scratch_shapes=[pltpu.SemaphoreType.DMA((pairs + 5,))],
        name="pack",
    )(weights, parents, accept, log_cond.reshape(-1, nz), potential.reshape(-1, nz), noise, source)


def choose_kernel(parents_ref, weight_ref, mine_ref, other_ref, chosen_ref, root_ref):
    member = lax.axis_index("member")
    rows = chosen_ref.shape[1]
    for place in range(chosen_ref.shape[0]):
        parent = parents_ref[place * pair + member]
        here = lax.rem(parent, pair) == member
        at = lax.div(parent, pair)
        chosen_ref[place] = jnp.where(
            here, mine_ref[at, pl.ds(0, rows)], other_ref[at, pl.ds(0, rows)]
        )
    total = jnp.zeros_like(root_ref)
    for place in range(chosen_ref.shape[0]):
        total += mine_ref[place, rows:rows + 8] + other_ref[place, rows:rows + 8]
    root_ref[...] = jnp.sqrt(weight_ref[0] / total)


def choose(parents, weights, mine, other):
    pairs, rows, nz = mine.shape
    return pl.pallas_call(
        choose_kernel,
        out_shape=(
            pltpu.VMEM((pairs, rows - 8, nz), jnp.float32),
            pltpu.VMEM((8, nz), jnp.float32),
        ),
        in_specs=[SMEM, SMEM, VMEM, VMEM],
        out_specs=(VMEM, VMEM),
        name="choose",
    )(in_smem(parents), in_smem(weights), in_vmem(mine), in_vmem(other))


def shifts(here):
    ny, nz = here.shape
    return [pltpu.roll(here, by, axis) for by, axis in [(1, 0), (ny - 1, 0), (1, 1), (nz - 1, 1)]]


def outer(shape):
    row = lax.broadcasted_iota(jnp.int32, shape, 0)
    lane = lax.broadcasted_iota(jnp.int32, shape, 1)
    return [row == 0, row == shape[0] - 1, lane == 0, lane == shape[1] - 1]


def layout(moves):
    reach = 2 * moves
    depth = [reach] + [reach - 2 * m for m in range(moves)] + [reach - 1]
    return [sum(depth[:i]) for i in range(len(depth))], depth


def edges_kernel(accept_ref, moved_ref, noise_ref, source_ref, low_ref, high_ref):
    moves, width = noise_ref.shape[:2]
    at, depth = layout(moves)
    for out_ref, place in [(low_ref, lambda h, i: i), (high_ref, lambda h, i: width - h + i)]:
        for i in range(depth[0]):
            out_ref[at[0] + i] = moved_ref[1, place(depth[0], i)]
        for i in range(depth[-1]):
            out_ref[at[-1] + i] = source_ref[place(depth[-1], i)]
        conduct = {place(depth[1], i): moved_ref[0, place(depth[1], i)] for i in range(depth[1])}
        for m in range(moves):
            accepted = accept_ref[m] > 0
            for i in range(depth[1 + m]):
                layer = place(depth[1 + m], i)
                proposal = prior_keep * conduct[layer] + prior_fresh * noise_ref[m, layer]
                out_ref[at[1 + m] + i] = proposal
                conduct[layer] = jnp.where(accepted, proposal, conduct[layer])


def edges(accept, moved, noise, source):
    at, depth = layout(noise.shape[0])
    out = pltpu.VMEM((sum(depth),) + source.shape[1:], jnp.float32)
    return pl.pallas_call(
        edges_kernel,
        out_shape=(out, out),
        in_specs=[SMEM] + [VMEM] * 3,
        out_specs=(VMEM, VMEM),
        name="edges",
    )(in_smem(accept), *[in_vmem(field) for field in (moved, noise, source)])


def moves_kernel(
    accept_ref, root_ref, moved_ref, noise_ref, source_ref, low_ref, high_ref,
    cond_out, pot_out, traces_out, pot, once, conductivity, gain, faces,
):
    moves, width, ny, nz = noise_ref.shape
    reach = 2 * moves
    span = width + 2 * reach
    at, depth = layout(moves)
    tile = lax.axis_index("tile")
    first = tile == 0
    last = tile == lax.axis_size("tile") - 1

    def halo(number, i):
        if i < 0:
            return low_ref[at[number] + depth[number] + i]
        return high_ref[at[number] + i - width]

    def own(i):
        return 0 <= i < width

    def keep_inside(value, i):
        outside = (first & (i < reach)) | (last & (i >= reach + width))
        return jnp.where(outside, 0.0, value)

    def sweep(old, lo, hi):
        for i in range(lo, hi):
            here, here_k = old[i], conductivity[i]
            flux = (here_k + conductivity[i - 1]) * old[i - 1] + (
                here_k + conductivity[i + 1]
            ) * old[i + 1]
            for side, near in enumerate(shifts(here)):
                flux += faces[side, i] * near
            x = i - reach
            source = source_ref[x] if own(x) else halo(1 + moves, x)
            value = (1.0 - relax_weight) * here + (
                2.0 * source + flux
            ) * gain[i]
            yield i, keep_inside(value, i)

    for i in range(span):
        x = i - reach
        pot[i] = moved_ref[1, x] if own(x) else halo(0, x)
        if own(x):
            cond_out[x] = moved_ref[0, x]

    for m in range(moves):
        start = 2 * m
        accepted = accept_ref[m] > 0
        for i in range(start, span - start):
            x = i - reach
            if own(x):
                conduct = cond_out[x]
                proposal = prior_keep * conduct + prior_fresh * noise_ref[m, x]
                cond_out[x] = jnp.where(accepted, proposal, conduct)
            else:
                proposal = halo(1 + m, x)
            conductivity[i] = jnp.exp(proposal)
        for i in range(start + 1, span - start - 1):
            here_k = conductivity[i]
            total = 6.0 * here_k + conductivity[i - 1] + conductivity[i + 1]
            for side, (near, outside) in enumerate(zip(shifts(here_k), outer((ny, nz)))):
                total += jnp.where(outside, 1.0, near)
                faces[side, i] = jnp.where(outside, 0.0, here_k + near)
            gain[i] = relax_weight / total
        for i, value in sweep(pot, start + 1, span - start - 1):
            once[i] = value
        for i, value in sweep(once, start + 2, span - start - 2):
            pot[i] = jnp.where(accepted, value, pot[i])

    root = root_ref[0:1]
    for x in range(width):
        value = pot[x + reach]
        pot_out[x] = value
        traces_out[:, x * nz:(x + 1) * nz] = value * root


def run_moves(accept, root, *fields):
    moves, width, ny, nz = fields[1].shape
    span = width + 4 * moves
    return pl.pallas_call(
        moves_kernel,
        out_shape=(
            pltpu.VMEM((width, ny, nz), jnp.float32),
            pltpu.VMEM((width, ny, nz), jnp.float32),
            pltpu.VMEM((ny, width * nz), jnp.float32),
        ),
        in_specs=[SMEM] + [VMEM] * (1 + len(fields)),
        out_specs=(VMEM, VMEM, VMEM),
        scratch_shapes=[pltpu.VMEM((span, ny, nz), jnp.float32)] * 4
        + [pltpu.VMEM((4, span, ny, nz), jnp.float32)],
        name="moves",
    )(in_smem(accept), in_vmem(root), *[in_vmem(field) for field in fields])


def sum_parts_kernel(parts_ref, total_ref):
    total = parts_ref[0]
    for place in range(1, parts_ref.shape[0]):
        total += parts_ref[place]
    total_ref[...] = total


def sum_parts(parts):
    return pl.pallas_call(
        sum_parts_kernel,
        out_shape=pltpu.VMEM(parts.shape[1:], jnp.float32),
        in_specs=[VMEM],
        out_specs=VMEM,
        name="sum_parts",
    )(in_vmem(parts))


def own_rows(ref, rows, owner):
    return ref.at[pl.ds(pl.multiple_of(owner * rows, rows), rows)]


def store_kernel(cond_ref, pot_ref, half_ref, cond_out, pot_out, rows_out, sems):
    own = own_rows(rows_out, half_ref.shape[0], lax.axis_index("member"))
    pairs = [(cond_ref, cond_out), (pot_ref, pot_out), (half_ref, own)]
    copies = [
        pltpu.make_async_copy(here, there, sems.at[i]) for i, (here, there) in enumerate(pairs)
    ]
    for copy in copies:
        copy.start()
    for copy in copies:
        copy.wait()


def store(conduct, pot, half):
    return pl.pallas_call(
        store_kernel,
        out_shape=(
            jax.ShapeDtypeStruct(conduct.shape, jnp.float32),
            jax.ShapeDtypeStruct(pot.shape, jnp.float32),
            jax.ShapeDtypeStruct((pair * half.shape[0], half.shape[1]), jnp.float32),
        ),
        in_specs=[VMEM] * 3,
        out_specs=(ANY,) * 3,
        scratch_shapes=[pltpu.SemaphoreType.DMA((3,))],
        name="store",
    )(in_vmem(conduct), in_vmem(pot), in_vmem(half))


def store_other_kernel(at, part_ref, held_ref, rows_out, sem):
    other = own_rows(rows_out, rows_out.shape[0] // pair, 1 - lax.axis_index("member"))
    copy = pltpu.make_async_copy(part_ref, other.at[pl.ds(at, part_ref.shape[0])], sem)
    copy.start()
    copy.wait()


def store_other(part, held, at):
    return pl.pallas_call(
        functools.partial(store_other_kernel, at),
        out_shape=jax.ShapeDtypeStruct(held.shape, jnp.float32),
        in_specs=[VMEM, ANY],
        out_specs=ANY,
        scratch_shapes=[pltpu.SemaphoreType.DMA],
        input_output_aliases={1: 0},
        name="store_other",
    )(in_vmem(part), held)


def exchange_halo(low_edge, high_edge):
    count = lax.axis_size("tile")
    forward = [(i, i + 1) for i in range(count - 1)]
    backward = [(target, source) for source, target in forward]
    low = lax.ppermute(high_edge, "tile", forward)
    high = lax.ppermute(low_edge, "tile", backward)
    return low, high


def swap(block):
    return lax.ppermute(block, "member", [(0, 1), (1, 0)])


def local(log_cond, potential, noise, source, parents, accept, weights):
    width, ny, nz = source.shape

    weights, parents, accept, pieces, noise, source = pack(
        weights, parents, accept[:, 0], log_cond, potential, noise[:, 0], source,
        lax.axis_size("pairs"),
    )
    pieces = lax.all_to_all(pieces, "pairs", 0, 0, tiled=True)
    chosen, root = choose(parents, weights, pieces, swap(pieces))
    moved = lax.all_to_all(chosen, "pairs", 0, 0, tiled=True).reshape(2, width, ny, nz)
    low, high = exchange_halo(*edges(accept, moved, noise, source))
    conduct, pot, traces = run_moves(accept, root, moved, noise, source, low, high)

    rows = traces.shape[1] // (lax.axis_size("tile") * pair)
    member = lax.axis_index("member")
    piece = lax.all_gather(traces, "tile", axis=0, tiled=True)

    def product(owner):
        columns = lax.dynamic_slice_in_dim(
            piece, (lax.axis_index("tile") * pair + owner) * rows, rows, 1
        )
        return lax.dot_general(
            columns,
            piece,
            (((0,), (0,)), ((), ())),
            precision=lax.Precision.HIGH,
            preferred_element_type=jnp.float32,
        ).reshape(lax.axis_size("pairs"), -1, piece.shape[1])

    got = swap(product(1 - member))
    parts = lax.all_to_all(product(member) + got, "pairs", 0, 0, tiled=True)
    mine = lax.all_gather(sum_parts(parts), "pairs", axis=0, tiled=True)
    half = rows // 2
    others = [swap(mine.reshape(rows, -1)[at:at + half]) for at in (0, half)]
    conduct, pot, moments = store(conduct, pot, mine.reshape(rows, -1))
    for at, other in zip((0, half), others):
        moments = store_other(other, moments, at)
    return (conduct[None], pot[None], moments)


def solution(mesh):
    tiles = mesh.shape["tile"]
    split = jax.sharding.Mesh(
        mesh.devices.reshape(-1, pair, tiles), ("pairs", "member", "tile")
    )
    placed = (
        P(group, "tile", None, None),
        P(group, "tile", None, None),
        P(None, group, "tile", None, None),
        P("tile", None, None),
        P(),
        P(None, group),
        P(group),
    )
    return jax.shard_map(
        local,
        mesh=split,
        in_specs=placed,
        out_specs=(P(group, "tile", None, None), P(group, "tile", None, None), P("tile", None)),
        check_vma=False,
    )
```

```python
import functools

import jax
import jax.numpy as jnp
from jax import lax
from jax.experimental import pallas as pl
from jax.experimental.pallas import tpu as pltpu
from jax.sharding import PartitionSpec as P

prior_keep = 0.8
prior_fresh = 0.6
relax_weight = 0.8
pair = 2
group = ("pairs", "member")

SMEM = pl.BlockSpec(memory_space=pltpu.SMEM)
VMEM = pl.BlockSpec(memory_space=pltpu.VMEM)
ANY = pl.BlockSpec(memory_space=pl.ANY)


def in_smem(array):
    return pltpu.with_memory_space_constraint(array, pltpu.SMEM)


def in_vmem(array):
    return pltpu.with_memory_space_constraint(array, pltpu.VMEM)


def pack_kernel(
    rows, weight_ref, parents_ref, accept_ref, cond_ref, pot_ref, noise_ref, source_ref,
    weight_out, parents_out, accept_out, pieces_ref, noise_out, source_out, sems,
):
    pairs = [(weight_ref, weight_out), (parents_ref, parents_out), (accept_ref, accept_out)]
    for piece in range(pieces_ref.shape[0]):
        row = piece * rows
        field = cond_ref if row < cond_ref.shape[0] else pot_ref
        row %= cond_ref.shape[0]
        pairs.append((field.at[pl.ds(row, rows)], pieces_ref.at[piece, pl.ds(0, rows)]))
    pairs += [(noise_ref, noise_out), (source_ref, source_out)]
    copies = [
        pltpu.make_async_copy(here, there, sems.at[i]) for i, (here, there) in enumerate(pairs)
    ]
    for copy in copies:
        copy.start()
    for copy in copies:
        copy.wait()
    weight = jnp.full((8, pieces_ref.shape[2]), weight_out[0], jnp.float32)
    for piece in range(pieces_ref.shape[0]):
        pieces_ref[piece, rows:rows + 8] = weight


def pack(weights, parents, accept, log_cond, potential, noise, source, pairs):
    nz = source.shape[2]
    rows = 2 * log_cond.size // (pairs * nz)
    return pl.pallas_call(
        functools.partial(pack_kernel, rows),
        out_shape=(
            pltpu.SMEM(weights.shape, jnp.float32),
            pltpu.SMEM(parents.shape, jnp.int32),
            pltpu.SMEM(accept.shape, jnp.int32),
            pltpu.VMEM((pairs, rows + 8, nz), jnp.float32),
            pltpu.VMEM(noise.shape, jnp.float32),
            pltpu.VMEM(source.shape, jnp.float32),
        ),
        in_specs=[ANY] * 7,
        out_specs=(SMEM,) * 3 + (VMEM,) * 3,
        scratch_shapes=[pltpu.SemaphoreType.DMA((pairs + 5,))],
        name="pack",
    )(weights, parents, accept, log_cond.reshape(-1, nz), potential.reshape(-1, nz), noise, source)


def choose_kernel(parents_ref, weight_ref, mine_ref, other_ref, chosen_ref, root_ref):
    member = lax.axis_index("member")
    rows = chosen_ref.shape[1]
    for place in range(chosen_ref.shape[0]):
        parent = parents_ref[place * pair + member]
        here = lax.rem(parent, pair) == member
        at = lax.div(parent, pair)
        chosen_ref[place] = jnp.where(
            here, mine_ref[at, pl.ds(0, rows)], other_ref[at, pl.ds(0, rows)]
        )
    total = jnp.zeros_like(root_ref)
    for place in range(chosen_ref.shape[0]):
        total += mine_ref[place, rows:rows + 8] + other_ref[place, rows:rows + 8]
    root_ref[...] = jnp.sqrt(weight_ref[0] / total)


def choose(parents, weights, mine, other):
    pairs, rows, nz = mine.shape
    return pl.pallas_call(
        choose_kernel,
        out_shape=(
            pltpu.VMEM((pairs, rows - 8, nz), jnp.float32),
            pltpu.VMEM((8, nz), jnp.float32),
        ),
        in_specs=[SMEM, SMEM, VMEM, VMEM],
        out_specs=(VMEM, VMEM),
        name="choose",
    )(in_smem(parents), in_smem(weights), in_vmem(mine), in_vmem(other))


def shifts(here):
    ny, nz = here.shape
    return [pltpu.roll(here, by, axis) for by, axis in [(1, 0), (ny - 1, 0), (1, 1), (nz - 1, 1)]]


def outer(shape):
    row = lax.broadcasted_iota(jnp.int32, shape, 0)
    lane = lax.broadcasted_iota(jnp.int32, shape, 1)
    return [row == 0, row == shape[0] - 1, lane == 0, lane == shape[1] - 1]


def layout(moves):
    reach = 2 * moves
    depth = [reach] + [reach - 2 * m for m in range(moves)] + [reach - 1]
    return [sum(depth[:i]) for i in range(len(depth))], depth


def edges_kernel(accept_ref, moved_ref, noise_ref, source_ref, low_ref, high_ref):
    moves, width = noise_ref.shape[:2]
    at, depth = layout(moves)
    for out_ref, place in [(low_ref, lambda h, i: i), (high_ref, lambda h, i: width - h + i)]:
        for i in range(depth[0]):
            out_ref[at[0] + i] = moved_ref[1, place(depth[0], i)]
        for i in range(depth[-1]):
            out_ref[at[-1] + i] = source_ref[place(depth[-1], i)]
        conduct = {place(depth[1], i): moved_ref[0, place(depth[1], i)] for i in range(depth[1])}
        for m in range(moves):
            accepted = accept_ref[m] > 0
            for i in range(depth[1 + m]):
                layer = place(depth[1 + m], i)
                proposal = prior_keep * conduct[layer] + prior_fresh * noise_ref[m, layer]
                out_ref[at[1 + m] + i] = proposal
                conduct[layer] = jnp.where(accepted, proposal, conduct[layer])


def edges(accept, moved, noise, source):
    at, depth = layout(noise.shape[0])
    out = pltpu.VMEM((sum(depth),) + source.shape[1:], jnp.float32)
    return pl.pallas_call(
        edges_kernel,
        out_shape=(out, out),
        in_specs=[SMEM] + [VMEM] * 3,
        out_specs=(VMEM, VMEM),
        name="edges",
    )(in_smem(accept), *[in_vmem(field) for field in (moved, noise, source)])


def moves_kernel(
    accept_ref, root_ref, moved_ref, noise_ref, source_ref, low_ref, high_ref,
    cond_out, pot_out, traces_out, pot, once, conductivity, gain, faces,
):
    moves, width, ny, nz = noise_ref.shape
    reach = 2 * moves
    span = width + 2 * reach
    at, depth = layout(moves)
    tile = lax.axis_index("tile")
    first = tile == 0
    last = tile == lax.axis_size("tile") - 1

    def halo(number, i):
        if i < 0:
            return low_ref[at[number] + depth[number] + i]
        return high_ref[at[number] + i - width]

    def own(i):
        return 0 <= i < width

    def keep_inside(value, i):
        outside = (first & (i < reach)) | (last & (i >= reach + width))
        return jnp.where(outside, 0.0, value)

    def sweep(old, lo, hi):
        for i in range(lo, hi):
            here, here_k = old[i], conductivity[i]
            flux = (here_k + conductivity[i - 1]) * old[i - 1] + (
                here_k + conductivity[i + 1]
            ) * old[i + 1]
            for side, near in enumerate(shifts(here)):
                flux += faces[side, i] * near
            x = i - reach
            source = source_ref[x] if own(x) else halo(1 + moves, x)
            value = (1.0 - relax_weight) * here + (
                2.0 * source + flux
            ) * gain[i]
            yield i, keep_inside(value, i)

    for i in range(span):
        x = i - reach
        pot[i] = moved_ref[1, x] if own(x) else halo(0, x)
        if own(x):
            cond_out[x] = moved_ref[0, x]

    for m in range(moves):
        start = 2 * m
        accepted = accept_ref[m] > 0
        for i in range(start, span - start):
            x = i - reach
            if own(x):
                conduct = cond_out[x]
                proposal = prior_keep * conduct + prior_fresh * noise_ref[m, x]
                cond_out[x] = jnp.where(accepted, proposal, conduct)
            else:
                proposal = halo(1 + m, x)
            conductivity[i] = jnp.exp(proposal)
        for i in range(start + 1, span - start - 1):
            here_k = conductivity[i]
            total = 6.0 * here_k + conductivity[i - 1] + conductivity[i + 1]
            for side, (near, outside) in enumerate(zip(shifts(here_k), outer((ny, nz)))):
                total += jnp.where(outside, 1.0, near)
                faces[side, i] = jnp.where(outside, 0.0, here_k + near)
            gain[i] = relax_weight / total
        for i, value in sweep(pot, start + 1, span - start - 1):
            once[i] = value
        for i, value in sweep(once, start + 2, span - start - 2):
            pot[i] = jnp.where(accepted, value, pot[i])

    root = root_ref[0:1]
    for x in range(width):
        value = pot[x + reach]
        pot_out[x] = value
        traces_out[:, x * nz:(x + 1) * nz] = value * root


def run_moves(accept, root, *fields):
    moves, width, ny, nz = fields[1].shape
    span = width + 4 * moves
    return pl.pallas_call(
        moves_kernel,
        out_shape=(
            pltpu.VMEM((width, ny, nz), jnp.float32),
            pltpu.VMEM((width, ny, nz), jnp.float32),
            pltpu.VMEM((ny, width * nz), jnp.float32),
        ),
        in_specs=[SMEM] + [VMEM] * (1 + len(fields)),
        out_specs=(VMEM, VMEM, VMEM),
        scratch_shapes=[pltpu.VMEM((span, ny, nz), jnp.float32)] * 4
        + [pltpu.VMEM((4, span, ny, nz), jnp.float32)],
        name="moves",
    )(in_smem(accept), in_vmem(root), *[in_vmem(field) for field in fields])


def sum_parts_kernel(parts_ref, total_ref):
    total = parts_ref[0]
    for place in range(1, parts_ref.shape[0]):
        total += parts_ref[place]
    total_ref[...] = total


def sum_parts(parts):
    return pl.pallas_call(
        sum_parts_kernel,
        out_shape=pltpu.VMEM(parts.shape[1:], jnp.float32),
        in_specs=[VMEM],
        out_specs=VMEM,
        name="sum_parts",
    )(in_vmem(parts))


def own_rows(ref, rows, owner):
    return ref.at[pl.ds(pl.multiple_of(owner * rows, rows), rows)]


def store_kernel(cond_ref, pot_ref, half_ref, cond_out, pot_out, rows_out, sems):
    own = own_rows(rows_out, half_ref.shape[0], lax.axis_index("member"))
    pairs = [(cond_ref, cond_out), (pot_ref, pot_out), (half_ref, own)]
    copies = [
        pltpu.make_async_copy(here, there, sems.at[i]) for i, (here, there) in enumerate(pairs)
    ]
    for copy in copies:
        copy.start()
    for copy in copies:
        copy.wait()


def store(conduct, pot, half):
    return pl.pallas_call(
        store_kernel,
        out_shape=(
            jax.ShapeDtypeStruct(conduct.shape, jnp.float32),
            jax.ShapeDtypeStruct(pot.shape, jnp.float32),
            jax.ShapeDtypeStruct((pair * half.shape[0], half.shape[1]), jnp.float32),
        ),
        in_specs=[VMEM] * 3,
        out_specs=(ANY,) * 3,
        scratch_shapes=[pltpu.SemaphoreType.DMA((3,))],
        name="store",
    )(in_vmem(conduct), in_vmem(pot), in_vmem(half))


def store_other_kernel(half_ref, held_ref, rows_out, sem):
    other = own_rows(rows_out, half_ref.shape[0], 1 - lax.axis_index("member"))
    copy = pltpu.make_async_copy(half_ref, other, sem)
    copy.start()
    copy.wait()


def store_other(half, held):
    return pl.pallas_call(
        store_other_kernel,
        out_shape=jax.ShapeDtypeStruct(held.shape, jnp.float32),
        in_specs=[VMEM, ANY],
        out_specs=ANY,
        scratch_shapes=[pltpu.SemaphoreType.DMA],
        input_output_aliases={1: 0},
        name="store_other",
    )(in_vmem(half), held)


def exchange_halo(low_edge, high_edge):
    count = lax.axis_size("tile")
    forward = [(i, i + 1) for i in range(count - 1)]
    backward = [(target, source) for source, target in forward]
    high = lax.ppermute(low_edge, "tile", backward)
    low = lax.ppermute(high_edge, "tile", forward)
    return low, high


def swap(block):
    return lax.ppermute(block, "member", [(0, 1), (1, 0)])


def local(log_cond, potential, noise, source, parents, accept, weights):
    width, ny, nz = source.shape

    weights, parents, accept, pieces, noise, source = pack(
        weights, parents, accept[:, 0], log_cond, potential, noise[:, 0], source,
        lax.axis_size("pairs"),
    )
    pieces = lax.all_to_all(pieces, "pairs", 0, 0, tiled=True)
    chosen, root = choose(parents, weights, pieces, swap(pieces))
    moved = lax.all_to_all(chosen, "pairs", 0, 0, tiled=True).reshape(2, width, ny, nz)
    low, high = exchange_halo(*edges(accept, moved, noise, source))
    conduct, pot, traces = run_moves(accept, root, moved, noise, source, low, high)

    rows = traces.shape[1] // (lax.axis_size("tile") * pair)
    member = lax.axis_index("member")
    piece = lax.all_gather(traces, "tile", axis=0, tiled=True)

    def product(owner):
        columns = lax.dynamic_slice_in_dim(
            piece, (lax.axis_index("tile") * pair + owner) * rows, rows, 1
        )
        return lax.dot_general(
            columns,
            piece,
            (((0,), (0,)), ((), ())),
            precision=lax.Precision.HIGH,
            preferred_element_type=jnp.float32,
        ).reshape(lax.axis_size("pairs"), -1, piece.shape[1])

    got = swap(product(1 - member))
    parts = lax.all_to_all(product(member) + got, "pairs", 0, 0, tiled=True)
    mine = lax.all_gather(sum_parts(parts), "pairs", axis=0, tiled=True)
    other = swap(mine).reshape(rows, -1)
    conduct, pot, held = store(conduct, pot, mine.reshape(rows, -1))
    moments = store_other(other, held)
    return (conduct[None], pot[None], moments)


def solution(mesh):
    tiles = mesh.shape["tile"]
    split = jax.sharding.Mesh(
        mesh.devices.reshape(-1, pair, tiles), ("pairs", "member", "tile")
    )
    placed = (
        P(group, "tile", None, None),
        P(group, "tile", None, None),
        P(None, group, "tile", None, None),
        P("tile", None, None),
        P(),
        P(None, group),
        P(group),
    )
    return jax.shard_map(
        local,
        mesh=split,
        in_specs=placed,
        out_specs=(P(group, "tile", None, None), P(group, "tile", None, None), P("tile", None)),
        check_vma=False,
    )
```
